256 devices in a mesh: row: 32 (over z, x), col: 8 (over y, core).
Axes of the slice: x: 4, y: 4, z: 8, core: 2. Of those that a mesh axis runs over, the one named last changes fastest.
Arguments:
- panel: float32 [128, 524288], P('col', 'row'), may hold values from -6 to 6
- signs: int32 [524288], P('row'), may hold values from -1 to 1, as said below
- offsets: int32 [32768], P('row'), may hold values from 0 to 16383
- owners: int32 [32768, 1], P('row'), may hold values from 0 to 31; in each aligned block of 1024 rows (0 to 1023, 1024 to 2047, ...) at most 64 rows name the same one
Outputs:
- grams: float32 [32, 128, 128], P('row', 'col')
The draws below stay inside these ranges and needn't reach their ends.
Inputs may be any that keep to these rules, and one draw needn't show every extreme that they name: `signs`: each entry is +1 or -1. `owners`: in each aligned block of 1024 samples (the list of one source), no owner is named more than 64 times, a bound that some block reaches; every owner is named somewhere.
All inputs are finite; a program needn't handle non-finite values.
Results may differ from the reference program's by a relative error of at most 0.0003.
Values sent between devices are 32-bit elements; how exact they have to be, the bound alone decides.
A program may use at most 128 MiB of HBM per device.

```python
import math
import jax
import jax.numpy as jnp
import numpy as np
from jax import lax

C = 128
ROWS_DEV = 16384
KDEV = 1024
ROWS = 524288
SAMPLES = 32768
OWNERS = 32
CAP = 64
N_ROW = 32


def draw_signs(key, part):
    return 2 * jax.random.randint(key, (ROWS,), 0, 2, dtype=jnp.int32) - 1


def plant(drawn, rng, low, high):
    longest = drawn.shape.index(max(drawn.shape))
    spots = []
    for shift in (0, 1):
        where = [jax.random.randint(jax.random.fold_in(rng, axis), (), 0, length) for axis, length in enumerate(drawn.shape)]
        where[longest] = (where[longest] + shift) % drawn.shape[longest]
        spots.append(tuple(where))
    return drawn.at[spots[0]].set(low).at[spots[1]].set(high)


def block_levels(key, extent, pieces, low, top_value):
    def one(axis_at, shards_of):
        heights = jax.random.uniform(jax.random.fold_in(jax.random.fold_in(key, 6), axis_at), (shards_of,), jnp.float32, low / len(pieces), top_value / len(pieces))
        return jnp.repeat(jnp.exp(heights), extent[axis_at] // shards_of).reshape((-1,) + (1,) * (len(extent) - axis_at - 1))

    loudness = one(*pieces[0])
    for cut in pieces[1:]:
        loudness = loudness * one(*cut)
    return loudness


def assign_block(own_key, own, number, rows, amount, top, limit, lean):
    order = jax.random.permutation(own_key, amount)
    packed, usual = shares(amount, rows * top, limit, lean, True), shares(amount, rows * top, limit, lean, False)
    places = jnp.arange(amount)

    def named(tallies, rotation):
        used = int((tallies > 0).sum())
        fixed = max(1, used // 4)
        shifted = fixed + (places - fixed + rotation * (used - fixed)) % max(1, amount - fixed)
        return jnp.zeros((amount,), jnp.int32).at[order[jnp.where(places < fixed, places, shifted)]].set(jnp.asarray(tallies, jnp.int32))

    tallies = jnp.where(number % 4 == 0, named(packed, number // 4), named(usual, number - number // 4 - 1))
    mixed = jax.random.permutation(jax.random.fold_in(own, 3), amount)
    source_of, sink = mixed[0:amount // 2 * 2:2], mixed[1:amount // 2 * 2:2]
    room = jnp.minimum(tallies[source_of] - 1, limit - tallies[sink]) // 2
    room = jnp.where((source_of == order[0]) | (sink == order[0]) | (tallies[sink] == 0), 0, jnp.maximum(room, 0))
    shifted = jax.random.randint(jax.random.fold_in(own, 4), (amount // 2,), 0, 1 << 20) % (room + 1)
    tallies = tallies.at[source_of].add(-shifted).at[sink].add(shifted)
    items = jnp.searchsorted(jnp.cumsum(tallies), jnp.arange(rows * top), side="right").astype(jnp.int32)
    grid = items.reshape(top, rows).T
    grid = grid[jax.random.permutation(jax.random.fold_in(own, 1), rows)]
    rotation = jax.random.randint(jax.random.fold_in(own, 2), (rows, 1), 0, top)
    return jnp.take_along_axis(grid, (jnp.arange(top)[None, :] + rotation) % top, axis=1)


def shares(amount, total, reach, lean, full):
    portions = [(1 << 20) // math.isqrt(rank ** lean) + 1 for rank in range(1, amount + 1)]
    largest = reach if full else min(reach, max(-(-total // amount), total * portions[0] // sum(portions)))
    least = 1 if total - largest >= amount - 1 else 0
    counts, surplus = [largest] + [least] * (amount - 1), total - largest - least * (amount - 1)
    while surplus > 0:
        free = [i for i in range(1, amount) if counts[i] < largest] or [i for i in range(1, amount) if counts[i] < reach]
        pool, budget = sum([portions[i] for i in free]), surplus
        for i in free:
            addition = min(reach - counts[i], max(1, budget * portions[i] // pool), surplus)
            counts[i] = counts[i] + addition
            surplus = surplus - addition
    return np.array(counts)


def gaussian(key, dims, scale, reach, cuts=(), kind=jnp.bfloat16):
    level = block_levels(key, dims, cuts, -0.22, 0.18) if cuts else 1.0
    entries = jax.random.normal(key, dims, jnp.float32) * scale * level
    return jnp.minimum(jnp.maximum(entries, -reach), reach).astype(kind)


def setup_inputs(seed: int = 0) -> dict:
    keys = jax.random.split(jax.random.key(seed), 5)
    panel = gaussian(keys[0], (C, ROWS), 1.0, 6.0, ((0, 8), (1, 32)), jnp.float32)
    signs = draw_signs(jax.random.fold_in(keys[4], 71), 0)
    offsets = plant(jax.random.randint(keys[2], (SAMPLES,), 0, ROWS_DEV), jax.random.fold_in(keys[2], 1), 0, ROWS_DEV - 1).astype(jnp.int32)
    owners_keys = jax.random.split(jax.random.fold_in(keys[3], 1), SAMPLES // KDEV)
    owners_turns = jax.random.permutation(jax.random.fold_in(keys[3], 3), SAMPLES // KDEV)
    owners = jax.vmap(lambda own, number: assign_block(jax.random.fold_in(keys[3], 2), own, number, KDEV, OWNERS, 1, CAP, 2))(owners_keys, owners_turns).reshape((SAMPLES, 1))
    return dict(panel=panel, signs=signs, offsets=offsets, owners=owners)


def sylvester(order):
    index = jnp.arange(order, dtype=jnp.int32)
    common = jnp.bitwise_and(index[:, None], index[None, :])
    parity = jnp.zeros((order, order), jnp.int32)
    for level in range(max(order.bit_length() - 1, 0)):
        parity = parity + jnp.bitwise_and(jnp.right_shift(common, level), 1)
    return (1 - 2 * (parity % 2)).astype(jnp.float32)

def reference(panel, signs, offsets, owners):
    devices = N_ROW
    blocks = ROWS_DEV // 128
    table_a = sylvester(128)
    table_b = sylvester(blocks)
    table_p = sylvester(devices)
    scale = 1.0 / jnp.sqrt(jnp.float32(ROWS))
    source = jnp.arange(SAMPLES, dtype=jnp.int32) // KDEV
    mixing = table_p[source]
    sign_rows = signs.astype(jnp.float32).reshape(devices, 128, blocks)
    high = lax.Precision.HIGHEST

    def one_block(columns):
        signed = columns.reshape(-1, devices, 128, blocks) * sign_rows
        inner = jnp.einsum('cqab,bd->cqad', signed, table_b, precision=high)
        outer = jnp.einsum('ea,cqad->cqed', table_a, inner, precision=high)
        outer = outer.reshape(-1, devices, ROWS_DEV)
        picked = outer[:, :, offsets]
        return jnp.einsum('cqk,kq->ck', picked, mixing, precision=high) * scale
    sketch = lax.map(one_block, panel.reshape(C // 16, 16, ROWS)).reshape(C, SAMPLES)
    owner_ids = owners[:, 0]

    def one_owner(owner):
        weight = (owner_ids == owner).astype(jnp.float32)
        return jnp.einsum('ck,dk->cd', sketch * weight[None, :], sketch, precision=high) / KDEV
    return lax.map(one_owner, jnp.arange(OWNERS, dtype=jnp.int32))
```

```python
import functools

import jax
import jax.numpy as jnp
from jax import lax
from jax.experimental import pallas as pl
from jax.experimental.pallas import tpu as pltpu
from jax.sharding import PartitionSpec as P

MESH = pl.DeviceIdType.MESH
F32 = jnp.float32
BF16 = jnp.bfloat16
NT = (((1,), (1,)), ((), ()))
VMEM = pl.BlockSpec(memory_space=pltpu.VMEM)
SLOTS = 32


def place():
    row, col = lax.axis_index("row"), lax.axis_index("col")
    return row // 4, row % 4, col // 2, col % 2


def at(z, x, y, core):
    return {"row": z * 4 + x, "col": y * 2 + core}


def iota(shape, dim):
    return lax.broadcasted_iota(jnp.int32, shape, dim)


def sylvester(order):
    v = iota((order, order), 0) & iota((order, order), 1)
    for shift in (4, 2, 1):
        v = v ^ (v >> shift)
    return (1 - 2 * (v & 1)).astype(F32)


def butterfly(vals):
    vals, step = list(vals), 1
    while step < len(vals):
        for i in range(len(vals)):
            if i & step == 0:
                a, b = vals[i], vals[i + step]
                vals[i], vals[i + step] = a + b, a - b
        step *= 2
    return vals


def split(v):
    hi = v.astype(BF16)
    return hi, (v - hi.astype(F32)).astype(BF16)


def wait_bytes(ref, sem):
    pltpu.make_async_copy(ref, ref, sem).wait()


def mix_kernel(panel, signs, out, y_ref, r_ref, t_ref, send_sem, recv_sem, core_send, core_recv):
    z, x, y, core = place()
    table = sylvester(128).astype(BF16)
    table = jnp.concatenate([table, table], axis=0)

    def inner(i, carry):
        sign = signs[pl.ds(i * 16, 16), :].astype(F32)
        rows = []
        for j in range(16):
            start = pl.multiple_of((i * 16 + j) * 128, 128)
            rows.append(panel[:, pl.ds(start, 128)] * sign[j : j + 1, :])
        hi, lo = split(jnp.concatenate(rows, axis=0))
        pieces = jnp.concatenate([hi, lo], axis=1)
        done = jnp.dot(pieces, table, preferred_element_type=F32)
        y_ref[pl.ds(i * 16, 16)] = done.reshape(16, 16, 128)
        return carry

    lax.fori_loop(0, 8, inner, 0)

    def outer_high(g, carry):
        vals = butterfly([y_ref[g + 8 * j] for j in range(16)])
        for j in range(16):
            y_ref[g + 8 * j] = vals[j]
        return carry

    lax.fori_loop(0, 8, outer_high, 0)

    def outer_low(g, carry):
        vals = butterfly([y_ref[g * 8 + j] for j in range(8)])
        for j in range(8):
            y_ref[g * 8 + j] = vals[j]
        return carry

    lax.fori_loop(0, 16, outer_low, 0)

    slot = y * 32 + z * 4 + x

    def send(i, carry):
        off = (i * 37) % 128
        tz, tx, ty = (z + off // 16) % 8, (x + off // 4 % 4) % 4, (y + off % 4) % 4
        pltpu.make_async_remote_copy(
            src_ref=y_ref.at[tz * 16 + tx * 4 + ty],
            dst_ref=r_ref.at[slot],
            send_sem=send_sem,
            recv_sem=recv_sem,
            device_id=at(tz, tx, ty, core),
            device_id_type=MESH,
        ).start()
        return carry

    lax.fori_loop(1, 128, send, 0)
    r_ref[slot] = y_ref[z * 16 + x * 4 + y]
    wait_bytes(r_ref.at[pl.ds(0, 127)], recv_sem)

    turn = (1 - 2 * core).astype(F32)

    def across(v, carry):
        for h in range(2):
            rows = pl.ds(8 * h, 8)
            low = [r_ref[v * 32 + q, rows, :] for q in range(16)]
            high = [r_ref[v * 32 + 16 + q, rows, :] * turn for q in range(16)]
            kept = butterfly([a + b for a, b in zip(low, high)])
            for p in range(16):
                out[p, v, core, rows, :] = kept[p]
            given = butterfly([a - b for a, b in zip(low, high)])
            for p in range(16):
                t_ref[v, p, rows, :] = given[p]
        pltpu.make_async_remote_copy(
            src_ref=t_ref.at[v],
            dst_ref=out.at[:, v, core],
            send_sem=core_send,
            recv_sem=core_recv,
            device_id=at(z, x, y, 1 - core),
            device_id_type=MESH,
        ).start()
        return carry

    lax.fori_loop(0, 4, across, 0)
    wait_bytes(r_ref.at[pl.ds(0, 127)], send_sem)
    wait_bytes(t_ref, core_send)
    wait_bytes(t_ref, core_recv)


def gram_kernel(mixed, offsets, owners, out, wide, picked):
    z, x, y, core = place()
    slab = z * 16 + x * 4 + y
    for p in range(16):
        hi, lo = split(mixed[p])
        wide[0:128, 128 * p : 128 * p + 128] = hi
        wide[128:256, 128 * p : 128 * p + 128] = lo
    here = offsets[...] - slab * 128
    inside = (here >= 0) & (here < 128)
    mask = jnp.where(inside, 1.0, 0.0).astype(F32)
    before = (iota((128, 128), 0) < iota((128, 128), 1)).astype(F32).astype(BF16)
    rank, seen = [], jnp.zeros((16, 1), F32)
    for b in range(8):
        piece = mask[:, 128 * b : 128 * b + 128]
        rank.append(jnp.dot(piece.astype(BF16), before, preferred_element_type=F32) + seen)
        seen = seen + jnp.sum(piece, axis=1, keepdims=True)
    rank = jnp.where(inside, jnp.concatenate(rank, axis=1), -1.0).astype(jnp.int32)
    lane = jnp.where(inside, here, 0).astype(F32)
    name = jnp.where(inside, owners[...] + 1, 0).astype(F32)
    rounds = (jnp.max(seen).astype(jnp.int32) + SLOTS - 1) // SLOTS
    out[...] = jnp.zeros_like(out)

    def one_round(r, carry):
        names = []
        for g in range(4):
            hot = []
            for p in range(4 * g, 4 * g + 4):
                hot.append(rank[p : p + 1, :] == iota((SLOTS, 1024), 0) + r * SLOTS)
            hot = jnp.concatenate(hot, axis=0).astype(F32).astype(BF16)
            facts = jnp.concatenate([lane[4 * g : 4 * g + 4], name[4 * g : 4 * g + 4]], axis=0)
            found = lax.dot_general(facts.astype(BF16), hot, NT, preferred_element_type=F32)
            which = iota((1, 128), 1) // SLOTS
            at_lane, its_name = jnp.zeros((1, 128), F32), jnp.zeros((1, 128), F32)
            for p in range(4):
                at_lane = jnp.where(which == p, found[p : p + 1, :], at_lane)
                its_name = jnp.where(which == p, found[4 + p : 5 + p, :], its_name)
            spot = jnp.where(its_name > 0.5, at_lane.astype(jnp.int32) + which * 128, -1)
            pick = (iota((512, 128), 0) == spot).astype(F32).astype(BF16)
            got = jnp.dot(wide[:, 512 * g : 512 * g + 512], pick, preferred_element_type=F32)
            picked[:, 128 * g : 128 * g + 128] = got.astype(BF16)
            names.append(its_name)
        names = jnp.concatenate(names, axis=1)

        def one_owner(o, carry):
            member = (names == (o + 1).astype(F32)).astype(F32).astype(BF16)
            both = lax.dot_general(picked[...] * member, picked[...], NT, preferred_element_type=F32)
            total = (both[:128, :128] + both[128:, 128:]) + (both[:128, 128:] + both[128:, :128])
            out[o] += total * (2.0 ** -29)
            return carry

        lax.fori_loop(0, 32, one_owner, 0)
        return carry

    lax.fori_loop(0, rounds, one_round, 0)


def sum_kernel(gram, out, c_ref, ha, hb, a1, b1, sa, sb, a2, b2, sz, zr, s0, r0, s1, r1, s2, r2, s3, r3):
    z, x, y, core = place()

    def push(src, dst, ss, rs, where):
        pltpu.make_async_remote_copy(
            src_ref=src, dst_ref=dst, send_sem=ss, recv_sem=rs, device_id=where, device_id_type=MESH
        ).start()

    push(gram.at[:, :, :, 1 - core], c_ref, s0, r0, at(z, x, y, 1 - core))
    wait_bytes(c_ref, r0)

    def add_core(i, carry):
        for tx in range(4):
            for ty in range(4):
                ha[tx, i, ty] = gram[i, tx, ty, core, 0:8, :] + c_ref[i, tx, ty, 0:8, :]
                hb[ty, i, tx] = gram[i, tx, ty, core, 8:16, :] + c_ref[i, tx, ty, 8:16, :]
        return carry

    lax.fori_loop(0, 8, add_core, 0)
    for d in (2, 1, 3):
        tx, ty = (x + d) % 4, (y + d) % 4
        push(ha.at[tx], a1.at[x], s1.at[0], r1.at[0], at(z, tx, y, core))
        push(hb.at[ty], b1.at[y], s1.at[1], r1.at[1], at(z, x, ty, core))
    a1[x] = ha[x]
    b1[y] = hb[y]
    wait_bytes(a1.at[pl.ds(0, 3)], r1.at[0])
    wait_bytes(b1.at[pl.ds(0, 3)], r1.at[1])

    def add_first(i, carry):
        for t in range(4):
            sa[t, i] = (a1[0, i, t] + a1[1, i, t]) + (a1[2, i, t] + a1[3, i, t])
            sb[t, i] = (b1[0, i, t] + b1[1, i, t]) + (b1[2, i, t] + b1[3, i, t])
        return carry

    lax.fori_loop(0, 8, add_first, 0)
    for d in (2, 1, 3):
        tx, ty = (x + d) % 4, (y + d) % 4
        push(sa.at[ty], a2.at[y], s2.at[0], r2.at[0], at(z, x, ty, core))
        push(sb.at[tx], b2.at[x], s2.at[1], r2.at[1], at(z, tx, y, core))
    a2[y] = sa[y]
    b2[x] = sb[x]
    wait_bytes(a2.at[pl.ds(0, 3)], r2.at[0])
    wait_bytes(b2.at[pl.ds(0, 3)], r2.at[1])
    for i in range(8):
        sz[i, 0:8, :] = (a2[0, i] + a2[1, i]) + (a2[2, i] + a2[3, i])
        sz[i, 8:16, :] = (b2[0, i] + b2[1, i]) + (b2[2, i] + b2[3, i])
    for d in (4, 3, 5, 2, 6, 1, 7):
        tz = (z + d) % 8
        push(sz.at[tz], zr.at[z], s3, r3, at(tz, x, y, core))
    zr[z] = sz[z]
    wait_bytes(zr.at[pl.ds(0, 7)], r3)
    v = [zr[i] for i in range(8)]
    out[...] = ((v[0] + v[1]) + (v[2] + v[3])) + ((v[4] + v[5]) + (v[6] + v[7]))
    wait_bytes(c_ref, s0)
    for n in range(2):
        wait_bytes(a1.at[pl.ds(0, 3)], s1.at[n])
        wait_bytes(a2.at[pl.ds(0, 3)], s2.at[n])
    wait_bytes(zr.at[pl.ds(0, 7)], s3)


def body(panel, signs, offsets, owners):
    params = functools.partial(pltpu.CompilerParams, vmem_limit_bytes=48 << 20)
    dma = pltpu.SemaphoreType.DMA
    listed = lax.all_gather(offsets, "row", axis=0)
    named = lax.all_gather(owners.reshape(-1), "row", axis=0)
    core = lax.axis_index("col") % 2
    listed = lax.dynamic_slice_in_dim(listed, core * 16, 16, 0)
    named = lax.dynamic_slice_in_dim(named, core * 16, 16, 0)
    mixed = pl.pallas_call(
        mix_kernel,
        out_shape=jax.ShapeDtypeStruct((16, 4, 2, 16, 128), F32),
        in_specs=[VMEM] * 2,
        out_specs=VMEM,
        scratch_shapes=[
            pltpu.VMEM((128, 16, 128), F32),
            pltpu.VMEM((128, 16, 128), F32),
            pltpu.VMEM((4, 16, 16, 128), F32),
            dma, dma, dma, dma,
        ],
        compiler_params=params(has_side_effects=True),
        name="mix",
    )(panel, signs.reshape(128, 128))
    gram = pl.pallas_call(
        gram_kernel,
        out_shape=jax.ShapeDtypeStruct((32, 128, 128), F32),
        in_specs=[VMEM] * 3,
        out_specs=VMEM,
        scratch_shapes=[pltpu.VMEM((256, 2048), BF16), pltpu.VMEM((256, 512), BF16)],
        compiler_params=params(),
        name="gram",
    )(mixed.reshape(16, 128, 128), listed, named)
    summed = pl.pallas_call(
        sum_kernel,
        out_shape=jax.ShapeDtypeStruct((16, 128), F32),
        in_specs=[VMEM],
        out_specs=VMEM,
        scratch_shapes=[
            pltpu.VMEM((8, 4, 4, 16, 128), F32),
            pltpu.VMEM((4, 8, 4, 8, 128), F32),
            pltpu.VMEM((4, 8, 4, 8, 128), F32),
            pltpu.VMEM((4, 8, 4, 8, 128), F32),
            pltpu.VMEM((4, 8, 4, 8, 128), F32),
            pltpu.VMEM((4, 8, 8, 128), F32),
            pltpu.VMEM((4, 8, 8, 128), F32),
            pltpu.VMEM((4, 8, 8, 128), F32),
            pltpu.VMEM((4, 8, 8, 128), F32),
            pltpu.VMEM((8, 16, 128), F32),
            pltpu.VMEM((8, 16, 128), F32),
        ] + [dma] * 2 + [dma((2,))] * 4 + [dma] * 2,
        compiler_params=params(has_side_effects=True),
        name="sum",
    )(gram.reshape(8, 4, 4, 2, 16, 128))
    return summed[None]


def solution(mesh):
    placed = (P("col", "row"), P("row"), P("row"), P("row", None))
    return jax.shard_map(
        body, mesh=mesh, in_specs=placed, out_specs=P("row", "col", None), check_vma=False
    )
```

```python
import functools

import jax
import jax.numpy as jnp
from jax import lax
from jax.experimental import pallas as pl
from jax.experimental.pallas import tpu as pltpu
from jax.sharding import PartitionSpec as P

MESH = pl.DeviceIdType.MESH
F32 = jnp.float32
BF16 = jnp.bfloat16
NT = (((1,), (1,)), ((), ()))
VMEM = pl.BlockSpec(memory_space=pltpu.VMEM)
SLOTS = 32


def place():
    row, col = lax.axis_index("row"), lax.axis_index("col")
    return row // 4, row % 4, col // 2, col % 2


def at(z, x, y, core):
    return {"row": z * 4 + x, "col": y * 2 + core}


def iota(shape, dim):
    return lax.broadcasted_iota(jnp.int32, shape, dim)


def sylvester(order):
    v = iota((order, order), 0) & iota((order, order), 1)
    for shift in (4, 2, 1):
        v = v ^ (v >> shift)
    return (1 - 2 * (v & 1)).astype(F32)


def butterfly(vals):
    vals, step = list(vals), 1
    while step < len(vals):
        for i in range(len(vals)):
            if i & step == 0:
                a, b = vals[i], vals[i + step]
                vals[i], vals[i + step] = a + b, a - b
        step *= 2
    return vals


def split(v):
    hi = v.astype(BF16)
    return hi, (v - hi.astype(F32)).astype(BF16)


def wait_bytes(ref, sem):
    pltpu.make_async_copy(ref, ref, sem).wait()


def greet(z, x, y, core, barrier):
    for d in range(1, 8):
        tell(barrier, at((z + d) % 8, x, y, core))
    for d in range(1, 4):
        tell(barrier, at(z, (x + d) % 4, y, core))
        tell(barrier, at(z, x, (y + d) % 4, core))
    tell(barrier, at(z, x, y, 1 - core))


def tell(sem, where):
    pl.semaphore_signal(sem, inc=1, device_id=where, device_id_type=MESH)


def push(src, dst, send_sem, recv_sem, where):
    pltpu.make_async_remote_copy(
        src_ref=src, dst_ref=dst, send_sem=send_sem, recv_sem=recv_sem, device_id=where, device_id_type=MESH
    ).start()


def mix_kernel(
    panel_hbm, signs, offsets, owners, out, lists, panel, y_ref, r_ref, t_ref, mine,
    load_sem, send_sem, recv_sem, core_send, core_recv, list_send, list_recv, plane_sem, all_sem,
):
    z, x, y, core = place()
    barrier = pltpu.get_barrier_semaphore()
    greet(z, x, y, core, barrier)

    def load(i):
        span = pl.ds(4096 * i, 4096)
        return pltpu.make_async_copy(panel_hbm.at[:, span], panel.at[:, span], load_sem.at[i])

    for i in range(4):
        load(i).start()
    mine[0:8, :] = offsets[...]
    mine[8:16, :] = owners[...]
    table = sylvester(128).astype(BF16)
    table = jnp.concatenate([table, table], axis=0)

    for part in range(4):
        load(part).wait()
        for i in range(2 * part, 2 * part + 2):
            sign = signs[16 * i : 16 * i + 16, :].astype(F32)
            rows = []
            for j in range(16):
                start = (i * 16 + j) * 128
                rows.append(panel[:, start : start + 128] * sign[j : j + 1, :])
            hi, lo = split(jnp.concatenate(rows, axis=0))
            pieces = jnp.concatenate([hi, lo], axis=1)
            done = jnp.dot(pieces, table, preferred_element_type=F32)
            y_ref[16 * i : 16 * i + 16] = done.reshape(16, 16, 128)

    pl.semaphore_wait(barrier, 14)
    for d in range(1, 4):
        tell(plane_sem, at(z, (x + d) % 4, y, core))

    def outer_high(g, carry):
        vals = butterfly([y_ref[g + 8 * j] for j in range(16)])
        for j in range(16):
            y_ref[g + 8 * j] = vals[j]
        return carry

    lax.fori_loop(0, 8, outer_high, 0)
    pl.semaphore_wait(plane_sem, 3)
    for d in range(1, 4):
        tell(all_sem, at(z, x, (y + d) % 4, core))
    pl.semaphore_wait(all_sem, 3)

    slot = y * 32 + z * 4 + x
    to_x = [(x + d) % 4 for d in range(4)]
    to_y = [(y + d) % 4 for d in range(4)]
    sends_list = z // 4 == core

    def send(i, carry):
        tz = (z + i * 3 + 4) % 8
        for g in range(2):
            vals = butterfly([y_ref[tz * 16 + g * 8 + j] for j in range(8)])
            for j in range(8):
                y_ref[tz * 16 + g * 8 + j] = vals[j]
        for dx in range(4):
            for dy in range(4):
                def go():
                    push(
                        y_ref.at[tz * 16 + to_x[dx] * 4 + to_y[dy]], r_ref.at[slot],
                        send_sem, recv_sem, at(tz, to_x[dx], to_y[dy], core),
                    )
                def go_list():
                    push(mine, lists.at[z % 4 * 4 + x], list_send, list_recv, at(tz, to_x[dx], y, core))
                if dx or dy:
                    go()
                else:
                    pl.when(tz != z)(go)
                if dy == 0:
                    pl.when(sends_list if dx else sends_list & (tz != z))(go_list)
        return carry

    lax.fori_loop(0, 8, send, 0)
    r_ref[slot] = y_ref[z * 16 + x * 4 + y]

    @pl.when(sends_list)
    def _():
        lists[z % 4 * 4 + x] = mine[...]
        wait_bytes(lists.at[pl.ds(0, 15)], list_recv)

    @pl.when(jnp.logical_not(sends_list))
    def _():
        wait_bytes(lists, list_recv)

    wait_bytes(r_ref.at[pl.ds(0, 127)], recv_sem)

    turn = (1 - 2 * core).astype(F32)

    def across(v, carry):
        for h in range(2):
            rows = pl.ds(8 * h, 8)
            low = [r_ref[v * 32 + q, rows, :] for q in range(16)]
            high = [r_ref[v * 32 + 16 + q, rows, :] * turn for q in range(16)]
            given = butterfly([a - b for a, b in zip(low, high)])
            for p in range(16):
                t_ref[v, p, rows, :] = given[p]
            kept = butterfly([a + b for a, b in zip(low, high)])
            for p in range(16):
                out[p, v, core, rows, :] = kept[p]
        push(t_ref.at[v], out.at[:, v, core], core_send, core_recv, at(z, x, y, 1 - core))
        return carry

    lax.fori_loop(0, 4, across, 0)
    wait_bytes(r_ref.at[pl.ds(0, 127)], send_sem)

    @pl.when(sends_list)
    def _():
        for n in range(31):
            wait_bytes(mine, list_send)

    wait_bytes(t_ref, core_send)
    wait_bytes(t_ref, core_recv)


def gram_kernel(mixed, lists, out, wide, picked):
    z, x, y, core = place()
    slab = z * 16 + x * 4 + y
    for p in range(16):
        hi, lo = split(mixed[p])
        wide[0:128, 128 * p : 128 * p + 128] = hi
        wide[128:256, 128 * p : 128 * p + 128] = lo
    here = jnp.concatenate([lists[:, b, :] for b in range(8)], axis=1) - slab * 128
    owner = jnp.concatenate([lists[:, 8 + b, :] for b in range(8)], axis=1)
    inside = (here >= 0) & (here < 128)
    mask = jnp.where(inside, 1.0, 0.0).astype(F32)
    before = (iota((128, 128), 0) < iota((128, 128), 1)).astype(F32).astype(BF16)
    rank, seen = [], jnp.zeros((16, 1), F32)
    for b in range(8):
        piece = mask[:, 128 * b : 128 * b + 128]
        rank.append(jnp.dot(piece.astype(BF16), before, preferred_element_type=F32) + seen)
        seen = seen + jnp.sum(piece, axis=1, keepdims=True)
    rank = jnp.where(inside, jnp.concatenate(rank, axis=1), -1.0).astype(jnp.int32)
    lane = jnp.where(inside, here, 0).astype(F32)
    name = jnp.where(inside, owner + 1, 0).astype(F32)
    rounds = (jnp.max(seen).astype(jnp.int32) + SLOTS - 1) // SLOTS
    out[...] = jnp.zeros_like(out)

    def one_round(r, carry):
        names = []
        for g in range(4):
            hot = []
            for p in range(4 * g, 4 * g + 4):
                hot.append(rank[p : p + 1, :] == iota((SLOTS, 1024), 0) + r * SLOTS)
            hot = jnp.concatenate(hot, axis=0).astype(F32).astype(BF16)
            facts = jnp.concatenate([lane[4 * g : 4 * g + 4], name[4 * g : 4 * g + 4]], axis=0)
            found = lax.dot_general(facts.astype(BF16), hot, NT, preferred_element_type=F32)
            which = iota((1, 128), 1) // SLOTS
            at_lane, its_name = jnp.zeros((1, 128), F32), jnp.zeros((1, 128), F32)
            for p in range(4):
                at_lane = jnp.where(which == p, found[p : p + 1, :], at_lane)
                its_name = jnp.where(which == p, found[4 + p : 5 + p, :], its_name)
            spot = jnp.where(its_name > 0.5, at_lane.astype(jnp.int32) + which * 128, -1)
            pick = (iota((512, 128), 0) == spot).astype(F32).astype(BF16)
            got = jnp.dot(wide[:, 512 * g : 512 * g + 512], pick, preferred_element_type=F32)
            picked[:, 128 * g : 128 * g + 128] = got.astype(BF16)
            names.append(its_name)
        names = jnp.concatenate(names, axis=1)

        def one_owner(o, carry):
            member = (names == (o + 1).astype(F32)).astype(F32).astype(BF16)
            both = lax.dot_general(picked[...] * member, picked[...], NT, preferred_element_type=F32)
            total = (both[:128, :128] + both[128:, 128:]) + (both[:128, 128:] + both[128:, :128])
            out[o] += total * (2.0 ** -29)
            return carry

        lax.fori_loop(0, 32, one_owner, 0)
        return carry

    lax.fori_loop(0, rounds, one_round, 0)


def sum_kernel(gram, out, c_ref, ha, hb, a1, b1, sa, sb, a2, b2, sz, zr, s0, r0, s1, r1, s2, r2, s3, r3):
    z, x, y, core = place()

    barrier = pltpu.get_barrier_semaphore()
    greet(z, x, y, core, barrier)
    pl.semaphore_wait(barrier, 14)
    push(gram.at[:, :, :, 1 - core], c_ref, s0, r0, at(z, x, y, 1 - core))
    wait_bytes(c_ref, r0)

    def add_core(i, carry):
        for tx in range(4):
            for ty in range(4):
                ha[tx, i, ty] = gram[i, tx, ty, core, 0:8, :] + c_ref[i, tx, ty, 0:8, :]
                hb[ty, i, tx] = gram[i, tx, ty, core, 8:16, :] + c_ref[i, tx, ty, 8:16, :]
        return carry

    lax.fori_loop(0, 8, add_core, 0)
    for d in (2, 1, 3):
        tx, ty = (x + d) % 4, (y + d) % 4
        push(ha.at[tx], a1.at[x], s1.at[0], r1.at[0], at(z, tx, y, core))
        push(hb.at[ty], b1.at[y], s1.at[1], r1.at[1], at(z, x, ty, core))
    a1[x] = ha[x]
    b1[y] = hb[y]
    wait_bytes(a1.at[pl.ds(0, 3)], r1.at[0])
    wait_bytes(b1.at[pl.ds(0, 3)], r1.at[1])

    def add_first(i, carry):
        for t in range(4):
            sa[t, i] = (a1[0, i, t] + a1[1, i, t]) + (a1[2, i, t] + a1[3, i, t])
            sb[t, i] = (b1[0, i, t] + b1[1, i, t]) + (b1[2, i, t] + b1[3, i, t])
        return carry

    lax.fori_loop(0, 8, add_first, 0)
    for d in (2, 1, 3):
        tx, ty = (x + d) % 4, (y + d) % 4
        push(sa.at[ty], a2.at[y], s2.at[0], r2.at[0], at(z, x, ty, core))
        push(sb.at[tx], b2.at[x], s2.at[1], r2.at[1], at(z, tx, y, core))
    a2[y] = sa[y]
    b2[x] = sb[x]
    wait_bytes(a2.at[pl.ds(0, 3)], r2.at[0])
    wait_bytes(b2.at[pl.ds(0, 3)], r2.at[1])
    for i in range(8):
        sz[i, 0:8, :] = (a2[0, i] + a2[1, i]) + (a2[2, i] + a2[3, i])
        sz[i, 8:16, :] = (b2[0, i] + b2[1, i]) + (b2[2, i] + b2[3, i])
    for d in (4, 3, 5, 2, 6, 1, 7):
        tz = (z + d) % 8
        push(sz.at[tz], zr.at[z], s3, r3, at(tz, x, y, core))
    zr[z] = sz[z]
    wait_bytes(zr.at[pl.ds(0, 7)], r3)
    v = [zr[i] for i in range(8)]
    out[...] = ((v[0] + v[1]) + (v[2] + v[3])) + ((v[4] + v[5]) + (v[6] + v[7]))
    wait_bytes(c_ref, s0)
    for n in range(2):
        wait_bytes(a1.at[pl.ds(0, 3)], s1.at[n])
        wait_bytes(a2.at[pl.ds(0, 3)], s2.at[n])
    wait_bytes(zr.at[pl.ds(0, 7)], s3)


def body(panel, signs, offsets, owners):
    params = functools.partial(pltpu.CompilerParams, vmem_limit_bytes=48 << 20)
    dma = pltpu.SemaphoreType.DMA
    mixed, lists = pl.pallas_call(
        mix_kernel,
        out_shape=[
            jax.ShapeDtypeStruct((16, 4, 2, 16, 128), F32),
            jax.ShapeDtypeStruct((16, 16, 128), jnp.int32),
        ],
        in_specs=[pl.BlockSpec(memory_space=pl.ANY)] + [VMEM] * 3,
        out_specs=[VMEM] * 2,
        scratch_shapes=[
            pltpu.VMEM((16, 16384), F32),
            pltpu.VMEM((128, 16, 128), F32),
            pltpu.VMEM((128, 16, 128), F32),
            pltpu.VMEM((4, 16, 16, 128), F32),
            pltpu.VMEM((16, 128), jnp.int32),
            dma((4,)), dma, dma, dma, dma, dma, dma,
            pltpu.SemaphoreType.REGULAR, pltpu.SemaphoreType.REGULAR,
        ],
        compiler_params=params(has_side_effects=True, collective_id=1),
        name="mix",
    )(panel, signs.reshape(128, 128), offsets.reshape(8, 128), owners.reshape(8, 128))
    gram = pl.pallas_call(
        gram_kernel,
        out_shape=jax.ShapeDtypeStruct((32, 128, 128), F32),
        in_specs=[VMEM] * 2,
        out_specs=VMEM,
        scratch_shapes=[pltpu.VMEM((256, 2048), BF16), pltpu.VMEM((256, 512), BF16)],
        compiler_params=params(),
        name="gram",
    )(mixed.reshape(16, 128, 128), lists)
    summed = pl.pallas_call(
        sum_kernel,
        out_shape=jax.ShapeDtypeStruct((16, 128), F32),
        in_specs=[VMEM],
        out_specs=VMEM,
        scratch_shapes=[
            pltpu.VMEM((8, 4, 4, 16, 128), F32),
            pltpu.VMEM((4, 8, 4, 8, 128), F32),
            pltpu.VMEM((4, 8, 4, 8, 128), F32),
            pltpu.VMEM((4, 8, 4, 8, 128), F32),
            pltpu.VMEM((4, 8, 4, 8, 128), F32),
            pltpu.VMEM((4, 8, 8, 128), F32),
            pltpu.VMEM((4, 8, 8, 128), F32),
            pltpu.VMEM((4, 8, 8, 128), F32),
            pltpu.VMEM((4, 8, 8, 128), F32),
            pltpu.VMEM((8, 16, 128), F32),
            pltpu.VMEM((8, 16, 128), F32),
        ] + [dma] * 2 + [dma((2,))] * 4 + [dma] * 2,
        compiler_params=params(has_side_effects=True, collective_id=2),
        name="sum",
    )(gram.reshape(8, 4, 4, 2, 16, 128))
    return summed[None]


def solution(mesh):
    placed = (P("col", "row"), P("row"), P("row"), P("row", None))
    return jax.shard_map(
        body, mesh=mesh, in_specs=placed, out_specs=P("row", "col", None), check_vma=False
    )
```

```python
import functools

import jax
import jax.numpy as jnp
from jax import lax
from jax.experimental import pallas as pl
from jax.experimental.pallas import tpu as pltpu
from jax.sharding import PartitionSpec as P

MESH = pl.DeviceIdType.MESH
F32 = jnp.float32
BF16 = jnp.bfloat16
NT = (((1,), (1,)), ((), ()))
VMEM = pl.BlockSpec(memory_space=pltpu.VMEM)
HBM = pl.BlockSpec(memory_space=pltpu.HBM)
SLOTS = 32


def place():
    row, col = lax.axis_index("row"), lax.axis_index("col")
    return row // 4, row % 4, col // 2, col % 2


def at(z, x, y, core):
    return {"row": z * 4 + x, "col": y * 2 + core}


def iota(shape, dim):
    return lax.broadcasted_iota(jnp.int32, shape, dim)


def sylvester(order):
    v = iota((order, order), 0) & iota((order, order), 1)
    for shift in (4, 2, 1):
        v = v ^ (v >> shift)
    return (1 - 2 * (v & 1)).astype(F32)


def butterfly(vals):
    vals, step = list(vals), 1
    while step < len(vals):
        for i in range(len(vals)):
            if i & step == 0:
                a, b = vals[i], vals[i + step]
                vals[i], vals[i + step] = a + b, a - b
        step *= 2
    return vals


def split(v):
    hi = v.astype(BF16)
    return hi, (v - hi.astype(F32)).astype(BF16)


def wait_bytes(ref, sem):
    pltpu.make_async_copy(ref, ref, sem).wait()


def greet(z, x, y, core, barrier):
    for d in range(1, 8):
        tell(barrier, at((z + d) % 8, x, y, core))
    for d in range(1, 4):
        tell(barrier, at(z, (x + d) % 4, y, core))
        tell(barrier, at(z, x, (y + d) % 4, core))
    tell(barrier, at(z, x, y, 1 - core))


def tell(sem, where):
    pl.semaphore_signal(sem, inc=1, device_id=where, device_id_type=MESH)


def push(src, dst, send_sem, recv_sem, where):
    pltpu.make_async_remote_copy(
        src_ref=src, dst_ref=dst, send_sem=send_sem, recv_sem=recv_sem, device_id=where, device_id_type=MESH
    ).start()


def mix_kernel(
    panel_hbm, signs_hbm, offsets, owners, out, lists, panel, signs, y_ref, r_ref, t_ref, mine,
    load_sem, small_sem, send_sem, recv_sem, core_send, core_recv, list_send, list_recv, plane_sem, all_sem,
):
    z, x, y, core = place()
    barrier = pltpu.get_barrier_semaphore()
    greet(z, x, y, core, barrier)

    def load(i):
        span = pl.ds(4096 * i, 4096)
        return pltpu.make_async_copy(panel_hbm.at[:, span], panel.at[:, span], load_sem.at[i])

    small = [
        pltpu.make_async_copy(signs_hbm, signs, small_sem.at[0]),
        pltpu.make_async_copy(offsets, mine.at[pl.ds(0, 8)], small_sem.at[1]),
        pltpu.make_async_copy(owners, mine.at[pl.ds(8, 8)], small_sem.at[2]),
    ]
    small[0].start()
    for i in range(4):
        load(i).start()
    small[1].start()
    small[2].start()
    table = sylvester(128).astype(BF16)
    table = jnp.concatenate([table, table], axis=0)

    small[0].wait()
    for part in range(4):
        load(part).wait()
        for i in range(2 * part, 2 * part + 2):
            sign = signs[16 * i : 16 * i + 16, :].astype(F32)
            rows = []
            for j in range(16):
                start = (i * 16 + j) * 128
                rows.append(panel[:, start : start + 128] * sign[j : j + 1, :])
            hi, lo = split(jnp.concatenate(rows, axis=0))
            pieces = jnp.concatenate([hi, lo], axis=1)
            done = jnp.dot(pieces, table, preferred_element_type=F32)
            y_ref[16 * i : 16 * i + 16] = done.reshape(16, 16, 128)

    pl.semaphore_wait(barrier, 14)
    for d in range(1, 4):
        tell(plane_sem, at(z, (x + d) % 4, y, core))

    def outer_high(g, carry):
        vals = butterfly([y_ref[g + 8 * j] for j in range(16)])
        for j in range(16):
            y_ref[g + 8 * j] = vals[j]
        return carry

    lax.fori_loop(0, 8, outer_high, 0)
    pl.semaphore_wait(plane_sem, 3)
    for d in range(1, 4):
        tell(all_sem, at(z, x, (y + d) % 4, core))
    pl.semaphore_wait(all_sem, 3)

    slot = y * 32 + z * 4 + x
    to_x = [(x + d) % 4 for d in range(4)]
    to_y = [(y + d) % 4 for d in range(4)]
    sends_list = z // 4 == core

    small[1].wait()
    small[2].wait()

    def send(tz, dx, dy):
        push(
            y_ref.at[tz * 16 + to_x[dx] * 4 + to_y[dy]], r_ref.at[slot],
            send_sem, recv_sem.at[dy], at(tz, to_x[dx], to_y[dy], core),
        )

    def send_list(tz, dx):
        push(mine, lists.at[z % 4 * 4 + x], list_send, list_recv, at(tz, to_x[dx], y, core))

    def first(i, carry):
        tz = (z + i * 3 + 4) % 8
        for g in range(2):
            vals = butterfly([y_ref[tz * 16 + g * 8 + j] for j in range(8)])
            for j in range(8):
                y_ref[tz * 16 + g * 8 + j] = vals[j]
        for dx in range(4):
            if dx:
                send(tz, dx, 0)
                pl.when(sends_list)(functools.partial(send_list, tz, dx))
            else:
                pl.when(tz != z)(functools.partial(send, tz, 0, 0))
                pl.when(sends_list & (tz != z))(functools.partial(send_list, tz, 0))
        return carry

    lax.fori_loop(0, 8, first, 0)

    for dy in range(1, 4):
        def later(i, carry):
            for dx in range(4):
                send((z + i * 3 + 4) % 8, dx, dy)
            return carry

        lax.fori_loop(0, 8, later, 0)

    r_ref[slot] = y_ref[z * 16 + x * 4 + y]

    @pl.when(sends_list)
    def _():
        lists[z % 4 * 4 + x] = mine[...]
        wait_bytes(lists.at[pl.ds(0, 15)], list_recv)

    @pl.when(jnp.logical_not(sends_list))
    def _():
        wait_bytes(lists, list_recv)

    turn = (1 - 2 * core).astype(F32)

    def across(dy, carry):
        v = (y + 4 - dy) % 4
        for h in range(2):
            rows = pl.ds(8 * h, 8)
            low = [r_ref[v * 32 + q, rows, :] for q in range(16)]
            high = [r_ref[v * 32 + 16 + q, rows, :] * turn for q in range(16)]
            given = butterfly([a - b for a, b in zip(low, high)])
            for p in range(16):
                t_ref[v, p, rows, :] = given[p]
            kept = butterfly([a + b for a, b in zip(low, high)])
            for p in range(16):
                out[p, v, core, rows, :] = kept[p]
        push(t_ref.at[v], out.at[:, v, core], core_send, core_recv, at(z, x, y, 1 - core))
        return carry

    wait_bytes(r_ref.at[pl.ds(0, 31)], recv_sem.at[0])
    across(0, 0)

    def across_next(dy, carry):
        wait_bytes(r_ref.at[pl.ds(0, 32)], recv_sem.at[dy])
        return across(dy, carry)

    lax.fori_loop(1, 4, across_next, 0)
    wait_bytes(r_ref.at[pl.ds(0, 127)], send_sem)

    @pl.when(sends_list)
    def _():
        for n in range(31):
            wait_bytes(mine, list_send)

    wait_bytes(t_ref, core_send)
    wait_bytes(t_ref, core_recv)


def gram_kernel(mixed, lists, out, wide, picked):
    z, x, y, core = place()
    slab = z * 16 + x * 4 + y
    for p in range(16):
        hi, lo = split(mixed[p])
        wide[0:128, 128 * p : 128 * p + 128] = hi
        wide[128:256, 128 * p : 128 * p + 128] = lo
    here = jnp.concatenate([lists[:, b, :] for b in range(8)], axis=1) - slab * 128
    owner = jnp.concatenate([lists[:, 8 + b, :] for b in range(8)], axis=1)
    inside = (here >= 0) & (here < 128)
    mask = jnp.where(inside, 1.0, 0.0).astype(F32)
    before = (iota((128, 128), 0) < iota((128, 128), 1)).astype(F32).astype(BF16)
    rank, seen = [], jnp.zeros((16, 1), F32)
    for b in range(8):
        piece = mask[:, 128 * b : 128 * b + 128]
        rank.append(jnp.dot(piece.astype(BF16), before, preferred_element_type=F32) + seen)
        seen = seen + jnp.sum(piece, axis=1, keepdims=True)
    rank = jnp.where(inside, jnp.concatenate(rank, axis=1), -1.0).astype(jnp.int32)
    lane = jnp.where(inside, here, 0).astype(F32)
    name = jnp.where(inside, owner + 1, 0).astype(F32)
    rounds = (jnp.max(seen).astype(jnp.int32) + SLOTS - 1) // SLOTS
    out[...] = jnp.zeros_like(out)

    def one_round(r, carry):
        names = []
        for g in range(4):
            hot = []
            for p in range(4 * g, 4 * g + 4):
                hot.append(rank[p : p + 1, :] == iota((SLOTS, 1024), 0) + r * SLOTS)
            hot = jnp.concatenate(hot, axis=0).astype(F32).astype(BF16)
            facts = jnp.concatenate([lane[4 * g : 4 * g + 4], name[4 * g : 4 * g + 4]], axis=0)
            found = lax.dot_general(facts.astype(BF16), hot, NT, preferred_element_type=F32)
            which = iota((1, 128), 1) // SLOTS
            at_lane, its_name = jnp.zeros((1, 128), F32), jnp.zeros((1, 128), F32)
            for p in range(4):
                at_lane = jnp.where(which == p, found[p : p + 1, :], at_lane)
                its_name = jnp.where(which == p, found[4 + p : 5 + p, :], its_name)
            spot = jnp.where(its_name > 0.5, at_lane.astype(jnp.int32) + which * 128, -1)
            pick = (iota((512, 128), 0) == spot).astype(F32).astype(BF16)
            got = jnp.dot(wide[:, 512 * g : 512 * g + 512], pick, preferred_element_type=F32)
            picked[:, 128 * g : 128 * g + 128] = got.astype(BF16)
            names.append(its_name)
        names = jnp.concatenate(names, axis=1)

        def one_owner(o, carry):
            member = (names == (o + 1).astype(F32)).astype(F32).astype(BF16)
            both = lax.dot_general(picked[...] * member, picked[...], NT, preferred_element_type=F32)
            total = (both[:128, :128] + both[128:, 128:]) + (both[:128, 128:] + both[128:, :128])
            out[o] += total * (2.0 ** -29)
            return carry

        lax.fori_loop(0, 32, one_owner, 0)
        return carry

    lax.fori_loop(0, rounds, one_round, 0)


def sum_kernel(gram, out, c_ref, ha, hb, a1, b1, sa, sb, a2, b2, sz, zr, s0, r0, s1, r1, s2, r2, s3, r3):
    z, x, y, core = place()

    barrier = pltpu.get_barrier_semaphore()
    greet(z, x, y, core, barrier)
    pl.semaphore_wait(barrier, 14)
    push(gram.at[:, :, :, 1 - core], c_ref, s0, r0, at(z, x, y, 1 - core))
    wait_bytes(c_ref, r0)

    def add_core(i, carry):
        for tx in range(4):
            for ty in range(4):
                ha[tx, i, ty] = gram[i, tx, ty, core, 0:8, :] + c_ref[i, tx, ty, 0:8, :]
                hb[ty, i, tx] = gram[i, tx, ty, core, 8:16, :] + c_ref[i, tx, ty, 8:16, :]
        return carry

    lax.fori_loop(0, 8, add_core, 0)
    for d in (2, 1, 3):
        tx, ty = (x + d) % 4, (y + d) % 4
        push(ha.at[tx], a1.at[x], s1.at[0], r1.at[0], at(z, tx, y, core))
        push(hb.at[ty], b1.at[y], s1.at[1], r1.at[1], at(z, x, ty, core))
    a1[x] = ha[x]
    b1[y] = hb[y]
    wait_bytes(a1.at[pl.ds(0, 3)], r1.at[0])
    wait_bytes(b1.at[pl.ds(0, 3)], r1.at[1])

    def add_first(i, carry):
        for t in range(4):
            sa[t, i] = (a1[0, i, t] + a1[1, i, t]) + (a1[2, i, t] + a1[3, i, t])
            sb[t, i] = (b1[0, i, t] + b1[1, i, t]) + (b1[2, i, t] + b1[3, i, t])
        return carry

    lax.fori_loop(0, 8, add_first, 0)
    for d in (2, 1, 3):
        tx, ty = (x + d) % 4, (y + d) % 4
        push(sa.at[ty], a2.at[y], s2.at[0], r2.at[0], at(z, x, ty, core))
        push(sb.at[tx], b2.at[x], s2.at[1], r2.at[1], at(z, tx, y, core))
    a2[y] = sa[y]
    b2[x] = sb[x]
    wait_bytes(a2.at[pl.ds(0, 3)], r2.at[0])
    wait_bytes(b2.at[pl.ds(0, 3)], r2.at[1])
    for i in range(8):
        sz[i, 0:8, :] = (a2[0, i] + a2[1, i]) + (a2[2, i] + a2[3, i])
        sz[i, 8:16, :] = (b2[0, i] + b2[1, i]) + (b2[2, i] + b2[3, i])
    for d in (4, 3, 5, 2, 6, 1, 7):
        tz = (z + d) % 8
        push(sz.at[tz], zr.at[z], s3, r3, at(tz, x, y, core))
    zr[z] = sz[z]
    wait_bytes(zr.at[pl.ds(0, 7)], r3)
    v = [zr[i] for i in range(8)]
    out[...] = ((v[0] + v[1]) + (v[2] + v[3])) + ((v[4] + v[5]) + (v[6] + v[7]))
    wait_bytes(c_ref, s0)
    for n in range(2):
        wait_bytes(a1.at[pl.ds(0, 3)], s1.at[n])
        wait_bytes(a2.at[pl.ds(0, 3)], s2.at[n])
    wait_bytes(zr.at[pl.ds(0, 7)], s3)


def body(panel, signs, offsets, owners):
    params = functools.partial(pltpu.CompilerParams, vmem_limit_bytes=48 << 20)
    dma = pltpu.SemaphoreType.DMA
    mixed, lists = pl.pallas_call(
        mix_kernel,
        out_shape=[
            jax.ShapeDtypeStruct((16, 4, 2, 16, 128), F32),
            jax.ShapeDtypeStruct((16, 16, 128), jnp.int32),
        ],
        in_specs=[HBM] * 4,
        out_specs=[VMEM] * 2,
        scratch_shapes=[
            pltpu.VMEM((16, 16384), F32),
            pltpu.VMEM((128, 128), jnp.int32),
            pltpu.VMEM((128, 16, 128), F32),
            pltpu.VMEM((128, 16, 128), F32),
            pltpu.VMEM((4, 16, 16, 128), F32),
            pltpu.VMEM((16, 128), jnp.int32),
            dma((4,)), dma((3,)), dma, dma((4,)), dma, dma, dma, dma,
            pltpu.SemaphoreType.REGULAR, pltpu.SemaphoreType.REGULAR,
        ],
        compiler_params=params(has_side_effects=True, collective_id=1),
        name="mix",
    )(panel, signs.reshape(128, 128), offsets.reshape(8, 128), owners.reshape(8, 128))
    gram = pl.pallas_call(
        gram_kernel,
        out_shape=jax.ShapeDtypeStruct((32, 128, 128), F32),
        in_specs=[VMEM] * 2,
        out_specs=VMEM,
        scratch_shapes=[pltpu.VMEM((256, 2048), BF16), pltpu.VMEM((256, 512), BF16)],
        compiler_params=params(),
        name="gram",
    )(mixed.reshape(16, 128, 128), lists)
    summed = pl.pallas_call(
        sum_kernel,
        out_shape=jax.ShapeDtypeStruct((16, 128), F32),
        in_specs=[VMEM],
        out_specs=VMEM,
        scratch_shapes=[
            pltpu.VMEM((8, 4, 4, 16, 128), F32),
            pltpu.VMEM((4, 8, 4, 8, 128), F32),
            pltpu.VMEM((4, 8, 4, 8, 128), F32),
            pltpu.VMEM((4, 8, 4, 8, 128), F32),
            pltpu.VMEM((4, 8, 4, 8, 128), F32),
            pltpu.VMEM((4, 8, 8, 128), F32),
            pltpu.VMEM((4, 8, 8, 128), F32),
            pltpu.VMEM((4, 8, 8, 128), F32),
            pltpu.VMEM((4, 8, 8, 128), F32),
            pltpu.VMEM((8, 16, 128), F32),
            pltpu.VMEM((8, 16, 128), F32),
        ] + [dma] * 2 + [dma((2,))] * 4 + [dma] * 2,
        compiler_params=params(has_side_effects=True, collective_id=2),
        name="sum",
    )(gram.reshape(8, 4, 4, 2, 16, 128))
    return summed[None]


def solution(mesh):
    placed = (P("col", "row"), P("row"), P("row"), P("row", None))
    return jax.shard_map(
        body, mesh=mesh, in_specs=placed, out_specs=P("row", "col", None), check_vma=False
    )
```

```python
import functools

import jax
import jax.numpy as jnp
from jax import lax
from jax.experimental import pallas as pl
from jax.experimental.pallas import tpu as pltpu
from jax.sharding import PartitionSpec as P

MESH = pl.DeviceIdType.MESH
F32 = jnp.float32
BF16 = jnp.bfloat16
NT = (((1,), (1,)), ((), ()))
VMEM = pl.BlockSpec(memory_space=pltpu.VMEM)
HBM = pl.BlockSpec(memory_space=pltpu.HBM)
SLOTS = 32
MIX_VMEM = 60 << 20
GRAM_SCALE = 2.0 ** -29


def place():
    row, col = lax.axis_index("row"), lax.axis_index("col")
    return row // 4, row % 4, col // 2, col % 2


def at(z, x, y, core):
    return {"row": z * 4 + x, "col": y * 2 + core}


def iota(shape, dim):
    return lax.broadcasted_iota(jnp.int32, shape, dim)


def sylvester(order):
    v = iota((order, order), 0) & iota((order, order), 1)
    for shift in (4, 2, 1):
        v = v ^ (v >> shift)
    return (1 - 2 * (v & 1)).astype(F32)


def butterfly(vals):
    vals, step = list(vals), 1
    while step < len(vals):
        for i in range(len(vals)):
            if i & step == 0:
                a, b = vals[i], vals[i + step]
                vals[i], vals[i + step] = a + b, a - b
        step *= 2
    return vals


def split(v):
    hi = v.astype(BF16)
    return hi, (v - hi.astype(F32)).astype(BF16)


def wait_bytes(ref, sem):
    pltpu.make_async_copy(ref, ref, sem).wait()


def greet(z, x, y, core, barrier):
    for d in range(1, 8):
        tell(barrier, at((z + d) % 8, x, y, core))
    for d in range(1, 4):
        tell(barrier, at(z, (x + d) % 4, y, core))
        tell(barrier, at(z, x, (y + d) % 4, core))
    tell(barrier, at(z, x, y, 1 - core))


def tell(sem, where):
    pl.semaphore_signal(sem, inc=1, device_id=where, device_id_type=MESH)


def push(src, dst, send_sem, recv_sem, where):
    pltpu.make_async_remote_copy(
        src_ref=src, dst_ref=dst, send_sem=send_sem, recv_sem=recv_sem, device_id=where, device_id_type=MESH
    ).start()


def mix_kernel(
    panel_hbm, signs_hbm, offsets, owners, result, crowded, lists, kept_hbm,
    panel, signs, y_ref, r_ref, t_ref, mine, out, picks, names, picked, full_here, full_there,
    g_ref, c_ref, ha, hb, a1, b1, sa, sb, a2, b2, sz, zr,
    load_sem, small_sem, send_sem, recv_sem, core_send, core_recv, list_send, list_recv, plane_sem, all_sem,
    keep_sem, full_send, full_recv, s0, r0, s1, r1a, r1b, s2, r2a, r2b, s3, r3,
):
    z, x, y, core = place()
    barrier = pltpu.get_barrier_semaphore()
    greet(z, x, y, core, barrier)

    def load(i):
        span = pl.ds(4096 * i, 4096)
        return pltpu.make_async_copy(panel_hbm.at[:, span], panel.at[:, span], load_sem.at[i])

    small = [
        pltpu.make_async_copy(signs_hbm, signs, small_sem.at[0]),
        pltpu.make_async_copy(offsets, mine.at[pl.ds(0, 8)], small_sem.at[1]),
        pltpu.make_async_copy(owners, mine.at[pl.ds(8, 8)], small_sem.at[2]),
    ]
    small[0].start()
    for i in range(4):
        load(i).start()
    small[1].start()
    small[2].start()
    table = sylvester(128).astype(BF16)
    table = jnp.concatenate([table, table], axis=0)

    small[0].wait()
    for part in range(4):
        load(part).wait()
        for i in range(2 * part, 2 * part + 2):
            sign = signs[16 * i : 16 * i + 16, :].astype(F32)
            rows = []
            for j in range(16):
                start = (i * 16 + j) * 128
                rows.append(panel[:, start : start + 128] * sign[j : j + 1, :])
            hi, lo = split(jnp.concatenate(rows, axis=0))
            pieces = jnp.concatenate([hi, lo], axis=1)
            done = jnp.dot(pieces, table, preferred_element_type=F32)
            y_ref[16 * i : 16 * i + 16] = done.reshape(16, 16, 128)

    pl.semaphore_wait(barrier, 14)
    for d in range(1, 4):
        tell(plane_sem, at(z, (x + d) % 4, y, core))

    def outer_high(g, carry):
        vals = butterfly([y_ref[g + 8 * j] for j in range(16)])
        for j in range(16):
            y_ref[g + 8 * j] = vals[j]
        return carry

    lax.fori_loop(0, 8, outer_high, 0)
    pl.semaphore_wait(plane_sem, 3)
    for d in range(1, 4):
        tell(all_sem, at(z, x, (y + d) % 4, core))
    pl.semaphore_wait(all_sem, 3)

    slot = y * 32 + z * 4 + x
    to_x = [(x + d) % 4 for d in range(4)]
    to_y = [(y + d) % 4 for d in range(4)]
    sends_list = z // 4 == core

    small[1].wait()
    small[2].wait()

    def send(tz, dx, dy):
        push(
            y_ref.at[tz * 16 + to_x[dx] * 4 + to_y[dy]], r_ref.at[slot],
            send_sem, recv_sem.at[dy], at(tz, to_x[dx], to_y[dy], core),
        )

    def send_list(tz, dx):
        push(mine, lists.at[z % 4 * 4 + x], list_send, list_recv, at(tz, to_x[dx], y, core))

    def first(i, carry):
        tz = (z + i * 3 + 4) % 8
        for g in range(2):
            vals = butterfly([y_ref[tz * 16 + g * 8 + j] for j in range(8)])
            for j in range(8):
                y_ref[tz * 16 + g * 8 + j] = vals[j]
        for dx in range(4):
            if dx:
                send(tz, dx, 0)
                pl.when(sends_list)(functools.partial(send_list, tz, dx))
            else:
                pl.when(tz != z)(functools.partial(send, tz, 0, 0))
                pl.when(sends_list & (tz != z))(functools.partial(send_list, tz, 0))
        return carry

    lax.fori_loop(0, 8, first, 0)

    for dy in range(1, 4):
        def later(i, carry):
            for dx in range(4):
                send((z + i * 3 + 4) % 8, dx, dy)
            return carry

        lax.fori_loop(0, 8, later, 0)

    r_ref[slot] = y_ref[z * 16 + x * 4 + y]

    @pl.when(sends_list)
    def _():
        lists[z % 4 * 4 + x] = mine[...]
        wait_bytes(lists.at[pl.ds(0, 15)], list_recv)

    @pl.when(jnp.logical_not(sends_list))
    def _():
        wait_bytes(lists, list_recv)

    turn = (1 - 2 * core).astype(F32)

    def across(dy, carry):
        v = (y + 4 - dy) % 4
        for h in range(2):
            rows = pl.ds(8 * h, 8)
            low = [r_ref[v * 32 + q, rows, :] for q in range(16)]
            high = [r_ref[v * 32 + 16 + q, rows, :] * turn for q in range(16)]
            given = butterfly([a - b for a, b in zip(low, high)])
            for p in range(16):
                t_ref[v, p, rows, :] = given[p]
            kept = butterfly([a + b for a, b in zip(low, high)])
            for p in range(16):
                out[p, v, core, rows, :] = kept[p]
        push(t_ref.at[v], out.at[:, v, core], core_send, core_recv, at(z, x, y, 1 - core))
        return carry

    rank, lane, name, seen = ranked(lists, z * 16 + x * 4 + y)
    for g in range(4):
        pick, its_name = chosen(rank, lane, name, g, 0.0)
        picks[g] = pick
        names[0:1, 128 * g : 128 * g + 128] = its_name

    def tally(p, most):
        slabs = lists[p, 0:8, :] // 128
        count = jnp.zeros((128, 128), F32)
        for b in range(8):
            count = count + (slabs[b : b + 1, :] == iota((128, 128), 0)).astype(F32)
        return jnp.maximum(most, jnp.sum(count, axis=1, keepdims=True))

    most = lax.fori_loop(0, 16, tally, jnp.zeros((128, 1), F32))
    most = jnp.max(most, axis=0, keepdims=True)
    full_here[...] = jnp.broadcast_to(jnp.where(most > SLOTS, 1.0, 0.0), (8, 128))
    push(full_here, full_there, full_send, full_recv, at(z, x, y, 1 - core))

    wait_bytes(r_ref.at[pl.ds(0, 31)], recv_sem.at[0])
    across(0, 0)

    def across_next(dy, carry):
        wait_bytes(r_ref.at[pl.ds(0, 32)], recv_sem.at[dy])
        return across(dy, carry)

    lax.fori_loop(1, 4, across_next, 0)
    wait_bytes(t_ref, core_recv)
    keep = pltpu.make_async_copy(out, kept_hbm, keep_sem)
    keep.start()
    for g in range(4):
        got = jnp.dot(stacked(out, g), picks[g], preferred_element_type=F32)
        picked[:, 128 * g : 128 * g + 128] = got.astype(BF16)

    def make(i):
        for tx in range(4):
            total = owner_gram(picked[...], names[0:1, :], i * 4 + tx)
            g_ref[i, tx] = total.reshape(4, 2, 16, 128)
        push(g_ref.at[i, :, :, 1 - core], c_ref.at[i], s0, r0.at[i], at(z, x, y, 1 - core))

    def forward(i):
        wait_bytes(c_ref.at[i], r0.at[i])
        for tx in range(4):
            for ty in range(4):
                ha[i, tx, ty] = g_ref[i, tx, ty, core, 0:8, :] + c_ref[i, tx, ty, 0:8, :]
                hb[i, ty, tx] = g_ref[i, tx, ty, core, 8:16, :] + c_ref[i, tx, ty, 8:16, :]
        for d in (2, 1, 3):
            push(ha.at[i, to_x[d]], a1.at[x, i], s1.at[0], r1a.at[i // 4], at(z, to_x[d], y, core))
            push(hb.at[i, to_y[d]], b1.at[y, i], s1.at[1], r1b.at[i // 4], at(z, x, to_y[d], core))
        a1[x, i] = ha[i, x]
        b1[y, i] = hb[i, y]

    def step(i, carry):
        make(i)
        forward(i - 1)
        return carry

    make(jnp.int32(0))
    lax.fori_loop(1, 8, step, 0)
    forward(jnp.int32(7))

    for h in range(2):
        wait_bytes(a1.at[pl.ds(0, 3), pl.ds(0, 4)], r1a.at[h])
        wait_bytes(b1.at[pl.ds(0, 3), pl.ds(0, 4)], r1b.at[h])
        for i in range(4):
            for t in range(4):
                n = 4 * h + i
                sa[h, t, i] = (a1[0, n, t] + a1[1, n, t]) + (a1[2, n, t] + a1[3, n, t])
                sb[h, t, i] = (b1[0, n, t] + b1[1, n, t]) + (b1[2, n, t] + b1[3, n, t])
        for d in (2, 1, 3):
            push(sa.at[h, to_y[d]], a2.at[h, y], s2.at[0], r2a.at[h], at(z, x, to_y[d], core))
            push(sb.at[h, to_x[d]], b2.at[h, x], s2.at[1], r2b.at[h], at(z, to_x[d], y, core))
        a2[h, y] = sa[h, y]
        b2[h, x] = sb[h, x]

    for h in range(2):
        wait_bytes(a2.at[h, pl.ds(0, 3)], r2a.at[h])
        wait_bytes(b2.at[h, pl.ds(0, 3)], r2b.at[h])
        for i in range(4):
            n = 4 * h + i
            sz[n, 0:8, :] = (a2[h, 0, i] + a2[h, 1, i]) + (a2[h, 2, i] + a2[h, 3, i])
            sz[n, 8:16, :] = (b2[h, 0, i] + b2[h, 1, i]) + (b2[h, 2, i] + b2[h, 3, i])
            pl.when(z != n)(functools.partial(push, sz.at[n], zr.at[z], s3, r3, at(n, x, y, core)))

    zr[z] = sz[z]
    wait_bytes(zr.at[pl.ds(0, 7)], r3)
    v = [zr[i] for i in range(8)]
    total = ((v[0] + v[1]) + (v[2] + v[3])) + ((v[4] + v[5]) + (v[6] + v[7]))
    result[...] = total * GRAM_SCALE
    wait_bytes(full_there, full_recv)
    crowded[...] = jnp.maximum(full_here[...], full_there[...])

    wait_bytes(r_ref.at[pl.ds(0, 127)], send_sem)

    @pl.when(sends_list)
    def _():
        for n in range(31):
            wait_bytes(mine, list_send)

    keep.wait()
    wait_bytes(full_here, full_send)
    wait_bytes(t_ref, core_send)
    wait_bytes(c_ref, s0)
    wait_bytes(a1.at[pl.ds(0, 3)], s1.at[0])
    wait_bytes(b1.at[pl.ds(0, 3)], s1.at[1])
    wait_bytes(a2.at[:, pl.ds(0, 3)], s2.at[0])
    wait_bytes(b2.at[:, pl.ds(0, 3)], s2.at[1])
    wait_bytes(zr.at[pl.ds(0, 7)], s3)


def ranked(lists, slab):
    here = jnp.concatenate([lists[:, b, :] for b in range(8)], axis=1) - slab * 128
    owner = jnp.concatenate([lists[:, 8 + b, :] for b in range(8)], axis=1)
    inside = (here >= 0) & (here < 128)
    mask = jnp.where(inside, 1.0, 0.0).astype(F32)
    before = (iota((128, 128), 0) < iota((128, 128), 1)).astype(F32).astype(BF16)
    rank, seen = [], jnp.zeros((16, 1), F32)
    for b in range(8):
        piece = mask[:, 128 * b : 128 * b + 128]
        rank.append(jnp.dot(piece.astype(BF16), before, preferred_element_type=F32) + seen)
        seen = seen + jnp.sum(piece, axis=1, keepdims=True)
    rank = jnp.where(inside, jnp.concatenate(rank, axis=1), -1.0)
    lane = jnp.where(inside, here, 0).astype(F32)
    name = jnp.where(inside, owner + 1, 0).astype(F32)
    return rank, lane, name, seen


def chosen(rank, lane, name, g, first):
    wanted = iota((SLOTS, 1024), 0).astype(F32) + first
    hot = [rank[p : p + 1, :] == wanted for p in range(4 * g, 4 * g + 4)]
    hot = jnp.concatenate([h.astype(F32) for h in hot], axis=0).astype(BF16)
    facts = jnp.concatenate([lane[4 * g : 4 * g + 4], name[4 * g : 4 * g + 4]], axis=0)
    found = lax.dot_general(facts.astype(BF16), hot, NT, preferred_element_type=F32)
    which = iota((1, 128), 1) // SLOTS
    at_lane, its_name = jnp.zeros((1, 128), F32), jnp.zeros((1, 128), F32)
    for p in range(4):
        at_lane = jnp.where(which == p, found[p : p + 1, :] + 128.0 * p, at_lane)
        its_name = jnp.where(which == p, found[4 + p : 5 + p, :], its_name)
    spot = jnp.where(its_name > 0.5, at_lane, -1.0)
    pick = (iota((512, 128), 0).astype(F32) == spot).astype(F32).astype(BF16)
    return pick, its_name


def stacked(mixed, g):
    columns = []
    for p in range(4 * g, 4 * g + 4):
        hi, lo = split(mixed[p].reshape(128, 128))
        columns.append(jnp.concatenate([hi, lo], axis=0))
    return jnp.concatenate(columns, axis=1)


def owner_gram(picked, names, o):
    member = (names == o.astype(F32) + 1.0).astype(F32).astype(BF16)
    both = lax.dot_general(picked * member, picked, NT, preferred_element_type=F32)
    return (both[:128, :128] + both[128:, 128:]) + (both[:128, 128:] + both[128:, :128])


def gram_kernel(mixed, lists, out, picked):
    z, x, y, core = place()
    rank, lane, name, seen = ranked(lists, z * 16 + x * 4 + y)
    rounds = (jnp.max(seen).astype(jnp.int32) + SLOTS - 1) // SLOTS
    out[...] = jnp.zeros_like(out)

    def one_round(r, carry):
        names = []
        for g in range(4):
            pick, its_name = chosen(rank, lane, name, g, (r * SLOTS).astype(F32))
            got = jnp.dot(stacked(mixed, g), pick, preferred_element_type=F32)
            picked[:, 128 * g : 128 * g + 128] = got.astype(BF16)
            names.append(its_name)
        names = jnp.concatenate(names, axis=1)

        def one_owner(o, carry):
            out[o] += owner_gram(picked[...], names, o) * GRAM_SCALE
            return carry

        lax.fori_loop(0, 32, one_owner, 0)
        return carry

    lax.fori_loop(1, rounds, one_round, 0)


def sum_kernel(gram, out, c_ref, ha, hb, a1, b1, sa, sb, a2, b2, sz, zr, s0, r0, s1, r1, s2, r2, s3, r3):
    z, x, y, core = place()

    barrier = pltpu.get_barrier_semaphore()
    greet(z, x, y, core, barrier)
    pl.semaphore_wait(barrier, 14)
    push(gram.at[:, :, :, 1 - core], c_ref, s0, r0, at(z, x, y, 1 - core))
    wait_bytes(c_ref, r0)

    def add_core(i, carry):
        for tx in range(4):
            for ty in range(4):
                ha[tx, i, ty] = gram[i, tx, ty, core, 0:8, :] + c_ref[i, tx, ty, 0:8, :]
                hb[ty, i, tx] = gram[i, tx, ty, core, 8:16, :] + c_ref[i, tx, ty, 8:16, :]
        return carry

    lax.fori_loop(0, 8, add_core, 0)
    for d in (2, 1, 3):
        tx, ty = (x + d) % 4, (y + d) % 4
        push(ha.at[tx], a1.at[x], s1.at[0], r1.at[0], at(z, tx, y, core))
        push(hb.at[ty], b1.at[y], s1.at[1], r1.at[1], at(z, x, ty, core))
    a1[x] = ha[x]
    b1[y] = hb[y]
    wait_bytes(a1.at[pl.ds(0, 3)], r1.at[0])
    wait_bytes(b1.at[pl.ds(0, 3)], r1.at[1])

    def add_first(i, carry):
        for t in range(4):
            sa[t, i] = (a1[0, i, t] + a1[1, i, t]) + (a1[2, i, t] + a1[3, i, t])
            sb[t, i] = (b1[0, i, t] + b1[1, i, t]) + (b1[2, i, t] + b1[3, i, t])
        return carry

    lax.fori_loop(0, 8, add_first, 0)
    for d in (2, 1, 3):
        tx, ty = (x + d) % 4, (y + d) % 4
        push(sa.at[ty], a2.at[y], s2.at[0], r2.at[0], at(z, x, ty, core))
        push(sb.at[tx], b2.at[x], s2.at[1], r2.at[1], at(z, tx, y, core))
    a2[y] = sa[y]
    b2[x] = sb[x]
    wait_bytes(a2.at[pl.ds(0, 3)], r2.at[0])
    wait_bytes(b2.at[pl.ds(0, 3)], r2.at[1])
    for i in range(8):
        sz[i, 0:8, :] = (a2[0, i] + a2[1, i]) + (a2[2, i] + a2[3, i])
        sz[i, 8:16, :] = (b2[0, i] + b2[1, i]) + (b2[2, i] + b2[3, i])
    for d in (4, 3, 5, 2, 6, 1, 7):
        tz = (z + d) % 8
        push(sz.at[tz], zr.at[z], s3, r3, at(tz, x, y, core))
    zr[z] = sz[z]
    wait_bytes(zr.at[pl.ds(0, 7)], r3)
    v = [zr[i] for i in range(8)]
    out[...] = ((v[0] + v[1]) + (v[2] + v[3])) + ((v[4] + v[5]) + (v[6] + v[7]))
    wait_bytes(c_ref, s0)
    for n in range(2):
        wait_bytes(a1.at[pl.ds(0, 3)], s1.at[n])
        wait_bytes(a2.at[pl.ds(0, 3)], s2.at[n])
    wait_bytes(zr.at[pl.ds(0, 7)], s3)


def body(panel, signs, offsets, owners):
    params = functools.partial(pltpu.CompilerParams, has_side_effects=True)
    dma, vmem = pltpu.SemaphoreType.DMA, pltpu.VMEM
    result, crowded, lists, mixed = pl.pallas_call(
        mix_kernel,
        out_shape=[
            jax.ShapeDtypeStruct((16, 128), F32),
            jax.ShapeDtypeStruct((8, 128), F32),
            jax.ShapeDtypeStruct((16, 16, 128), jnp.int32),
            jax.ShapeDtypeStruct((16, 4, 2, 16, 128), F32),
        ],
        in_specs=[HBM] * 4,
        out_specs=[VMEM] * 3 + [HBM],
        scratch_shapes=[
            vmem((16, 16384), F32),
            vmem((128, 128), jnp.int32),
            vmem((128, 16, 128), F32),
            vmem((128, 16, 128), F32),
            vmem((4, 16, 16, 128), F32),
            vmem((16, 128), jnp.int32),
            vmem((16, 4, 2, 16, 128), F32),
            vmem((4, 512, 128), BF16),
            vmem((8, 512), F32),
            vmem((256, 512), BF16),
            vmem((8, 128), F32),
            vmem((8, 128), F32),
            vmem((8, 4, 4, 2, 16, 128), F32),
            vmem((8, 4, 4, 16, 128), F32),
            vmem((8, 4, 4, 8, 128), F32),
            vmem((8, 4, 4, 8, 128), F32),
            vmem((4, 8, 4, 8, 128), F32),
            vmem((4, 8, 4, 8, 128), F32),
            vmem((2, 4, 4, 8, 128), F32),
            vmem((2, 4, 4, 8, 128), F32),
            vmem((2, 4, 4, 8, 128), F32),
            vmem((2, 4, 4, 8, 128), F32),
            vmem((8, 16, 128), F32),
            vmem((8, 16, 128), F32),
            dma((4,)), dma((3,)), dma, dma((4,)), dma, dma, dma, dma,
            pltpu.SemaphoreType.REGULAR, pltpu.SemaphoreType.REGULAR,
            dma, dma, dma, dma, dma((8,)), dma((2,)), dma((2,)), dma((2,)),
            dma((2,)), dma((2,)), dma((2,)), dma, dma,
        ],
        compiler_params=params(collective_id=1, vmem_limit_bytes=MIX_VMEM),
        name="mix",
    )(panel, signs.reshape(128, 128), offsets.reshape(8, 128), owners.reshape(8, 128))

    def add_rest(result):
        gram = pl.pallas_call(
            gram_kernel,
            out_shape=jax.ShapeDtypeStruct((32, 128, 128), F32),
            in_specs=[VMEM] * 2,
            out_specs=VMEM,
            scratch_shapes=[vmem((256, 512), BF16)],
            compiler_params=pltpu.CompilerParams(vmem_limit_bytes=48 << 20),
            name="gram_rest",
        )(mixed.reshape(16, 128, 128), lists)
        rest = pl.pallas_call(
            sum_kernel,
            out_shape=jax.ShapeDtypeStruct((16, 128), F32),
            in_specs=[VMEM],
            out_specs=VMEM,
            scratch_shapes=[
                vmem((8, 4, 4, 16, 128), F32),
                vmem((4, 8, 4, 8, 128), F32),
                vmem((4, 8, 4, 8, 128), F32),
                vmem((4, 8, 4, 8, 128), F32),
                vmem((4, 8, 4, 8, 128), F32),
                vmem((4, 8, 8, 128), F32),
                vmem((4, 8, 8, 128), F32),
                vmem((4, 8, 8, 128), F32),
                vmem((4, 8, 8, 128), F32),
                vmem((8, 16, 128), F32),
                vmem((8, 16, 128), F32),
            ] + [dma] * 2 + [dma((2,))] * 4 + [dma] * 2,
            compiler_params=params(collective_id=2, vmem_limit_bytes=48 << 20),
            name="sum_rest",
        )(gram.reshape(8, 4, 4, 2, 16, 128))
        return result + rest

    return lax.cond(crowded[0, 0] > 0.5, add_rest, lambda r: r, result)[None]


def solution(mesh):
    placed = (P("col", "row"), P("row"), P("row"), P("row", None))
    return jax.shard_map(
        body, mesh=mesh, in_specs=placed, out_specs=P("row", "col", None), check_vma=False
    )
```

```python
import functools

import jax
import jax.numpy as jnp
from jax import lax
from jax.experimental import pallas as pl
from jax.experimental.pallas import tpu as pltpu
from jax.sharding import PartitionSpec as P

MESH = pl.DeviceIdType.MESH
F32 = jnp.float32
BF16 = jnp.bfloat16
NT = (((1,), (1,)), ((), ()))
VMEM = pl.BlockSpec(memory_space=pltpu.VMEM)
SMEM = pl.BlockSpec(memory_space=pltpu.SMEM)
HBM = pl.BlockSpec(memory_space=pltpu.HBM)
SLOTS = 32
TAKEN = 256
MIX_VMEM = 60 << 20
GRAM_SCALE = 2.0 ** -29


def place():
    row, col = lax.axis_index("row"), lax.axis_index("col")
    return row // 4, row % 4, col // 2, col % 2


def at(z, x, y, core):
    return {"row": z * 4 + x, "col": y * 2 + core}


def iota(shape, dim):
    return lax.broadcasted_iota(jnp.int32, shape, dim)


def sylvester(order):
    v = iota((order, order), 0) & iota((order, order), 1)
    for shift in (4, 2, 1):
        v = v ^ (v >> shift)
    return (1 - 2 * (v & 1)).astype(F32)


def butterfly(vals):
    vals, step = list(vals), 1
    while step < len(vals):
        for i in range(len(vals)):
            if i & step == 0:
                a, b = vals[i], vals[i + step]
                vals[i], vals[i + step] = a + b, a - b
        step *= 2
    return vals


def split(v):
    hi = v.astype(BF16)
    return hi, (v - hi.astype(F32)).astype(BF16)


def wait_bytes(ref, sem):
    pltpu.make_async_copy(ref, ref, sem).wait()


def greet(z, x, y, core, barrier):
    for d in range(1, 8):
        tell(barrier, at((z + d) % 8, x, y, core))
    for d in range(1, 4):
        tell(barrier, at(z, (x + d) % 4, y, core))
        tell(barrier, at(z, x, (y + d) % 4, core))
    tell(barrier, at(z, x, y, 1 - core))


def tell(sem, where):
    pl.semaphore_signal(sem, inc=1, device_id=where, device_id_type=MESH)


def push(src, dst, send_sem, recv_sem, where):
    pltpu.make_async_remote_copy(
        src_ref=src, dst_ref=dst, send_sem=send_sem, recv_sem=recv_sem, device_id=where, device_id_type=MESH
    ).start()


def mix_kernel(
    panel_hbm, signs_hbm, offsets, owners, result, crowded, lists, kept_hbm,
    panel, signs, y_ref, r_ref, t_ref, mine, out, lanes, ids, ranks, picks, names, picked, full_here, full_there,
    g_ref, c_ref, ha, hb, a1, b1, sa, sb, a2, b2, sz, zr,
    load_sem, small_sem, send_sem, recv_sem, core_send, core_recv, list_send, list_recv, plane_sem, all_sem,
    keep_sem, full_send, full_recv, s0, r0, s1, r1a, r1b, s2, r2a, r2b, s3, r3,
):
    z, x, y, core = place()
    barrier = pltpu.get_barrier_semaphore()
    greet(z, x, y, core, barrier)

    def load(i):
        span = pl.ds(4096 * i, 4096)
        return pltpu.make_async_copy(panel_hbm.at[:, span], panel.at[:, span], load_sem.at[i])

    small = [
        pltpu.make_async_copy(signs_hbm, signs, small_sem.at[0]),
        pltpu.make_async_copy(offsets, mine.at[pl.ds(0, 8)], small_sem.at[1]),
        pltpu.make_async_copy(owners, mine.at[pl.ds(8, 8)], small_sem.at[2]),
    ]
    small[0].start()
    for i in range(4):
        load(i).start()
    small[1].start()
    small[2].start()
    table = sylvester(128).astype(BF16)
    table = jnp.concatenate([table, table], axis=0)

    small[0].wait()
    for part in range(4):
        load(part).wait()
        for i in range(2 * part, 2 * part + 2):
            sign = signs[16 * i : 16 * i + 16, :].astype(F32)
            rows = []
            for j in range(16):
                start = (i * 16 + j) * 128
                rows.append(panel[:, start : start + 128] * sign[j : j + 1, :])
            hi, lo = split(jnp.concatenate(rows, axis=0))
            pieces = jnp.concatenate([hi, lo], axis=1)
            done = jnp.dot(pieces, table, preferred_element_type=F32)
            y_ref[16 * i : 16 * i + 16] = done.reshape(16, 16, 128)

    pl.semaphore_wait(barrier, 14)
    for d in range(1, 4):
        tell(plane_sem, at(z, (x + d) % 4, y, core))

    def outer_high(g, carry):
        vals = butterfly([y_ref[g + 8 * j] for j in range(16)])
        for j in range(16):
            y_ref[g + 8 * j] = vals[j]
        return carry

    lax.fori_loop(0, 8, outer_high, 0)
    pl.semaphore_wait(plane_sem, 3)
    for d in range(1, 4):
        tell(all_sem, at(z, x, (y + d) % 4, core))
    pl.semaphore_wait(all_sem, 3)

    slot = y * 32 + z * 4 + x
    to_x = [(x + d) % 4 for d in range(4)]
    to_y = [(y + d) % 4 for d in range(4)]
    sends_list = z // 4 == core

    small[1].wait()
    small[2].wait()

    def send(tz, dx, dy):
        push(
            y_ref.at[tz * 16 + to_x[dx] * 4 + to_y[dy]], r_ref.at[slot],
            send_sem, recv_sem.at[dy], at(tz, to_x[dx], to_y[dy], core),
        )

    def send_list(tz, dx):
        push(mine, lists.at[z % 4 * 4 + x], list_send, list_recv, at(tz, to_x[dx], y, core))

    def first(i, carry):
        tz = (z + i * 3 + 4) % 8
        for g in range(2):
            vals = butterfly([y_ref[tz * 16 + g * 8 + j] for j in range(8)])
            for j in range(8):
                y_ref[tz * 16 + g * 8 + j] = vals[j]
        for dx in range(4):
            if dx:
                send(tz, dx, 0)
                pl.when(sends_list)(functools.partial(send_list, tz, dx))
            else:
                pl.when(tz != z)(functools.partial(send, tz, 0, 0))
                pl.when(sends_list & (tz != z))(functools.partial(send_list, tz, 0))
        return carry

    lax.fori_loop(0, 8, first, 0)

    for dy in range(1, 4):
        def later(i, carry):
            for dx in range(4):
                send((z + i * 3 + 4) % 8, dx, dy)
            return carry

        lax.fori_loop(0, 8, later, 0)

    r_ref[slot] = y_ref[z * 16 + x * 4 + y]

    @pl.when(sends_list)
    def _():
        lists[z % 4 * 4 + x] = mine[...]
        wait_bytes(lists.at[pl.ds(0, 15)], list_recv)

    @pl.when(jnp.logical_not(sends_list))
    def _():
        wait_bytes(lists, list_recv)

    turn = (1 - 2 * core).astype(F32)

    def across(dy, carry):
        v = (y + 4 - dy) % 4
        for h in range(2):
            rows = pl.ds(8 * h, 8)
            low = [r_ref[v * 32 + q, rows, :] for q in range(16)]
            high = [r_ref[v * 32 + 16 + q, rows, :] * turn for q in range(16)]
            given = butterfly([a - b for a, b in zip(low, high)])
            for p in range(16):
                t_ref[v, p, rows, :] = given[p]
            kept = butterfly([a + b for a, b in zip(low, high)])
            for p in range(16):
                out[p, v, core, rows, :] = kept[p]
        push(t_ref.at[v], out.at[:, v, core], core_send, core_recv, at(z, x, y, 1 - core))
        return carry

    rank, lane, name, seen = ranked(lists, z * 16 + x * 4 + y)
    lanes[...], ids[...] = lane, name
    ahead = jnp.zeros((1, 1), F32)
    for p in range(16):
        row = rank[p : p + 1, :]
        ranks[p : p + 1, :] = jnp.where(row >= 0.0, row + ahead, -1.0)
        ahead = ahead + seen[p : p + 1, :]

    def locate(p, carry):
        spot, its_name = carry
        one = pl.ds(p, 1)
        hot = (iota((TAKEN, 1024), 0).astype(F32) == ranks[one, :]).astype(F32).astype(BF16)
        facts = jnp.concatenate([lanes[one, :], ids[one, :], jnp.zeros((6, 1024), F32)], axis=0)
        found = lax.dot_general(facts.astype(BF16), hot, NT, preferred_element_type=F32)
        base = (p * 128).astype(F32)
        spot = jnp.where(found[1:2, :] > 0.5, found[0:1, :] + base, spot)
        return spot, its_name + found[1:2, :]

    nowhere = jnp.zeros((1, TAKEN), F32)
    spot, its_name = lax.fori_loop(0, 16, locate, (nowhere - 1.0, nowhere))
    names[0:1, :] = its_name

    def mark(k, carry):
        rows = iota((256, TAKEN), 0).astype(F32) + (k * 256).astype(F32)
        picks[k] = (rows == spot).astype(F32).astype(BF16)
        return carry

    lax.fori_loop(0, 8, mark, 0)

    def tally(p, count):
        slabs = lists[p, 0:8, :] // 128
        for b in range(8):
            count = count + (slabs[b : b + 1, :] == iota((128, 128), 0)).astype(F32)
        return count

    count = lax.fori_loop(0, 16, tally, jnp.zeros((128, 128), F32))
    most = jnp.max(jnp.sum(count, axis=1, keepdims=True), axis=0, keepdims=True)
    full_here[...] = jnp.broadcast_to(jnp.where(most > TAKEN, 1, 0), (8, 128))
    push(full_here, full_there, full_send, full_recv, at(z, x, y, 1 - core))

    wait_bytes(r_ref.at[pl.ds(0, 31)], recv_sem.at[0])
    across(0, 0)

    def across_next(dy, carry):
        wait_bytes(r_ref.at[pl.ds(0, 32)], recv_sem.at[dy])
        return across(dy, carry)

    lax.fori_loop(1, 4, across_next, 0)
    wait_bytes(t_ref, core_recv)
    keep = pltpu.make_async_copy(out, kept_hbm, keep_sem)
    keep.start()
    got = jnp.zeros((256, TAKEN), F32)
    for g in range(4):
        pick = picks[2 * g : 2 * g + 2].reshape(512, TAKEN)
        got = got + jnp.dot(stacked(out, g), pick, preferred_element_type=F32)
    picked[...] = got.astype(BF16)

    def make(i):
        whole = picked[...]
        members = []
        for tx in range(4):
            wanted = (i * 4 + tx + 1).astype(F32)
            members.append(whole * (names[0:1, :] == wanted).astype(F32).astype(BF16))
        members = jnp.concatenate(members, axis=0)
        both = lax.dot_general(members, whole, NT, preferred_element_type=F32)
        for tx in range(4):
            g_ref[i, tx] = folded(both[256 * tx : 256 * tx + 256]).reshape(4, 2, 16, 128)
        push(g_ref.at[i, :, :, 1 - core], c_ref.at[i], s0, r0.at[i], at(z, x, y, 1 - core))

    def forward(i):
        wait_bytes(c_ref.at[i], r0.at[i])
        for tx in range(4):
            for ty in range(4):
                ha[i, tx, ty] = g_ref[i, tx, ty, core, 0:8, :] + c_ref[i, tx, ty, 0:8, :]
                hb[i, ty, tx] = g_ref[i, tx, ty, core, 8:16, :] + c_ref[i, tx, ty, 8:16, :]
        for d in (2, 1, 3):
            push(ha.at[i, to_x[d]], a1.at[x, i], s1.at[0], r1a.at[i // 2], at(z, to_x[d], y, core))
            push(hb.at[i, to_y[d]], b1.at[y, i], s1.at[1], r1b.at[i // 2], at(z, x, to_y[d], core))
        a1[x, i] = ha[i, x]
        b1[y, i] = hb[i, y]

    def second(h):
        wait_bytes(a1.at[pl.ds(0, 3), pl.ds(0, 2)], r1a.at[h])
        wait_bytes(b1.at[pl.ds(0, 3), pl.ds(0, 2)], r1b.at[h])
        for i in range(2):
            for t in range(4):
                n = 2 * h + i
                sa[h, t, i] = (a1[0, n, t] + a1[1, n, t]) + (a1[2, n, t] + a1[3, n, t])
                sb[h, t, i] = (b1[0, n, t] + b1[1, n, t]) + (b1[2, n, t] + b1[3, n, t])
        for d in (2, 1, 3):
            push(sa.at[h, to_y[d]], a2.at[h, y], s2.at[0], r2a.at[h], at(z, x, to_y[d], core))
            push(sb.at[h, to_x[d]], b2.at[h, x], s2.at[1], r2b.at[h], at(z, to_x[d], y, core))
        a2[h, y] = sa[h, y]
        b2[h, x] = sb[h, x]

    def third(h):
        wait_bytes(a2.at[h, pl.ds(0, 3)], r2a.at[h])
        wait_bytes(b2.at[h, pl.ds(0, 3)], r2b.at[h])
        for i in range(2):
            n = 2 * h + i
            sz[n, 0:8, :] = (a2[h, 0, i] + a2[h, 1, i]) + (a2[h, 2, i] + a2[h, 3, i])
            sz[n, 8:16, :] = (b2[h, 0, i] + b2[h, 1, i]) + (b2[h, 2, i] + b2[h, 3, i])
            pl.when(z != n)(functools.partial(push, sz.at[n], zr.at[z], s3, r3, at(n, x, y, core)))

    def step(j, carry):
        pl.when(j < 4)(functools.partial(make, 2 * j))
        pl.when((j >= 1) & (j < 5))(functools.partial(forward, 2 * j - 2))
        pl.when(j < 4)(functools.partial(make, 2 * j + 1))
        pl.when((j >= 1) & (j < 5))(functools.partial(forward, 2 * j - 1))
        pl.when((j >= 2) & (j < 6))(functools.partial(second, j - 2))
        pl.when(j >= 3)(functools.partial(third, j - 3))
        return carry

    lax.fori_loop(0, 7, step, 0)
    zr[z] = sz[z]
    wait_bytes(zr.at[pl.ds(0, 7)], r3)
    v = [zr[i] for i in range(8)]
    total = ((v[0] + v[1]) + (v[2] + v[3])) + ((v[4] + v[5]) + (v[6] + v[7]))
    result[...] = total * GRAM_SCALE
    wait_bytes(full_there, full_recv)
    crowded[0, 0] = jnp.max(jnp.maximum(full_here[...], full_there[...]))

    wait_bytes(r_ref.at[pl.ds(0, 127)], send_sem)

    @pl.when(sends_list)
    def _():
        for n in range(31):
            wait_bytes(mine, list_send)

    keep.wait()
    wait_bytes(full_here, full_send)
    wait_bytes(t_ref, core_send)
    wait_bytes(c_ref, s0)
    wait_bytes(a1.at[pl.ds(0, 3)], s1.at[0])
    wait_bytes(b1.at[pl.ds(0, 3)], s1.at[1])
    wait_bytes(a2.at[:, pl.ds(0, 3)], s2.at[0])
    wait_bytes(b2.at[:, pl.ds(0, 3)], s2.at[1])
    wait_bytes(zr.at[pl.ds(0, 7)], s3)


def ranked(lists, slab):
    here = jnp.concatenate([lists[:, b, :] for b in range(8)], axis=1) - slab * 128
    owner = jnp.concatenate([lists[:, 8 + b, :] for b in range(8)], axis=1)
    inside = (here >= 0) & (here < 128)
    mask = jnp.where(inside, 1.0, 0.0).astype(F32)
    before = (iota((128, 128), 0) < iota((128, 128), 1)).astype(F32).astype(BF16)
    rank, seen = [], jnp.zeros((16, 1), F32)
    for b in range(8):
        piece = mask[:, 128 * b : 128 * b + 128]
        rank.append(jnp.dot(piece.astype(BF16), before, preferred_element_type=F32) + seen)
        seen = seen + jnp.sum(piece, axis=1, keepdims=True)
    rank = jnp.where(inside, jnp.concatenate(rank, axis=1), -1.0)
    lane = jnp.where(inside, here, 0).astype(F32)
    name = jnp.where(inside, owner + 1, 0).astype(F32)
    return rank, lane, name, seen


def chosen(rank, lane, name, g, first):
    wanted = iota((SLOTS, 1024), 0).astype(F32) + first
    hot = [rank[p : p + 1, :] == wanted for p in range(4 * g, 4 * g + 4)]
    hot = jnp.concatenate([h.astype(F32) for h in hot], axis=0).astype(BF16)
    facts = jnp.concatenate([lane[4 * g : 4 * g + 4], name[4 * g : 4 * g + 4]], axis=0)
    found = lax.dot_general(facts.astype(BF16), hot, NT, preferred_element_type=F32)
    which = iota((1, 128), 1) // SLOTS
    at_lane, its_name = jnp.zeros((1, 128), F32), jnp.zeros((1, 128), F32)
    for p in range(4):
        at_lane = jnp.where(which == p, found[p : p + 1, :] + 128.0 * p, at_lane)
        its_name = jnp.where(which == p, found[4 + p : 5 + p, :], its_name)
    spot = jnp.where(its_name > 0.5, at_lane, -1.0)
    pick = (iota((512, 128), 0).astype(F32) == spot).astype(F32).astype(BF16)
    return pick, its_name


def stacked(mixed, g):
    columns = []
    for p in range(4 * g, 4 * g + 4):
        hi, lo = split(mixed[p].reshape(128, 128))
        columns.append(jnp.concatenate([hi, lo], axis=0))
    return jnp.concatenate(columns, axis=1)


def folded(both):
    return (both[:128, :128] + both[128:, 128:]) + (both[:128, 128:] + both[128:, :128])


def owner_gram(picked, names, o):
    member = (names == o.astype(F32) + 1.0).astype(F32).astype(BF16)
    both = lax.dot_general(picked * member, picked, NT, preferred_element_type=F32)
    return folded(both)


def gram_kernel(mixed, lists, out, picked):
    z, x, y, core = place()
    rank, lane, name, seen = ranked(lists, z * 16 + x * 4 + y)
    rounds = (jnp.max(seen).astype(jnp.int32) + SLOTS - 1) // SLOTS
    out[...] = jnp.zeros_like(out)

    def one_round(r, carry):
        names = []
        for g in range(4):
            pick, its_name = chosen(rank, lane, name, g, (r * SLOTS).astype(F32))
            got = jnp.dot(stacked(mixed, g), pick, preferred_element_type=F32)
            picked[:, 128 * g : 128 * g + 128] = got.astype(BF16)
            names.append(its_name)
        names = jnp.concatenate(names, axis=1)

        def one_owner(o, carry):
            out[o] += owner_gram(picked[...], names, o) * GRAM_SCALE
            return carry

        lax.fori_loop(0, 32, one_owner, 0)
        return carry

    lax.fori_loop(0, rounds, one_round, 0)


def sum_kernel(gram, out, c_ref, ha, hb, a1, b1, sa, sb, a2, b2, sz, zr, s0, r0, s1, r1, s2, r2, s3, r3):
    z, x, y, core = place()

    barrier = pltpu.get_barrier_semaphore()
    greet(z, x, y, core, barrier)
    pl.semaphore_wait(barrier, 14)
    push(gram.at[:, :, :, 1 - core], c_ref, s0, r0, at(z, x, y, 1 - core))
    wait_bytes(c_ref, r0)

    def add_core(i, carry):
        for tx in range(4):
            for ty in range(4):
                ha[tx, i, ty] = gram[i, tx, ty, core, 0:8, :] + c_ref[i, tx, ty, 0:8, :]
                hb[ty, i, tx] = gram[i, tx, ty, core, 8:16, :] + c_ref[i, tx, ty, 8:16, :]
        return carry

    lax.fori_loop(0, 8, add_core, 0)
    for d in (2, 1, 3):
        tx, ty = (x + d) % 4, (y + d) % 4
        push(ha.at[tx], a1.at[x], s1.at[0], r1.at[0], at(z, tx, y, core))
        push(hb.at[ty], b1.at[y], s1.at[1], r1.at[1], at(z, x, ty, core))
    a1[x] = ha[x]
    b1[y] = hb[y]
    wait_bytes(a1.at[pl.ds(0, 3)], r1.at[0])
    wait_bytes(b1.at[pl.ds(0, 3)], r1.at[1])

    def add_first(i, carry):
        for t in range(4):
            sa[t, i] = (a1[0, i, t] + a1[1, i, t]) + (a1[2, i, t] + a1[3, i, t])
            sb[t, i] = (b1[0, i, t] + b1[1, i, t]) + (b1[2, i, t] + b1[3, i, t])
        return carry

    lax.fori_loop(0, 8, add_first, 0)
    for d in (2, 1, 3):
        tx, ty = (x + d) % 4, (y + d) % 4
        push(sa.at[ty], a2.at[y], s2.at[0], r2.at[0], at(z, x, ty, core))
        push(sb.at[tx], b2.at[x], s2.at[1], r2.at[1], at(z, tx, y, core))
    a2[y] = sa[y]
    b2[x] = sb[x]
    wait_bytes(a2.at[pl.ds(0, 3)], r2.at[0])
    wait_bytes(b2.at[pl.ds(0, 3)], r2.at[1])
    for i in range(8):
        sz[i, 0:8, :] = (a2[0, i] + a2[1, i]) + (a2[2, i] + a2[3, i])
        sz[i, 8:16, :] = (b2[0, i] + b2[1, i]) + (b2[2, i] + b2[3, i])
    for d in (4, 3, 5, 2, 6, 1, 7):
        tz = (z + d) % 8
        push(sz.at[tz], zr.at[z], s3, r3, at(tz, x, y, core))
    zr[z] = sz[z]
    wait_bytes(zr.at[pl.ds(0, 7)], r3)
    v = [zr[i] for i in range(8)]
    out[...] = ((v[0] + v[1]) + (v[2] + v[3])) + ((v[4] + v[5]) + (v[6] + v[7]))
    wait_bytes(c_ref, s0)
    for n in range(2):
        wait_bytes(a1.at[pl.ds(0, 3)], s1.at[n])
        wait_bytes(a2.at[pl.ds(0, 3)], s2.at[n])
    wait_bytes(zr.at[pl.ds(0, 7)], s3)


def body(panel, signs, offsets, owners):
    params = functools.partial(pltpu.CompilerParams, has_side_effects=True)
    dma, vmem = pltpu.SemaphoreType.DMA, pltpu.VMEM
    result, crowded, lists, mixed = pl.pallas_call(
        mix_kernel,
        out_shape=[
            jax.ShapeDtypeStruct((16, 128), F32),
            jax.ShapeDtypeStruct((1, 1), jnp.int32),
            jax.ShapeDtypeStruct((16, 16, 128), jnp.int32),
            jax.ShapeDtypeStruct((16, 4, 2, 16, 128), F32),
        ],
        in_specs=[HBM] * 4,
        out_specs=[VMEM, SMEM, VMEM, HBM],
        scratch_shapes=[
            vmem((16, 16384), F32),
            vmem((128, 128), jnp.int32),
            vmem((128, 16, 128), F32),
            vmem((128, 16, 128), F32),
            vmem((4, 16, 16, 128), F32),
            vmem((16, 128), jnp.int32),
            vmem((16, 4, 2, 16, 128), F32),
            vmem((16, 1024), F32),
            vmem((16, 1024), F32),
            vmem((16, 1024), F32),
            vmem((8, 256, TAKEN), BF16),
            vmem((8, TAKEN), F32),
            vmem((256, TAKEN), BF16),
            vmem((8, 128), jnp.int32),
            vmem((8, 128), jnp.int32),
            vmem((8, 4, 4, 2, 16, 128), F32),
            vmem((8, 4, 4, 16, 128), F32),
            vmem((8, 4, 4, 8, 128), F32),
            vmem((8, 4, 4, 8, 128), F32),
            vmem((4, 8, 4, 8, 128), F32),
            vmem((4, 8, 4, 8, 128), F32),
            vmem((4, 4, 2, 8, 128), F32),
            vmem((4, 4, 2, 8, 128), F32),
            vmem((4, 4, 2, 8, 128), F32),
            vmem((4, 4, 2, 8, 128), F32),
            vmem((8, 16, 128), F32),
            vmem((8, 16, 128), F32),
            dma((4,)), dma((3,)), dma, dma((4,)), dma, dma, dma, dma,
            pltpu.SemaphoreType.REGULAR, pltpu.SemaphoreType.REGULAR,
            dma, dma, dma, dma, dma((8,)), dma((2,)), dma((4,)), dma((4,)),
            dma((2,)), dma((4,)), dma((4,)), dma, dma,
        ],
        compiler_params=params(collective_id=1, vmem_limit_bytes=MIX_VMEM),
        name="mix",
    )(panel, signs.reshape(128, 128), offsets.reshape(8, 128), owners.reshape(8, 128))

    def in_rounds():
        gram = pl.pallas_call(
            gram_kernel,
            out_shape=jax.ShapeDtypeStruct((32, 128, 128), F32),
            in_specs=[VMEM] * 2,
            out_specs=VMEM,
            scratch_shapes=[vmem((256, 512), BF16)],
            compiler_params=pltpu.CompilerParams(vmem_limit_bytes=48 << 20),
            name="gram_rounds",
        )(mixed.reshape(16, 128, 128), lists)
        return pl.pallas_call(
            sum_kernel,
            out_shape=jax.ShapeDtypeStruct((16, 128), F32),
            in_specs=[VMEM],
            out_specs=VMEM,
            scratch_shapes=[
                vmem((8, 4, 4, 16, 128), F32),
                vmem((4, 8, 4, 8, 128), F32),
                vmem((4, 8, 4, 8, 128), F32),
                vmem((4, 8, 4, 8, 128), F32),
                vmem((4, 8, 4, 8, 128), F32),
                vmem((4, 8, 8, 128), F32),
                vmem((4, 8, 8, 128), F32),
                vmem((4, 8, 8, 128), F32),
                vmem((4, 8, 8, 128), F32),
                vmem((8, 16, 128), F32),
                vmem((8, 16, 128), F32),
            ] + [dma] * 2 + [dma((2,))] * 4 + [dma] * 2,
            compiler_params=params(collective_id=2, vmem_limit_bytes=48 << 20),
            name="sum_rounds",
        )(gram.reshape(8, 4, 4, 2, 16, 128))

    return lax.cond(crowded[0, 0] > 0, in_rounds, lambda: result)[None]


def solution(mesh):
    placed = (P("col", "row"), P("row"), P("row"), P("row", None))
    return jax.shard_map(
        body, mesh=mesh, in_specs=placed, out_specs=P("row", "col", None), check_vma=False
    )
```

```python
import functools

import jax
import jax.numpy as jnp
from jax import lax
from jax.experimental import pallas as pl
from jax.experimental.pallas import tpu as pltpu
from jax.sharding import PartitionSpec as P

MESH = pl.DeviceIdType.MESH
F32 = jnp.float32
BF16 = jnp.bfloat16
NT = (((1,), (1,)), ((), ()))
VMEM = pl.BlockSpec(memory_space=pltpu.VMEM)
SMEM = pl.BlockSpec(memory_space=pltpu.SMEM)
HBM = pl.BlockSpec(memory_space=pltpu.HBM)
SLOTS = 32
TAKEN = 256
MIX_VMEM = 60 << 20
GRAM_SCALE = 2.0 ** -29


def place():
    row, col = lax.axis_index("row"), lax.axis_index("col")
    return row // 4, row % 4, col // 2, col % 2


def at(z, x, y, core):
    return {"row": z * 4 + x, "col": y * 2 + core}


def iota(shape, dim):
    return lax.broadcasted_iota(jnp.int32, shape, dim)


def sylvester(order):
    v = iota((order, order), 0) & iota((order, order), 1)
    for shift in (4, 2, 1):
        v = v ^ (v >> shift)
    return (1 - 2 * (v & 1)).astype(F32)


def butterfly(vals):
    vals, step = list(vals), 1
    while step < len(vals):
        for i in range(len(vals)):
            if i & step == 0:
                a, b = vals[i], vals[i + step]
                vals[i], vals[i + step] = a + b, a - b
        step *= 2
    return vals


def split(v):
    hi = v.astype(BF16)
    return hi, (v - hi.astype(F32)).astype(BF16)


def wait_bytes(ref, sem):
    pltpu.make_async_copy(ref, ref, sem).wait()


def greet(z, x, y, core, barrier):
    for d in range(1, 8):
        tell(barrier, at((z + d) % 8, x, y, core))
    for d in range(1, 4):
        tell(barrier, at(z, (x + d) % 4, y, core))
        tell(barrier, at(z, x, (y + d) % 4, core))
    tell(barrier, at(z, x, y, 1 - core))


def tell(sem, where):
    pl.semaphore_signal(sem, inc=1, device_id=where, device_id_type=MESH)


def push(src, dst, send_sem, recv_sem, where):
    pltpu.make_async_remote_copy(
        src_ref=src, dst_ref=dst, send_sem=send_sem, recv_sem=recv_sem, device_id=where, device_id_type=MESH
    ).start()


def mix_kernel(
    panel_hbm, signs_hbm, offsets, owners, result, crowded, lists, kept_hbm,
    panel, signs, y_ref, r_ref, t_ref, mine, out, lanes, ids, ranks, picks, names, picked, full_here, full_there,
    g_ref, c_ref, ha, hb, a1, b1, sa, sb, a2, b2, sz, zr,
    load_sem, small_sem, send_sem, recv_sem, core_send, core_recv, list_send, list_recv, plane_sem, all_sem,
    keep_sem, full_send, full_recv, s0, r0, s1, r1a, r1b, s2, r2a, r2b, s3, r3,
):
    z, x, y, core = place()
    barrier = pltpu.get_barrier_semaphore()
    greet(z, x, y, core, barrier)

    def load(i):
        span = pl.ds(4096 * i, 4096)
        return pltpu.make_async_copy(panel_hbm.at[:, span], panel.at[:, span], load_sem.at[i])

    small = [
        pltpu.make_async_copy(signs_hbm, signs, small_sem.at[0]),
        pltpu.make_async_copy(offsets, mine.at[pl.ds(0, 8)], small_sem.at[1]),
        pltpu.make_async_copy(owners, mine.at[pl.ds(8, 8)], small_sem.at[2]),
    ]
    small[0].start()
    for i in range(4):
        load(i).start()
    small[1].start()
    small[2].start()
    table = sylvester(128).astype(BF16)
    table = jnp.concatenate([table, table], axis=0)

    small[0].wait()
    for part in range(4):
        load(part).wait()
        for i in range(2 * part, 2 * part + 2):
            sign = signs[16 * i : 16 * i + 16, :].astype(F32)
            rows = []
            for j in range(16):
                start = (i * 16 + j) * 128
                rows.append(panel[:, start : start + 128] * sign[j : j + 1, :])
            hi, lo = split(jnp.concatenate(rows, axis=0))
            pieces = jnp.concatenate([hi, lo], axis=1)
            done = jnp.dot(pieces, table, preferred_element_type=F32)
            y_ref[16 * i : 16 * i + 16] = done.reshape(16, 16, 128)

    pl.semaphore_wait(barrier, 14)
    for d in range(1, 4):
        tell(plane_sem, at(z, (x + d) % 4, y, core))

    def outer_high(g, carry):
        vals = butterfly([y_ref[g + 8 * j] for j in range(16)])
        for j in range(16):
            y_ref[g + 8 * j] = vals[j]
        return carry

    lax.fori_loop(0, 8, outer_high, 0)

    def outer_low(g, carry):
        vals = butterfly([y_ref[g * 8 + j] for j in range(8)])
        for j in range(8):
            y_ref[g * 8 + j] = vals[j]
        return carry

    lax.fori_loop(0, 16, outer_low, 0)

    slot = y * 32 + z * 4 + x
    to_x = [(x + d) % 4 for d in range(4)]
    to_y = [(y + d) % 4 for d in range(4)]
    sends_list = z // 4 == core

    small[1].wait()
    small[2].wait()

    def send(tz, dx, dy):
        push(
            y_ref.at[tz * 16 + to_x[dx] * 4 + to_y[dy]], r_ref.at[slot],
            send_sem, recv_sem.at[dy], at(tz, to_x[dx], to_y[dy], core),
        )

    def send_list(tz, dx):
        push(mine, lists.at[z % 4 * 4 + x], list_send, list_recv, at(tz, to_x[dx], y, core))

    for d in (4, 7, 2, 5, 3, 6, 1):
        tz = (z + d) % 8
        send(tz, 0, 0)
        pl.when(sends_list)(functools.partial(send_list, tz, 0))
    pl.semaphore_wait(plane_sem, 3)
    for d in range(1, 4):
        tell(all_sem, at(z, x, (y + d) % 4, core))

    def sweep(dy, carry_list):
        def some(i, carry):
            tz = (z + i * 3 + 4) % 8
            for dx in range(1 if carry_list else 0, 4):
                send(tz, dx, dy)
                if carry_list:
                    pl.when(sends_list)(functools.partial(send_list, tz, dx))
            return carry

        lax.fori_loop(0, 8, some, 0)

    sweep(0, True)
    pl.semaphore_wait(all_sem, 3)
    for dy in range(1, 4):
        sweep(dy, False)

    r_ref[slot] = y_ref[z * 16 + x * 4 + y]

    @pl.when(sends_list)
    def _():
        lists[z % 4 * 4 + x] = mine[...]
        wait_bytes(lists.at[pl.ds(0, 15)], list_recv)

    @pl.when(jnp.logical_not(sends_list))
    def _():
        wait_bytes(lists, list_recv)

    turn = (1 - 2 * core).astype(F32)

    def across(dy, carry):
        v = (y + 4 - dy) % 4
        for h in range(2):
            rows = pl.ds(8 * h, 8)
            low = [r_ref[v * 32 + q, rows, :] for q in range(16)]
            high = [r_ref[v * 32 + 16 + q, rows, :] * turn for q in range(16)]
            given = butterfly([a - b for a, b in zip(low, high)])
            for p in range(16):
                t_ref[v, p, rows, :] = given[p]
            kept = butterfly([a + b for a, b in zip(low, high)])
            for p in range(16):
                out[p, v, core, rows, :] = kept[p]
        push(t_ref.at[v], out.at[:, v, core], core_send, core_recv, at(z, x, y, 1 - core))
        return carry

    rank, lane, name, seen = ranked(lists, z * 16 + x * 4 + y)
    lanes[...], ids[...] = lane, name
    ahead = jnp.zeros((1, 1), F32)
    for p in range(16):
        row = rank[p : p + 1, :]
        ranks[p : p + 1, :] = jnp.where(row >= 0.0, row + ahead, -1.0)
        ahead = ahead + seen[p : p + 1, :]

    def locate(p, carry):
        spot, its_name = carry
        one = pl.ds(p, 1)
        hot = (iota((TAKEN, 1024), 0).astype(F32) == ranks[one, :]).astype(F32).astype(BF16)
        facts = jnp.concatenate([lanes[one, :], ids[one, :], jnp.zeros((6, 1024), F32)], axis=0)
        found = lax.dot_general(facts.astype(BF16), hot, NT, preferred_element_type=F32)
        base = (p * 128).astype(F32)
        spot = jnp.where(found[1:2, :] > 0.5, found[0:1, :] + base, spot)
        return spot, its_name + found[1:2, :]

    nowhere = jnp.zeros((1, TAKEN), F32)
    spot, its_name = lax.fori_loop(0, 16, locate, (nowhere - 1.0, nowhere))
    names[0:1, :] = its_name

    def mark(k, carry):
        rows = iota((256, TAKEN), 0).astype(F32) + (k * 256).astype(F32)
        picks[k] = (rows == spot).astype(F32).astype(BF16)
        return carry

    lax.fori_loop(0, 8, mark, 0)

    def tally(p, count):
        slabs = lists[p, 0:8, :] // 128
        for b in range(8):
            count = count + (slabs[b : b + 1, :] == iota((128, 128), 0)).astype(F32)
        return count

    count = lax.fori_loop(0, 16, tally, jnp.zeros((128, 128), F32))
    most = jnp.max(jnp.sum(count, axis=1, keepdims=True), axis=0, keepdims=True)
    full_here[...] = jnp.broadcast_to(jnp.where(most > TAKEN, 1, 0), (8, 128))
    push(full_here, full_there, full_send, full_recv, at(z, x, y, 1 - core))

    wait_bytes(r_ref.at[pl.ds(0, 31)], recv_sem.at[0])
    across(0, 0)

    def across_next(dy, carry):
        wait_bytes(r_ref.at[pl.ds(0, 32)], recv_sem.at[dy])
        return across(dy, carry)

    lax.fori_loop(1, 4, across_next, 0)
    wait_bytes(t_ref, core_recv)
    keep = pltpu.make_async_copy(out, kept_hbm, keep_sem)
    keep.start()
    got = jnp.zeros((256, TAKEN), F32)
    for g in range(4):
        pick = picks[2 * g : 2 * g + 2].reshape(512, TAKEN)
        got = got + jnp.dot(stacked(out, g), pick, preferred_element_type=F32)
    picked[...] = got.astype(BF16)

    def make(i):
        whole = picked[...]
        members = []
        for tx in range(4):
            wanted = (i * 4 + tx + 1).astype(F32)
            members.append(whole * (names[0:1, :] == wanted).astype(F32).astype(BF16))
        members = jnp.concatenate(members, axis=0)
        both = lax.dot_general(members, whole, NT, preferred_element_type=F32)
        for tx in range(4):
            g_ref[i, tx] = folded(both[256 * tx : 256 * tx + 256]).reshape(4, 2, 16, 128)
        push(g_ref.at[i, :, :, 1 - core], c_ref.at[i], s0, r0.at[i], at(z, x, y, 1 - core))

    def forward(i):
        wait_bytes(c_ref.at[i], r0.at[i])
        for tx in range(4):
            for ty in range(4):
                ha[i, tx, ty] = g_ref[i, tx, ty, core, 0:8, :] + c_ref[i, tx, ty, 0:8, :]
                hb[i, ty, tx] = g_ref[i, tx, ty, core, 8:16, :] + c_ref[i, tx, ty, 8:16, :]
        for d in (2, 1, 3):
            push(ha.at[i, to_x[d]], a1.at[x, i], s1.at[0], r1a.at[i // 2], at(z, to_x[d], y, core))
            push(hb.at[i, to_y[d]], b1.at[y, i], s1.at[1], r1b.at[i // 2], at(z, x, to_y[d], core))
        a1[x, i] = ha[i, x]
        b1[y, i] = hb[i, y]

    def second(h):
        wait_bytes(a1.at[pl.ds(0, 3), pl.ds(0, 2)], r1a.at[h])
        wait_bytes(b1.at[pl.ds(0, 3), pl.ds(0, 2)], r1b.at[h])
        for i in range(2):
            for t in range(4):
                n = 2 * h + i
                sa[h, t, i] = (a1[0, n, t] + a1[1, n, t]) + (a1[2, n, t] + a1[3, n, t])
                sb[h, t, i] = (b1[0, n, t] + b1[1, n, t]) + (b1[2, n, t] + b1[3, n, t])
        for d in (2, 1, 3):
            push(sa.at[h, to_y[d]], a2.at[h, y], s2.at[0], r2a.at[h], at(z, x, to_y[d], core))
            push(sb.at[h, to_x[d]], b2.at[h, x], s2.at[1], r2b.at[h], at(z, to_x[d], y, core))
        a2[h, y] = sa[h, y]
        b2[h, x] = sb[h, x]

    def third(h):
        wait_bytes(a2.at[h, pl.ds(0, 3)], r2a.at[h])
        wait_bytes(b2.at[h, pl.ds(0, 3)], r2b.at[h])
        for i in range(2):
            n = 2 * h + i
            sz[n, 0:8, :] = (a2[h, 0, i] + a2[h, 1, i]) + (a2[h, 2, i] + a2[h, 3, i])
            sz[n, 8:16, :] = (b2[h, 0, i] + b2[h, 1, i]) + (b2[h, 2, i] + b2[h, 3, i])
            pl.when(z != n)(functools.partial(push, sz.at[n], zr.at[z], s3, r3, at(n, x, y, core)))

    def step(i, carry):
        make(i)
        forward(i - 1)
        return carry

    make(jnp.int32(0))
    lax.fori_loop(1, 8, step, 0)
    forward(jnp.int32(7))
    for stage, h in ((second, 0), (second, 1), (third, 0), (second, 2), (third, 1), (second, 3), (third, 2), (third, 3)):
        stage(h)
    zr[z] = sz[z]
    wait_bytes(zr.at[pl.ds(0, 7)], r3)
    v = [zr[i] for i in range(8)]
    total = ((v[0] + v[1]) + (v[2] + v[3])) + ((v[4] + v[5]) + (v[6] + v[7]))
    result[...] = total * GRAM_SCALE
    wait_bytes(full_there, full_recv)
    crowded[0, 0] = jnp.max(jnp.maximum(full_here[...], full_there[...]))

    wait_bytes(r_ref.at[pl.ds(0, 127)], send_sem)

    @pl.when(sends_list)
    def _():
        for n in range(31):
            wait_bytes(mine, list_send)

    keep.wait()
    wait_bytes(full_here, full_send)
    wait_bytes(t_ref, core_send)
    wait_bytes(c_ref, s0)
    wait_bytes(a1.at[pl.ds(0, 3)], s1.at[0])
    wait_bytes(b1.at[pl.ds(0, 3)], s1.at[1])
    wait_bytes(a2.at[:, pl.ds(0, 3)], s2.at[0])
    wait_bytes(b2.at[:, pl.ds(0, 3)], s2.at[1])
    wait_bytes(zr.at[pl.ds(0, 7)], s3)


def ranked(lists, slab):
    here = jnp.concatenate([lists[:, b, :] for b in range(8)], axis=1) - slab * 128
    owner = jnp.concatenate([lists[:, 8 + b, :] for b in range(8)], axis=1)
    inside = (here >= 0) & (here < 128)
    mask = jnp.where(inside, 1.0, 0.0).astype(F32)
    before = (iota((128, 128), 0) < iota((128, 128), 1)).astype(F32).astype(BF16)
    rank, seen = [], jnp.zeros((16, 1), F32)
    for b in range(8):
        piece = mask[:, 128 * b : 128 * b + 128]
        rank.append(jnp.dot(piece.astype(BF16), before, preferred_element_type=F32) + seen)
        seen = seen + jnp.sum(piece, axis=1, keepdims=True)
    rank = jnp.where(inside, jnp.concatenate(rank, axis=1), -1.0)
    lane = jnp.where(inside, here, 0).astype(F32)
    name = jnp.where(inside, owner + 1, 0).astype(F32)
    return rank, lane, name, seen


def chosen(rank, lane, name, g, first):
    wanted = iota((SLOTS, 1024), 0).astype(F32) + first
    hot = [rank[p : p + 1, :] == wanted for p in range(4 * g, 4 * g + 4)]
    hot = jnp.concatenate([h.astype(F32) for h in hot], axis=0).astype(BF16)
    facts = jnp.concatenate([lane[4 * g : 4 * g + 4], name[4 * g : 4 * g + 4]], axis=0)
    found = lax.dot_general(facts.astype(BF16), hot, NT, preferred_element_type=F32)
    which = iota((1, 128), 1) // SLOTS
    at_lane, its_name = jnp.zeros((1, 128), F32), jnp.zeros((1, 128), F32)
    for p in range(4):
        at_lane = jnp.where(which == p, found[p : p + 1, :] + 128.0 * p, at_lane)
        its_name = jnp.where(which == p, found[4 + p : 5 + p, :], its_name)
    spot = jnp.where(its_name > 0.5, at_lane, -1.0)
    pick = (iota((512, 128), 0).astype(F32) == spot).astype(F32).astype(BF16)
    return pick, its_name


def stacked(mixed, g):
    columns = []
    for p in range(4 * g, 4 * g + 4):
        hi, lo = split(mixed[p].reshape(128, 128))
        columns.append(jnp.concatenate([hi, lo], axis=0))
    return jnp.concatenate(columns, axis=1)


def folded(both):
    return (both[:128, :128] + both[128:, 128:]) + (both[:128, 128:] + both[128:, :128])


def owner_gram(picked, names, o):
    member = (names == o.astype(F32) + 1.0).astype(F32).astype(BF16)
    both = lax.dot_general(picked * member, picked, NT, preferred_element_type=F32)
    return folded(both)


def gram_kernel(mixed, lists, out, picked):
    z, x, y, core = place()
    rank, lane, name, seen = ranked(lists, z * 16 + x * 4 + y)
    rounds = (jnp.max(seen).astype(jnp.int32) + SLOTS - 1) // SLOTS
    out[...] = jnp.zeros_like(out)

    def one_round(r, carry):
        names = []
        for g in range(4):
            pick, its_name = chosen(rank, lane, name, g, (r * SLOTS).astype(F32))
            got = jnp.dot(stacked(mixed, g), pick, preferred_element_type=F32)
            picked[:, 128 * g : 128 * g + 128] = got.astype(BF16)
            names.append(its_name)
        names = jnp.concatenate(names, axis=1)

        def one_owner(o, carry):
            out[o] += owner_gram(picked[...], names, o) * GRAM_SCALE
            return carry

        lax.fori_loop(0, 32, one_owner, 0)
        return carry

    lax.fori_loop(0, rounds, one_round, 0)


def sum_kernel(gram, out, c_ref, ha, hb, a1, b1, sa, sb, a2, b2, sz, zr, s0, r0, s1, r1, s2, r2, s3, r3):
    z, x, y, core = place()

    barrier = pltpu.get_barrier_semaphore()
    greet(z, x, y, core, barrier)
    pl.semaphore_wait(barrier, 14)
    push(gram.at[:, :, :, 1 - core], c_ref, s0, r0, at(z, x, y, 1 - core))
    wait_bytes(c_ref, r0)

    def add_core(i, carry):
        for tx in range(4):
            for ty in range(4):
                ha[tx, i, ty] = gram[i, tx, ty, core, 0:8, :] + c_ref[i, tx, ty, 0:8, :]
                hb[ty, i, tx] = gram[i, tx, ty, core, 8:16, :] + c_ref[i, tx, ty, 8:16, :]
        return carry

    lax.fori_loop(0, 8, add_core, 0)
    for d in (2, 1, 3):
        tx, ty = (x + d) % 4, (y + d) % 4
        push(ha.at[tx], a1.at[x], s1.at[0], r1.at[0], at(z, tx, y, core))
        push(hb.at[ty], b1.at[y], s1.at[1], r1.at[1], at(z, x, ty, core))
    a1[x] = ha[x]
    b1[y] = hb[y]
    wait_bytes(a1.at[pl.ds(0, 3)], r1.at[0])
    wait_bytes(b1.at[pl.ds(0, 3)], r1.at[1])

    def add_first(i, carry):
        for t in range(4):
            sa[t, i] = (a1[0, i, t] + a1[1, i, t]) + (a1[2, i, t] + a1[3, i, t])
            sb[t, i] = (b1[0, i, t] + b1[1, i, t]) + (b1[2, i, t] + b1[3, i, t])
        return carry

    lax.fori_loop(0, 8, add_first, 0)
    for d in (2, 1, 3):
        tx, ty = (x + d) % 4, (y + d) % 4
        push(sa.at[ty], a2.at[y], s2.at[0], r2.at[0], at(z, x, ty, core))
        push(sb.at[tx], b2.at[x], s2.at[1], r2.at[1], at(z, tx, y, core))
    a2[y] = sa[y]
    b2[x] = sb[x]
    wait_bytes(a2.at[pl.ds(0, 3)], r2.at[0])
    wait_bytes(b2.at[pl.ds(0, 3)], r2.at[1])
    for i in range(8):
        sz[i, 0:8, :] = (a2[0, i] + a2[1, i]) + (a2[2, i] + a2[3, i])
        sz[i, 8:16, :] = (b2[0, i] + b2[1, i]) + (b2[2, i] + b2[3, i])
    for d in (4, 3, 5, 2, 6, 1, 7):
        tz = (z + d) % 8
        push(sz.at[tz], zr.at[z], s3, r3, at(tz, x, y, core))
    zr[z] = sz[z]
    wait_bytes(zr.at[pl.ds(0, 7)], r3)
    v = [zr[i] for i in range(8)]
    out[...] = ((v[0] + v[1]) + (v[2] + v[3])) + ((v[4] + v[5]) + (v[6] + v[7]))
    wait_bytes(c_ref, s0)
    for n in range(2):
        wait_bytes(a1.at[pl.ds(0, 3)], s1.at[n])
        wait_bytes(a2.at[pl.ds(0, 3)], s2.at[n])
    wait_bytes(zr.at[pl.ds(0, 7)], s3)


def body(panel, signs, offsets, owners):
    params = functools.partial(pltpu.CompilerParams, has_side_effects=True)
    dma, vmem = pltpu.SemaphoreType.DMA, pltpu.VMEM
    result, crowded, lists, mixed = pl.pallas_call(
        mix_kernel,
        out_shape=[
            jax.ShapeDtypeStruct((16, 128), F32),
            jax.ShapeDtypeStruct((1, 1), jnp.int32),
            jax.ShapeDtypeStruct((16, 16, 128), jnp.int32),
            jax.ShapeDtypeStruct((16, 4, 2, 16, 128), F32),
        ],
        in_specs=[HBM] * 4,
        out_specs=[VMEM, SMEM, VMEM, HBM],
        scratch_shapes=[
            vmem((16, 16384), F32),
            vmem((128, 128), jnp.int32),
            vmem((128, 16, 128), F32),
            vmem((128, 16, 128), F32),
            vmem((4, 16, 16, 128), F32),
            vmem((16, 128), jnp.int32),
            vmem((16, 4, 2, 16, 128), F32),
            vmem((16, 1024), F32),
            vmem((16, 1024), F32),
            vmem((16, 1024), F32),
            vmem((8, 256, TAKEN), BF16),
            vmem((8, TAKEN), F32),
            vmem((256, TAKEN), BF16),
            vmem((8, 128), jnp.int32),
            vmem((8, 128), jnp.int32),
            vmem((8, 4, 4, 2, 16, 128), F32),
            vmem((8, 4, 4, 16, 128), F32),
            vmem((8, 4, 4, 8, 128), F32),
            vmem((8, 4, 4, 8, 128), F32),
            vmem((4, 8, 4, 8, 128), F32),
            vmem((4, 8, 4, 8, 128), F32),
            vmem((4, 4, 2, 8, 128), F32),
            vmem((4, 4, 2, 8, 128), F32),
            vmem((4, 4, 2, 8, 128), F32),
            vmem((4, 4, 2, 8, 128), F32),
            vmem((8, 16, 128), F32),
            vmem((8, 16, 128), F32),
            dma((4,)), dma((3,)), dma, dma((4,)), dma, dma, dma, dma,
            pltpu.SemaphoreType.REGULAR, pltpu.SemaphoreType.REGULAR,
            dma, dma, dma, dma, dma((8,)), dma((2,)), dma((4,)), dma((4,)),
            dma((2,)), dma((4,)), dma((4,)), dma, dma,
        ],
        compiler_params=params(collective_id=1, vmem_limit_bytes=MIX_VMEM),
        name="mix",
    )(panel, signs.reshape(128, 128), offsets.reshape(8, 128), owners.reshape(8, 128))

    def in_rounds():
        gram = pl.pallas_call(
            gram_kernel,
            out_shape=jax.ShapeDtypeStruct((32, 128, 128), F32),
            in_specs=[VMEM] * 2,
            out_specs=VMEM,
            scratch_shapes=[vmem((256, 512), BF16)],
            compiler_params=pltpu.CompilerParams(vmem_limit_bytes=48 << 20),
            name="gram_rounds",
        )(mixed.reshape(16, 128, 128), lists)
        return pl.pallas_call(
            sum_kernel,
            out_shape=jax.ShapeDtypeStruct((16, 128), F32),
            in_specs=[VMEM],
            out_specs=VMEM,
            scratch_shapes=[
                vmem((8, 4, 4, 16, 128), F32),
                vmem((4, 8, 4, 8, 128), F32),
                vmem((4, 8, 4, 8, 128), F32),
                vmem((4, 8, 4, 8, 128), F32),
                vmem((4, 8, 4, 8, 128), F32),
                vmem((4, 8, 8, 128), F32),
                vmem((4, 8, 8, 128), F32),
                vmem((4, 8, 8, 128), F32),
                vmem((4, 8, 8, 128), F32),
                vmem((8, 16, 128), F32),
                vmem((8, 16, 128), F32),
            ] + [dma] * 2 + [dma((2,))] * 4 + [dma] * 2,
            compiler_params=params(collective_id=2, vmem_limit_bytes=48 << 20),
            name="sum_rounds",
        )(gram.reshape(8, 4, 4, 2, 16, 128))

    return lax.cond(crowded[0, 0] > 0, in_rounds, lambda: result)[None]


def solution(mesh):
    placed = (P("col", "row"), P("row"), P("row"), P("row", None))
    return jax.shard_map(
        body, mesh=mesh, in_specs=placed, out_specs=P("row", "col", None), check_vma=False
    )
```

```python
import functools

import jax
import jax.numpy as jnp
from jax import lax
from jax.experimental import pallas as pl
from jax.experimental.pallas import tpu as pltpu
from jax.sharding import PartitionSpec as P

MESH = pl.DeviceIdType.MESH
F32 = jnp.float32
BF16 = jnp.bfloat16
NT = (((1,), (1,)), ((), ()))
VMEM = pl.BlockSpec(memory_space=pltpu.VMEM)
SMEM = pl.BlockSpec(memory_space=pltpu.SMEM)
HBM = pl.BlockSpec(memory_space=pltpu.HBM)
SLOTS = 32
TAKEN = 256
MIX_VMEM = 60 << 20
GRAM_SCALE = 2.0 ** -29


def place():
    row, col = lax.axis_index("row"), lax.axis_index("col")
    return row // 4, row % 4, col // 2, col % 2


def at(z, x, y, core):
    return {"row": z * 4 + x, "col": y * 2 + core}


def iota(shape, dim):
    return lax.broadcasted_iota(jnp.int32, shape, dim)


def sylvester(order):
    v = iota((order, order), 0) & iota((order, order), 1)
    for shift in (4, 2, 1):
        v = v ^ (v >> shift)
    return (1 - 2 * (v & 1)).astype(F32)


def butterfly(vals):
    vals, step = list(vals), 1
    while step < len(vals):
        for i in range(len(vals)):
            if i & step == 0:
                a, b = vals[i], vals[i + step]
                vals[i], vals[i + step] = a + b, a - b
        step *= 2
    return vals


def split(v):
    hi = v.astype(BF16)
    return hi, (v - hi.astype(F32)).astype(BF16)


def wait_bytes(ref, sem):
    pltpu.make_async_copy(ref, ref, sem).wait()


def greet(z, x, y, core, barrier):
    for d in range(1, 8):
        tell(barrier, at((z + d) % 8, x, y, core))
    for d in range(1, 4):
        tell(barrier, at(z, (x + d) % 4, y, core))
        tell(barrier, at(z, x, (y + d) % 4, core))
    tell(barrier, at(z, x, y, 1 - core))


def tell(sem, where):
    pl.semaphore_signal(sem, inc=1, device_id=where, device_id_type=MESH)


def push(src, dst, send_sem, recv_sem, where):
    pltpu.make_async_remote_copy(
        src_ref=src, dst_ref=dst, send_sem=send_sem, recv_sem=recv_sem, device_id=where, device_id_type=MESH
    ).start()


def mix_kernel(
    panel_hbm, signs_hbm, offsets, owners, result, crowded, lists, kept_hbm,
    panel, signs, y_ref, r_ref, t_ref, mine, own, out, lanes, ids, ranks, picks, names_here, names_there,
    s_here, s_there, picked, full_here, full_there, ha, hb, a1, b1, sa, sb, a2, b2, sz, zr,
    load_sem, small_sem, send_sem, recv_sem, core_send, core_recv, list_send, list_recv, plane_sem, all_sem,
    keep_sem, full_send, full_recv, name_send, name_recv, pass_send, pass_recv, s0, r0, s1, r1a, r1b, s2, r2a, r2b, s3, r3,
):
    z, x, y, core = place()
    barrier = pltpu.get_barrier_semaphore()
    greet(z, x, y, core, barrier)

    def load(i):
        span = pl.ds(4096 * i, 4096)
        return pltpu.make_async_copy(panel_hbm.at[:, span], panel.at[:, span], load_sem.at[i])

    small = [
        pltpu.make_async_copy(signs_hbm, signs, small_sem.at[0]),
        pltpu.make_async_copy(offsets, own.at[pl.ds(0, 8)], small_sem.at[1]),
        pltpu.make_async_copy(owners, own.at[pl.ds(8, 8)], small_sem.at[2]),
    ]
    small[0].start()
    for i in range(4):
        load(i).start()
    small[1].start()
    small[2].start()
    table = sylvester(128).astype(BF16)
    table = jnp.concatenate([table, table], axis=0)

    small[0].wait()
    for part in range(4):
        load(part).wait()
        for i in range(2 * part, 2 * part + 2):
            sign = signs[16 * i : 16 * i + 16, :].astype(F32)
            rows = []
            for j in range(16):
                start = (i * 16 + j) * 128
                rows.append(panel[:, start : start + 128] * sign[j : j + 1, :])
            hi, lo = split(jnp.concatenate(rows, axis=0))
            pieces = jnp.concatenate([hi, lo], axis=1)
            done = jnp.dot(pieces, table, preferred_element_type=F32)
            y_ref[16 * i : 16 * i + 16] = done.reshape(16, 16, 128)

    pl.semaphore_wait(barrier, 14)
    for d in range(1, 4):
        tell(plane_sem, at(z, (x + d) % 4, y, core))

    def outer_high(g, carry):
        vals = butterfly([y_ref[g + 8 * j] for j in range(16)])
        for j in range(16):
            y_ref[g + 8 * j] = vals[j]
        return carry

    lax.fori_loop(0, 8, outer_high, 0)

    def outer_low(g, carry):
        vals = butterfly([y_ref[g * 8 + j] for j in range(8)])
        for j in range(8):
            y_ref[g * 8 + j] = vals[j]
        return carry

    lax.fori_loop(0, 16, outer_low, 0)

    slot = y * 32 + z * 4 + x
    to_x = [(x + d) % 4 for d in range(4)]
    to_y = [(y + d) % 4 for d in range(4)]
    sends_list = z // 4 == core

    small[1].wait()
    small[2].wait()
    for r in range(2):
        mine[r : r + 1, :] = own[pl.ds(2 * y + r, 1), :]
        mine[2 + r : 3 + r, :] = own[pl.ds(8 + 2 * y + r, 1), :]

    def send(tz, dx, dy):
        push(
            y_ref.at[tz * 16 + to_x[dx] * 4 + to_y[dy]], r_ref.at[slot],
            send_sem, recv_sem.at[dy], at(tz, to_x[dx], to_y[dy], core),
        )

    def send_list(tz, dx):
        push(mine, lists.at[y, z % 4 * 4 + x], list_send, list_recv, at(tz, to_x[dx], y, core))

    for d in (4, 7, 2, 5, 3, 6, 1):
        tz = (z + d) % 8
        send(tz, 0, 0)
        pl.when(sends_list)(functools.partial(send_list, tz, 0))
    pl.semaphore_wait(plane_sem, 3)
    for d in range(1, 4):
        tell(all_sem, at(z, x, (y + d) % 4, core))

    def sweep(dy, carry_list):
        def some(i, carry):
            tz = (z + i * 3 + 4) % 8
            for dx in range(1 if carry_list else 0, 4):
                send(tz, dx, dy)
                if carry_list:
                    pl.when(sends_list)(functools.partial(send_list, tz, dx))
            return carry

        lax.fori_loop(0, 8, some, 0)

    sweep(0, True)
    pl.semaphore_wait(all_sem, 3)
    for dy in range(1, 4):
        sweep(dy, False)

    r_ref[slot] = y_ref[z * 16 + x * 4 + y]

    @pl.when(sends_list)
    def _():
        lists[y, z % 4 * 4 + x] = mine[...]
        wait_bytes(lists.at[0, pl.ds(0, 15)], list_recv)

    @pl.when(jnp.logical_not(sends_list))
    def _():
        wait_bytes(lists.at[0], list_recv)

    for d in (2, 1, 3):
        push(lists.at[y], lists.at[y], pass_send, pass_recv, at(z, x, to_y[d], core))
    wait_bytes(lists.at[pl.ds(0, 3)], pass_recv)

    turn = (1 - 2 * core).astype(F32)

    def across(dy, carry):
        v = (y + 4 - dy) % 4
        for h in range(2):
            rows = pl.ds(8 * h, 8)
            low = [r_ref[v * 32 + q, rows, :] for q in range(16)]
            high = [r_ref[v * 32 + 16 + q, rows, :] * turn for q in range(16)]
            given = butterfly([a - b for a, b in zip(low, high)])
            for p in range(16):
                t_ref[v, p, rows, :] = given[p]
            kept = butterfly([a + b for a, b in zip(low, high)])
            for p in range(16):
                out[p, v, core, rows, :] = kept[p]
        push(t_ref.at[v], out.at[:, v, core], core_send, core_recv, at(z, x, y, 1 - core))
        return carry

    rank, lane, name, seen = ranked(lists, z * 16 + x * 4 + y)
    lanes[...], ids[...] = lane, name
    ahead = jnp.zeros((1, 1), F32)
    for p in range(16):
        row = rank[p : p + 1, :]
        ranks[p : p + 1, :] = jnp.where(row >= 0.0, row + ahead, -1.0)
        ahead = ahead + seen[p : p + 1, :]

    def locate(p, carry):
        spot, its_name = carry
        one = pl.ds(p, 1)
        hot = (iota((TAKEN, 1024), 0).astype(F32) == ranks[one, :]).astype(F32).astype(BF16)
        facts = jnp.concatenate([lanes[one, :], ids[one, :], jnp.zeros((6, 1024), F32)], axis=0)
        found = lax.dot_general(facts.astype(BF16), hot, NT, preferred_element_type=F32)
        base = (p * 128).astype(F32)
        spot = jnp.where(found[1:2, :] > 0.5, found[0:1, :] + base, spot)
        return spot, its_name + found[1:2, :]

    nowhere = jnp.zeros((1, TAKEN), F32)
    spot, its_name = lax.fori_loop(0, 16, locate, (nowhere - 1.0, nowhere))
    names_here[...] = jnp.broadcast_to(its_name, (8, TAKEN))
    push(names_here, names_there, name_send, name_recv, at(z, x, y, 1 - core))

    def mark(k, carry):
        rows = iota((256, TAKEN), 0).astype(F32) + (k * 256).astype(F32)
        picks[k] = (rows == spot).astype(F32).astype(BF16)
        return carry

    lax.fori_loop(0, 8, mark, 0)

    def tally(p, count):
        for q in range(4):
            slabs = lists[q, p] // 128
            for r in range(2):
                count = count + (slabs[r : r + 1, :] == iota((128, 128), 0)).astype(F32)
        return count

    count = lax.fori_loop(0, 16, tally, jnp.zeros((128, 128), F32))
    most = jnp.max(jnp.sum(count, axis=1, keepdims=True), axis=0, keepdims=True)
    full_here[...] = jnp.broadcast_to(jnp.where(most > TAKEN, 1, 0), (8, 128))
    push(full_here, full_there, full_send, full_recv, at(z, x, y, 1 - core))

    wait_bytes(r_ref.at[pl.ds(0, 31)], recv_sem.at[0])
    across(0, 0)

    def across_next(dy, carry):
        wait_bytes(r_ref.at[pl.ds(0, 32)], recv_sem.at[dy])
        return across(dy, carry)

    lax.fori_loop(1, 4, across_next, 0)
    wait_bytes(t_ref, core_recv)
    keep = pltpu.make_async_copy(out, kept_hbm, keep_sem)
    keep.start()
    got = jnp.zeros((256, TAKEN), F32)
    for g in range(4):
        pick = picks[2 * g : 2 * g + 2].reshape(512, TAKEN)
        got = got + jnp.dot(stacked(out, g), pick, preferred_element_type=F32)
    s_here[...] = got[0:128] + got[128:256]
    push(s_here, s_there, s0, r0, at(z, x, y, 1 - core))
    picked[:, :, :, :, 0:TAKEN] = got.astype(BF16).reshape(2, 4, 2, 16, TAKEN)
    wait_bytes(names_there, name_recv)
    names = jnp.concatenate([names_here[0:1, :], names_there[0:1, :]], axis=1)
    wait_bytes(s_there, r0)
    hi, lo = split(s_there[...])
    picked[0, :, :, :, TAKEN : 2 * TAKEN] = hi.reshape(4, 2, 16, TAKEN)
    picked[1, :, :, :, TAKEN : 2 * TAKEN] = lo.reshape(4, 2, 16, TAKEN)

    def make(i, carry):
        whole = picked[...].reshape(256, 2 * TAKEN)
        half = picked[:, :, core].reshape(128, 2 * TAKEN)
        members = []
        for tx in range(4):
            wanted = (i * 4 + tx + 1).astype(F32)
            members.append(half * (names == wanted).astype(F32).astype(BF16))
        both = lax.dot_general(jnp.concatenate(members, axis=0), whole, NT, preferred_element_type=F32)
        for tx in range(4):
            one = both[128 * tx : 128 * tx + 64] + both[128 * tx + 64 : 128 * tx + 128]
            one = (one[:, :128] + one[:, 128:]).reshape(4, 2, 8, 128)
            ha[i, tx] = one[:, 0]
            hb[i, :, tx] = one[:, 1]
        for d in (2, 1, 3):
            push(ha.at[i, to_x[d]], a1.at[x, i], s1.at[0], r1a.at[i // 2], at(z, to_x[d], y, core))
            push(hb.at[i, to_y[d]], b1.at[y, i], s1.at[1], r1b.at[i // 2], at(z, x, to_y[d], core))
        a1[x, i] = ha[i, x]
        b1[y, i] = hb[i, y]
        return carry

    def second(h):
        wait_bytes(a1.at[pl.ds(0, 3), pl.ds(0, 2)], r1a.at[h])
        wait_bytes(b1.at[pl.ds(0, 3), pl.ds(0, 2)], r1b.at[h])
        for i in range(2):
            for t in range(4):
                n = 2 * h + i
                sa[h, t, i] = (a1[0, n, t] + a1[1, n, t]) + (a1[2, n, t] + a1[3, n, t])
                sb[h, t, i] = (b1[0, n, t] + b1[1, n, t]) + (b1[2, n, t] + b1[3, n, t])
        for d in (2, 1, 3):
            push(sa.at[h, to_y[d]], a2.at[h, y], s2.at[0], r2a.at[h], at(z, x, to_y[d], core))
            push(sb.at[h, to_x[d]], b2.at[h, x], s2.at[1], r2b.at[h], at(z, to_x[d], y, core))
        a2[h, y] = sa[h, y]
        b2[h, x] = sb[h, x]

    def third(h):
        wait_bytes(a2.at[h, pl.ds(0, 3)], r2a.at[h])
        wait_bytes(b2.at[h, pl.ds(0, 3)], r2b.at[h])
        for i in range(2):
            n = 2 * h + i
            sz[n, 0:8, :] = (a2[h, 0, i] + a2[h, 1, i]) + (a2[h, 2, i] + a2[h, 3, i])
            sz[n, 8:16, :] = (b2[h, 0, i] + b2[h, 1, i]) + (b2[h, 2, i] + b2[h, 3, i])
            pl.when(z != n)(functools.partial(push, sz.at[n], zr.at[z], s3, r3, at(n, x, y, core)))

    lax.fori_loop(0, 8, make, 0)
    for stage, h in ((second, 0), (second, 1), (third, 0), (second, 2), (third, 1), (second, 3), (third, 2), (third, 3)):
        stage(h)
    zr[z] = sz[z]
    wait_bytes(zr.at[pl.ds(0, 7)], r3)
    v = [zr[i] for i in range(8)]
    total = ((v[0] + v[1]) + (v[2] + v[3])) + ((v[4] + v[5]) + (v[6] + v[7]))
    result[...] = total * GRAM_SCALE
    wait_bytes(full_there, full_recv)
    crowded[0, 0] = jnp.max(jnp.maximum(full_here[...], full_there[...]))

    wait_bytes(r_ref.at[pl.ds(0, 127)], send_sem)

    @pl.when(sends_list)
    def _():
        for n in range(31):
            wait_bytes(mine, list_send)

    keep.wait()
    wait_bytes(full_here, full_send)
    wait_bytes(names_here, name_send)
    wait_bytes(lists.at[pl.ds(0, 3)], pass_send)
    wait_bytes(s_here, s0)
    wait_bytes(t_ref, core_send)
    wait_bytes(a1.at[pl.ds(0, 3)], s1.at[0])
    wait_bytes(b1.at[pl.ds(0, 3)], s1.at[1])
    wait_bytes(a2.at[:, pl.ds(0, 3)], s2.at[0])
    wait_bytes(b2.at[:, pl.ds(0, 3)], s2.at[1])
    wait_bytes(zr.at[pl.ds(0, 7)], s3)


def ranked(lists, slab):
    here = jnp.concatenate([lists[b // 2, :, b % 2, :] for b in range(8)], axis=1) - slab * 128
    owner = jnp.concatenate([lists[b // 2, :, 2 + b % 2, :] for b in range(8)], axis=1)
    inside = (here >= 0) & (here < 128)
    mask = jnp.where(inside, 1.0, 0.0).astype(F32)
    before = (iota((128, 128), 0) < iota((128, 128), 1)).astype(F32).astype(BF16)
    rank, seen = [], jnp.zeros((16, 1), F32)
    for b in range(8):
        piece = mask[:, 128 * b : 128 * b + 128]
        rank.append(jnp.dot(piece.astype(BF16), before, preferred_element_type=F32) + seen)
        seen = seen + jnp.sum(piece, axis=1, keepdims=True)
    rank = jnp.where(inside, jnp.concatenate(rank, axis=1), -1.0)
    lane = jnp.where(inside, here, 0).astype(F32)
    name = jnp.where(inside, owner + 1, 0).astype(F32)
    return rank, lane, name, seen


def chosen(rank, lane, name, g, first):
    wanted = iota((SLOTS, 1024), 0).astype(F32) + first
    hot = [rank[p : p + 1, :] == wanted for p in range(4 * g, 4 * g + 4)]
    hot = jnp.concatenate([h.astype(F32) for h in hot], axis=0).astype(BF16)
    facts = jnp.concatenate([lane[4 * g : 4 * g + 4], name[4 * g : 4 * g + 4]], axis=0)
    found = lax.dot_general(facts.astype(BF16), hot, NT, preferred_element_type=F32)
    which = iota((1, 128), 1) // SLOTS
    at_lane, its_name = jnp.zeros((1, 128), F32), jnp.zeros((1, 128), F32)
    for p in range(4):
        at_lane = jnp.where(which == p, found[p : p + 1, :] + 128.0 * p, at_lane)
        its_name = jnp.where(which == p, found[4 + p : 5 + p, :], its_name)
    spot = jnp.where(its_name > 0.5, at_lane, -1.0)
    pick = (iota((512, 128), 0).astype(F32) == spot).astype(F32).astype(BF16)
    return pick, its_name


def stacked(mixed, g):
    columns = []
    for p in range(4 * g, 4 * g + 4):
        hi, lo = split(mixed[p].reshape(128, 128))
        columns.append(jnp.concatenate([hi, lo], axis=0))
    return jnp.concatenate(columns, axis=1)


def folded(both):
    return (both[:128, :128] + both[128:, 128:]) + (both[:128, 128:] + both[128:, :128])


def owner_gram(picked, names, o):
    member = (names == o.astype(F32) + 1.0).astype(F32).astype(BF16)
    both = lax.dot_general(picked * member, picked, NT, preferred_element_type=F32)
    return folded(both)


def gram_kernel(mixed, lists, out, picked):
    z, x, y, core = place()
    rank, lane, name, seen = ranked(lists, z * 16 + x * 4 + y)
    rounds = (jnp.max(seen).astype(jnp.int32) + SLOTS - 1) // SLOTS
    out[...] = jnp.zeros_like(out)

    def one_round(r, carry):
        names = []
        for g in range(4):
            pick, its_name = chosen(rank, lane, name, g, (r * SLOTS).astype(F32))
            got = jnp.dot(stacked(mixed, g), pick, preferred_element_type=F32)
            picked[:, 128 * g : 128 * g + 128] = got.astype(BF16)
            names.append(its_name)
        names = jnp.concatenate(names, axis=1)

        def one_owner(o, carry):
            out[o] += owner_gram(picked[...], names, o) * GRAM_SCALE
            return carry

        lax.fori_loop(0, 32, one_owner, 0)
        return carry

    lax.fori_loop(0, rounds, one_round, 0)


def sum_kernel(gram, out, c_ref, ha, hb, a1, b1, sa, sb, a2, b2, sz, zr, s0, r0, s1, r1, s2, r2, s3, r3):
    z, x, y, core = place()

    barrier = pltpu.get_barrier_semaphore()
    greet(z, x, y, core, barrier)
    pl.semaphore_wait(barrier, 14)
    push(gram.at[:, :, :, 1 - core], c_ref, s0, r0, at(z, x, y, 1 - core))
    wait_bytes(c_ref, r0)

    def add_core(i, carry):
        for tx in range(4):
            for ty in range(4):
                ha[tx, i, ty] = gram[i, tx, ty, core, 0:8, :] + c_ref[i, tx, ty, 0:8, :]
                hb[ty, i, tx] = gram[i, tx, ty, core, 8:16, :] + c_ref[i, tx, ty, 8:16, :]
        return carry

    lax.fori_loop(0, 8, add_core, 0)
    for d in (2, 1, 3):
        tx, ty = (x + d) % 4, (y + d) % 4
        push(ha.at[tx], a1.at[x], s1.at[0], r1.at[0], at(z, tx, y, core))
        push(hb.at[ty], b1.at[y], s1.at[1], r1.at[1], at(z, x, ty, core))
    a1[x] = ha[x]
    b1[y] = hb[y]
    wait_bytes(a1.at[pl.ds(0, 3)], r1.at[0])
    wait_bytes(b1.at[pl.ds(0, 3)], r1.at[1])

    def add_first(i, carry):
        for t in range(4):
            sa[t, i] = (a1[0, i, t] + a1[1, i, t]) + (a1[2, i, t] + a1[3, i, t])
            sb[t, i] = (b1[0, i, t] + b1[1, i, t]) + (b1[2, i, t] + b1[3, i, t])
        return carry

    lax.fori_loop(0, 8, add_first, 0)
    for d in (2, 1, 3):
        tx, ty = (x + d) % 4, (y + d) % 4
        push(sa.at[ty], a2.at[y], s2.at[0], r2.at[0], at(z, x, ty, core))
        push(sb.at[tx], b2.at[x], s2.at[1], r2.at[1], at(z, tx, y, core))
    a2[y] = sa[y]
    b2[x] = sb[x]
    wait_bytes(a2.at[pl.ds(0, 3)], r2.at[0])
    wait_bytes(b2.at[pl.ds(0, 3)], r2.at[1])
    for i in range(8):
        sz[i, 0:8, :] = (a2[0, i] + a2[1, i]) + (a2[2, i] + a2[3, i])
        sz[i, 8:16, :] = (b2[0, i] + b2[1, i]) + (b2[2, i] + b2[3, i])
    for d in (4, 3, 5, 2, 6, 1, 7):
        tz = (z + d) % 8
        push(sz.at[tz], zr.at[z], s3, r3, at(tz, x, y, core))
    zr[z] = sz[z]
    wait_bytes(zr.at[pl.ds(0, 7)], r3)
    v = [zr[i] for i in range(8)]
    out[...] = ((v[0] + v[1]) + (v[2] + v[3])) + ((v[4] + v[5]) + (v[6] + v[7]))
    wait_bytes(c_ref, s0)
    for n in range(2):
        wait_bytes(a1.at[pl.ds(0, 3)], s1.at[n])
        wait_bytes(a2.at[pl.ds(0, 3)], s2.at[n])
    wait_bytes(zr.at[pl.ds(0, 7)], s3)


def body(panel, signs, offsets, owners):
    params = functools.partial(pltpu.CompilerParams, has_side_effects=True)
    dma, vmem = pltpu.SemaphoreType.DMA, pltpu.VMEM
    result, crowded, lists, mixed = pl.pallas_call(
        mix_kernel,
        out_shape=[
            jax.ShapeDtypeStruct((16, 128), F32),
            jax.ShapeDtypeStruct((1, 1), jnp.int32),
            jax.ShapeDtypeStruct((4, 16, 4, 128), jnp.int32),
            jax.ShapeDtypeStruct((16, 4, 2, 16, 128), F32),
        ],
        in_specs=[HBM] * 4,
        out_specs=[VMEM, SMEM, VMEM, HBM],
        scratch_shapes=[
            vmem((16, 16384), F32),
            vmem((128, 128), jnp.int32),
            vmem((128, 16, 128), F32),
            vmem((128, 16, 128), F32),
            vmem((4, 16, 16, 128), F32),
            vmem((4, 128), jnp.int32),
            vmem((16, 128), jnp.int32),
            vmem((16, 4, 2, 16, 128), F32),
            vmem((16, 1024), F32),
            vmem((16, 1024), F32),
            vmem((16, 1024), F32),
            vmem((8, 256, TAKEN), BF16),
            vmem((8, TAKEN), F32),
            vmem((8, TAKEN), F32),
            vmem((128, TAKEN), F32),
            vmem((128, TAKEN), F32),
            vmem((2, 4, 2, 16, 2 * TAKEN), BF16),
            vmem((8, 128), jnp.int32),
            vmem((8, 128), jnp.int32),
            vmem((8, 4, 4, 8, 128), F32),
            vmem((8, 4, 4, 8, 128), F32),
            vmem((4, 8, 4, 8, 128), F32),
            vmem((4, 8, 4, 8, 128), F32),
            vmem((4, 4, 2, 8, 128), F32),
            vmem((4, 4, 2, 8, 128), F32),
            vmem((4, 4, 2, 8, 128), F32),
            vmem((4, 4, 2, 8, 128), F32),
            vmem((8, 16, 128), F32),
            vmem((8, 16, 128), F32),
            dma((4,)), dma((3,)), dma, dma((4,)), dma, dma, dma, dma,
            pltpu.SemaphoreType.REGULAR, pltpu.SemaphoreType.REGULAR,
            dma, dma, dma, dma, dma, dma, dma, dma, dma, dma((2,)), dma((4,)), dma((4,)),
            dma((2,)), dma((4,)), dma((4,)), dma, dma,
        ],
        compiler_params=params(collective_id=1, vmem_limit_bytes=MIX_VMEM),
        name="mix",
    )(panel, signs.reshape(128, 128), offsets.reshape(8, 128), owners.reshape(8, 128))

    def in_rounds():
        gram = pl.pallas_call(
            gram_kernel,
            out_shape=jax.ShapeDtypeStruct((32, 128, 128), F32),
            in_specs=[VMEM] * 2,
            out_specs=VMEM,
            scratch_shapes=[vmem((256, 512), BF16)],
            compiler_params=pltpu.CompilerParams(vmem_limit_bytes=48 << 20),
            name="gram_rounds",
        )(mixed.reshape(16, 128, 128), lists)
        return pl.pallas_call(
            sum_kernel,
            out_shape=jax.ShapeDtypeStruct((16, 128), F32),
            in_specs=[VMEM],
            out_specs=VMEM,
            scratch_shapes=[
                vmem((8, 4, 4, 16, 128), F32),
                vmem((4, 8, 4, 8, 128), F32),
                vmem((4, 8, 4, 8, 128), F32),
                vmem((4, 8, 4, 8, 128), F32),
                vmem((4, 8, 4, 8, 128), F32),
                vmem((4, 8, 8, 128), F32),
                vmem((4, 8, 8, 128), F32),
                vmem((4, 8, 8, 128), F32),
                vmem((4, 8, 8, 128), F32),
                vmem((8, 16, 128), F32),
                vmem((8, 16, 128), F32),
            ] + [dma] * 2 + [dma((2,))] * 4 + [dma] * 2,
            compiler_params=params(collective_id=2, vmem_limit_bytes=48 << 20),
            name="sum_rounds",
        )(gram.reshape(8, 4, 4, 2, 16, 128))

    return lax.cond(crowded[0, 0] > 0, in_rounds, lambda: result)[None]


def solution(mesh):
    placed = (P("col", "row"), P("row"), P("row"), P("row", None))
    return jax.shard_map(
        body, mesh=mesh, in_specs=placed, out_specs=P("row", "col", None), check_vma=False
    )
```

```python
import functools

import jax
import jax.numpy as jnp
from jax import lax
from jax.experimental import pallas as pl
from jax.experimental.pallas import tpu as pltpu
from jax.sharding import PartitionSpec as P

MESH = pl.DeviceIdType.MESH
F32 = jnp.float32
BF16 = jnp.bfloat16
NT = (((1,), (1,)), ((), ()))
VMEM = pl.BlockSpec(memory_space=pltpu.VMEM)
SMEM = pl.BlockSpec(memory_space=pltpu.SMEM)
HBM = pl.BlockSpec(memory_space=pltpu.HBM)
SLOTS = 32
TAKEN = 256
MIX_VMEM = 60 << 20
GRAM_SCALE = 2.0 ** -29


def place():
    row, col = lax.axis_index("row"), lax.axis_index("col")
    return row // 4, row % 4, col // 2, col % 2


def at(z, x, y, core):
    return {"row": z * 4 + x, "col": y * 2 + core}


def iota(shape, dim):
    return lax.broadcasted_iota(jnp.int32, shape, dim)


def sylvester(order):
    v = iota((order, order), 0) & iota((order, order), 1)
    for shift in (4, 2, 1):
        v = v ^ (v >> shift)
    return (1 - 2 * (v & 1)).astype(F32)


def butterfly(vals):
    vals, step = list(vals), 1
    while step < len(vals):
        for i in range(len(vals)):
            if i & step == 0:
                a, b = vals[i], vals[i + step]
                vals[i], vals[i + step] = a + b, a - b
        step *= 2
    return vals


def split(v):
    hi = v.astype(BF16)
    return hi, (v - hi.astype(F32)).astype(BF16)


def wait_bytes(ref, sem):
    pltpu.make_async_copy(ref, ref, sem).wait()


def greet(z, x, y, core, barrier):
    for d in range(1, 8):
        tell(barrier, at((z + d) % 8, x, y, core))
    for d in range(1, 4):
        tell(barrier, at(z, (x + d) % 4, y, core))
        tell(barrier, at(z, x, (y + d) % 4, core))
    tell(barrier, at(z, x, y, 1 - core))


def tell(sem, where):
    pl.semaphore_signal(sem, inc=1, device_id=where, device_id_type=MESH)


def push(src, dst, send_sem, recv_sem, where):
    pltpu.make_async_remote_copy(
        src_ref=src, dst_ref=dst, send_sem=send_sem, recv_sem=recv_sem, device_id=where, device_id_type=MESH
    ).start()


def mix_kernel(
    panel_hbm, signs_hbm, offsets, owners, result, crowded, lists, kept_hbm,
    panel, signs, y_ref, r_ref, t_ref, mine, own, out, lanes, ids, ranks, picks, names_here, names_there,
    s_here, s_there, picked, full_here, full_there, ha, hb, a1, b1, sa, sb, fa, fb,
    load_sem, small_sem, send_sem, recv_sem, core_send, core_recv, list_send, list_recv, plane_sem, all_sem,
    keep_sem, full_send, full_recv, name_send, name_recv, pass_send, pass_recv, s0, r0, s1, r1a, r1b, s2, r2,
):
    z, x, y, core = place()
    barrier = pltpu.get_barrier_semaphore()
    greet(z, x, y, core, barrier)

    def load(i):
        span = pl.ds(4096 * i, 4096)
        return pltpu.make_async_copy(panel_hbm.at[:, span], panel.at[:, span], load_sem.at[i])

    small = [
        pltpu.make_async_copy(signs_hbm, signs, small_sem.at[0]),
        pltpu.make_async_copy(offsets, own.at[pl.ds(0, 8)], small_sem.at[1]),
        pltpu.make_async_copy(owners, own.at[pl.ds(8, 8)], small_sem.at[2]),
    ]
    small[0].start()
    for i in range(4):
        load(i).start()
    small[1].start()
    small[2].start()
    table = sylvester(128).astype(BF16)
    table = jnp.concatenate([table, table], axis=0)

    small[0].wait()
    for part in range(4):
        load(part).wait()
        for i in range(2 * part, 2 * part + 2):
            sign = signs[16 * i : 16 * i + 16, :].astype(F32)
            rows = []
            for j in range(16):
                start = (i * 16 + j) * 128
                rows.append(panel[:, start : start + 128] * sign[j : j + 1, :])
            hi, lo = split(jnp.concatenate(rows, axis=0))
            pieces = jnp.concatenate([hi, lo], axis=1)
            done = jnp.dot(pieces, table, preferred_element_type=F32)
            y_ref[16 * i : 16 * i + 16] = done.reshape(16, 16, 128)

    pl.semaphore_wait(barrier, 14)
    for d in range(1, 4):
        tell(plane_sem, at(z, (x + d) % 4, y, core))

    def outer_high(g, carry):
        vals = butterfly([y_ref[g + 8 * j] for j in range(16)])
        for j in range(16):
            y_ref[g + 8 * j] = vals[j]
        return carry

    lax.fori_loop(0, 8, outer_high, 0)

    def outer_low(g, carry):
        vals = butterfly([y_ref[g * 8 + j] for j in range(8)])
        for j in range(8):
            y_ref[g * 8 + j] = vals[j]
        return carry

    lax.fori_loop(0, 16, outer_low, 0)

    slot = y * 32 + z * 4 + x
    to_x = [(x + d) % 4 for d in range(4)]
    to_y = [(y + d) % 4 for d in range(4)]
    sends_list = z // 4 == core

    small[1].wait()
    small[2].wait()
    for r in range(2):
        mine[r : r + 1, :] = own[pl.ds(2 * y + r, 1), :]
        mine[2 + r : 3 + r, :] = own[pl.ds(8 + 2 * y + r, 1), :]

    def send(tz, dx, dy):
        push(
            y_ref.at[tz * 16 + to_x[dx] * 4 + to_y[dy]], r_ref.at[slot],
            send_sem, recv_sem.at[dy], at(tz, to_x[dx], to_y[dy], core),
        )

    def send_list(tz, dx):
        push(mine, lists.at[y, z % 4 * 4 + x], list_send, list_recv, at(tz, to_x[dx], y, core))

    for d in (4, 7, 2, 5, 3, 6, 1):
        tz = (z + d) % 8
        send(tz, 0, 0)
        pl.when(sends_list)(functools.partial(send_list, tz, 0))
    pl.semaphore_wait(plane_sem, 3)
    for d in range(1, 4):
        tell(all_sem, at(z, x, (y + d) % 4, core))

    def sweep(dy, carry_list):
        def some(i, carry):
            tz = (z + i * 3 + 4) % 8
            for dx in range(1 if carry_list else 0, 4):
                send(tz, dx, dy)
                if carry_list:
                    pl.when(sends_list)(functools.partial(send_list, tz, dx))
            return carry

        lax.fori_loop(0, 8, some, 0)

    sweep(0, True)
    pl.semaphore_wait(all_sem, 3)
    for dy in range(1, 4):
        sweep(dy, False)

    r_ref[slot] = y_ref[z * 16 + x * 4 + y]

    @pl.when(sends_list)
    def _():
        lists[y, z % 4 * 4 + x] = mine[...]
        wait_bytes(lists.at[0, pl.ds(0, 15)], list_recv)

    @pl.when(jnp.logical_not(sends_list))
    def _():
        wait_bytes(lists.at[0], list_recv)

    for d in (2, 1, 3):
        push(lists.at[y], lists.at[y], pass_send, pass_recv, at(z, x, to_y[d], core))
    wait_bytes(lists.at[pl.ds(0, 3)], pass_recv)

    turn = (1 - 2 * core).astype(F32)

    def across(dy, carry):
        v = (y + 4 - dy) % 4
        for h in range(2):
            rows = pl.ds(8 * h, 8)
            low = [r_ref[v * 32 + q, rows, :] for q in range(16)]
            high = [r_ref[v * 32 + 16 + q, rows, :] * turn for q in range(16)]
            given = butterfly([a - b for a, b in zip(low, high)])
            for p in range(16):
                t_ref[v, p, rows, :] = given[p]
            kept = butterfly([a + b for a, b in zip(low, high)])
            for p in range(16):
                out[p, v, core, rows, :] = kept[p]
        push(t_ref.at[v], out.at[:, v, core], core_send, core_recv, at(z, x, y, 1 - core))
        return carry

    rank, lane, name, seen = ranked(lists, z * 16 + x * 4 + y)
    lanes[...], ids[...] = lane, name
    ahead = jnp.zeros((1, 1), F32)
    for p in range(16):
        row = rank[p : p + 1, :]
        ranks[p : p + 1, :] = jnp.where(row >= 0.0, row + ahead, -1.0)
        ahead = ahead + seen[p : p + 1, :]

    def locate(p, carry):
        spot, its_name = carry
        one = pl.ds(p, 1)
        hot = (iota((TAKEN, 1024), 0).astype(F32) == ranks[one, :]).astype(F32).astype(BF16)
        facts = jnp.concatenate([lanes[one, :], ids[one, :], jnp.zeros((6, 1024), F32)], axis=0)
        found = lax.dot_general(facts.astype(BF16), hot, NT, preferred_element_type=F32)
        base = (p * 128).astype(F32)
        spot = jnp.where(found[1:2, :] > 0.5, found[0:1, :] + base, spot)
        return spot, its_name + found[1:2, :]

    nowhere = jnp.zeros((1, TAKEN), F32)
    spot, its_name = lax.fori_loop(0, 16, locate, (nowhere - 1.0, nowhere))
    names_here[...] = jnp.broadcast_to(its_name, (8, TAKEN))
    push(names_here, names_there, name_send, name_recv, at(z, x, y, 1 - core))

    def mark(k, carry):
        rows = iota((256, TAKEN), 0).astype(F32) + (k * 256).astype(F32)
        picks[k] = (rows == spot).astype(F32).astype(BF16)
        return carry

    lax.fori_loop(0, 8, mark, 0)

    def tally(p, count):
        for q in range(4):
            slabs = lists[q, p] // 128
            for r in range(2):
                count = count + (slabs[r : r + 1, :] == iota((128, 128), 0)).astype(F32)
        return count

    count = lax.fori_loop(0, 16, tally, jnp.zeros((128, 128), F32))
    most = jnp.max(jnp.sum(count, axis=1, keepdims=True), axis=0, keepdims=True)
    full_here[...] = jnp.broadcast_to(jnp.where(most > TAKEN, 1, 0), (8, 128))
    push(full_here, full_there, full_send, full_recv, at(z, x, y, 1 - core))

    wait_bytes(r_ref.at[pl.ds(0, 31)], recv_sem.at[0])
    across(0, 0)

    def across_next(dy, carry):
        wait_bytes(r_ref.at[pl.ds(0, 32)], recv_sem.at[dy])
        return across(dy, carry)

    lax.fori_loop(1, 4, across_next, 0)
    wait_bytes(t_ref, core_recv)
    keep = pltpu.make_async_copy(out, kept_hbm, keep_sem)
    keep.start()
    got = jnp.zeros((256, TAKEN), F32)
    for g in range(4):
        pick = picks[2 * g : 2 * g + 2].reshape(512, TAKEN)
        got = got + jnp.dot(stacked(out, g), pick, preferred_element_type=F32)
    s_here[...] = got[0:128] + got[128:256]
    push(s_here, s_there, s0, r0, at(z, x, y, 1 - core))
    picked[:, :, :, :, 0:TAKEN] = got.astype(BF16).reshape(2, 4, 2, 16, TAKEN)
    wait_bytes(names_there, name_recv)
    names = jnp.concatenate([names_here[0:1, :], names_there[0:1, :]], axis=1)
    wait_bytes(s_there, r0)
    hi, lo = split(s_there[...])
    picked[0, :, :, :, TAKEN : 2 * TAKEN] = hi.reshape(4, 2, 16, TAKEN)
    picked[1, :, :, :, TAKEN : 2 * TAKEN] = lo.reshape(4, 2, 16, TAKEN)

    def make(k, carry):
        i = (z + k * 3 + 4) % 8
        whole = picked[...].reshape(256, 2 * TAKEN)
        half = picked[:, :, core].reshape(128, 2 * TAKEN)
        members = []
        for tx in range(4):
            wanted = (i * 4 + tx + 1).astype(F32)
            members.append(half * (names == wanted).astype(F32).astype(BF16))
        both = lax.dot_general(jnp.concatenate(members, axis=0), whole, NT, preferred_element_type=F32)
        for tx in range(4):
            one = both[128 * tx : 128 * tx + 64] + both[128 * tx + 64 : 128 * tx + 128]
            one = (one[:, :128] + one[:, 128:]).reshape(4, 2, 8, 128)
            ha[i, tx] = one[:, 0]
            hb[i, :, tx] = one[:, 1]
        for d in (2, 1, 3):
            push(ha.at[i, to_x[d]], a1.at[x, i], s1.at[0], r1a.at[i], at(z, to_x[d], y, core))
            push(hb.at[i, to_y[d]], b1.at[y, i], s1.at[1], r1b.at[i], at(z, x, to_y[d], core))
        a1[x, i] = ha[i, x]
        b1[y, i] = hb[i, y]
        return carry

    def direct(k, carry):
        i = (z + k * 3 + 4) % 8
        wait_bytes(a1.at[pl.ds(0, 3), i], r1a.at[i])
        for t in range(4):
            sa[i, t] = (a1[0, i, t] + a1[1, i, t]) + (a1[2, i, t] + a1[3, i, t])
        for d in (2, 1, 3, 0):
            go = functools.partial(
                push, sa.at[i, to_y[d]], fa.at[z * 4 + y], s2.at[0], r2.at[0], at(i, x, to_y[d], core)
            )
            go() if d else pl.when(i != z)(go)
        wait_bytes(b1.at[pl.ds(0, 3), i], r1b.at[i])
        for t in range(4):
            sb[i, t] = (b1[0, i, t] + b1[1, i, t]) + (b1[2, i, t] + b1[3, i, t])
        for d in (2, 1, 3, 0):
            go = functools.partial(
                push, sb.at[i, to_x[d]], fb.at[z * 4 + x], s2.at[1], r2.at[1], at(i, to_x[d], y, core)
            )
            go() if d else pl.when(i != z)(go)
        return carry

    lax.fori_loop(0, 8, make, 0)
    lax.fori_loop(0, 8, direct, 0)
    fa[z * 4 + y] = sa[z, y]
    fb[z * 4 + x] = sb[z, x]
    for n, ref in enumerate((fa, fb)):
        wait_bytes(ref.at[pl.ds(0, 31)], r2.at[n])
        parts = [ref[i] for i in range(32)]
        while len(parts) > 1:
            parts = [a + b for a, b in zip(parts[::2], parts[1::2])]
        result[8 * n : 8 * n + 8, :] = parts[0] * GRAM_SCALE
    wait_bytes(full_there, full_recv)
    crowded[0, 0] = jnp.max(jnp.maximum(full_here[...], full_there[...]))

    wait_bytes(r_ref.at[pl.ds(0, 127)], send_sem)

    @pl.when(sends_list)
    def _():
        for n in range(31):
            wait_bytes(mine, list_send)

    keep.wait()
    wait_bytes(full_here, full_send)
    wait_bytes(names_here, name_send)
    wait_bytes(lists.at[pl.ds(0, 3)], pass_send)
    wait_bytes(s_here, s0)
    wait_bytes(t_ref, core_send)
    wait_bytes(a1.at[pl.ds(0, 3)], s1.at[0])
    wait_bytes(b1.at[pl.ds(0, 3)], s1.at[1])
    wait_bytes(fa.at[pl.ds(0, 31)], s2.at[0])
    wait_bytes(fb.at[pl.ds(0, 31)], s2.at[1])


def ranked(lists, slab):
    here = jnp.concatenate([lists[b // 2, :, b % 2, :] for b in range(8)], axis=1) - slab * 128
    owner = jnp.concatenate([lists[b // 2, :, 2 + b % 2, :] for b in range(8)], axis=1)
    inside = (here >= 0) & (here < 128)
    mask = jnp.where(inside, 1.0, 0.0).astype(F32)
    before = (iota((128, 128), 0) < iota((128, 128), 1)).astype(F32).astype(BF16)
    rank, seen = [], jnp.zeros((16, 1), F32)
    for b in range(8):
        piece = mask[:, 128 * b : 128 * b + 128]
        rank.append(jnp.dot(piece.astype(BF16), before, preferred_element_type=F32) + seen)
        seen = seen + jnp.sum(piece, axis=1, keepdims=True)
    rank = jnp.where(inside, jnp.concatenate(rank, axis=1), -1.0)
    lane = jnp.where(inside, here, 0).astype(F32)
    name = jnp.where(inside, owner + 1, 0).astype(F32)
    return rank, lane, name, seen


def chosen(rank, lane, name, g, first):
    wanted = iota((SLOTS, 1024), 0).astype(F32) + first
    hot = [rank[p : p + 1, :] == wanted for p in range(4 * g, 4 * g + 4)]
    hot = jnp.concatenate([h.astype(F32) for h in hot], axis=0).astype(BF16)
    facts = jnp.concatenate([lane[4 * g : 4 * g + 4], name[4 * g : 4 * g + 4]], axis=0)
    found = lax.dot_general(facts.astype(BF16), hot, NT, preferred_element_type=F32)
    which = iota((1, 128), 1) // SLOTS
    at_lane, its_name = jnp.zeros((1, 128), F32), jnp.zeros((1, 128), F32)
    for p in range(4):
        at_lane = jnp.where(which == p, found[p : p + 1, :] + 128.0 * p, at_lane)
        its_name = jnp.where(which == p, found[4 + p : 5 + p, :], its_name)
    spot = jnp.where(its_name > 0.5, at_lane, -1.0)
    pick = (iota((512, 128), 0).astype(F32) == spot).astype(F32).astype(BF16)
    return pick, its_name


def stacked(mixed, g):
    columns = []
    for p in range(4 * g, 4 * g + 4):
        hi, lo = split(mixed[p].reshape(128, 128))
        columns.append(jnp.concatenate([hi, lo], axis=0))
    return jnp.concatenate(columns, axis=1)


def folded(both):
    return (both[:128, :128] + both[128:, 128:]) + (both[:128, 128:] + both[128:, :128])


def owner_gram(picked, names, o):
    member = (names == o.astype(F32) + 1.0).astype(F32).astype(BF16)
    both = lax.dot_general(picked * member, picked, NT, preferred_element_type=F32)
    return folded(both)


def gram_kernel(mixed, lists, out, picked):
    z, x, y, core = place()
    rank, lane, name, seen = ranked(lists, z * 16 + x * 4 + y)
    rounds = (jnp.max(seen).astype(jnp.int32) + SLOTS - 1) // SLOTS
    out[...] = jnp.zeros_like(out)

    def one_round(r, carry):
        names = []
        for g in range(4):
            pick, its_name = chosen(rank, lane, name, g, (r * SLOTS).astype(F32))
            got = jnp.dot(stacked(mixed, g), pick, preferred_element_type=F32)
            picked[:, 128 * g : 128 * g + 128] = got.astype(BF16)
            names.append(its_name)
        names = jnp.concatenate(names, axis=1)

        def one_owner(o, carry):
            out[o] += owner_gram(picked[...], names, o) * GRAM_SCALE
            return carry

        lax.fori_loop(0, 32, one_owner, 0)
        return carry

    lax.fori_loop(0, rounds, one_round, 0)


def sum_kernel(gram, out, c_ref, ha, hb, a1, b1, sa, sb, a2, b2, sz, zr, s0, r0, s1, r1, s2, r2, s3, r3):
    z, x, y, core = place()

    barrier = pltpu.get_barrier_semaphore()
    greet(z, x, y, core, barrier)
    pl.semaphore_wait(barrier, 14)
    push(gram.at[:, :, :, 1 - core], c_ref, s0, r0, at(z, x, y, 1 - core))
    wait_bytes(c_ref, r0)

    def add_core(i, carry):
        for tx in range(4):
            for ty in range(4):
                ha[tx, i, ty] = gram[i, tx, ty, core, 0:8, :] + c_ref[i, tx, ty, 0:8, :]
                hb[ty, i, tx] = gram[i, tx, ty, core, 8:16, :] + c_ref[i, tx, ty, 8:16, :]
        return carry

    lax.fori_loop(0, 8, add_core, 0)
    for d in (2, 1, 3):
        tx, ty = (x + d) % 4, (y + d) % 4
        push(ha.at[tx], a1.at[x], s1.at[0], r1.at[0], at(z, tx, y, core))
        push(hb.at[ty], b1.at[y], s1.at[1], r1.at[1], at(z, x, ty, core))
    a1[x] = ha[x]
    b1[y] = hb[y]
    wait_bytes(a1.at[pl.ds(0, 3)], r1.at[0])
    wait_bytes(b1.at[pl.ds(0, 3)], r1.at[1])

    def add_first(i, carry):
        for t in range(4):
            sa[t, i] = (a1[0, i, t] + a1[1, i, t]) + (a1[2, i, t] + a1[3, i, t])
            sb[t, i] = (b1[0, i, t] + b1[1, i, t]) + (b1[2, i, t] + b1[3, i, t])
        return carry

    lax.fori_loop(0, 8, add_first, 0)
    for d in (2, 1, 3):
        tx, ty = (x + d) % 4, (y + d) % 4
        push(sa.at[ty], a2.at[y], s2.at[0], r2.at[0], at(z, x, ty, core))
        push(sb.at[tx], b2.at[x], s2.at[1], r2.at[1], at(z, tx, y, core))
    a2[y] = sa[y]
    b2[x] = sb[x]
    wait_bytes(a2.at[pl.ds(0, 3)], r2.at[0])
    wait_bytes(b2.at[pl.ds(0, 3)], r2.at[1])
    for i in range(8):
        sz[i, 0:8, :] = (a2[0, i] + a2[1, i]) + (a2[2, i] + a2[3, i])
        sz[i, 8:16, :] = (b2[0, i] + b2[1, i]) + (b2[2, i] + b2[3, i])
    for d in (4, 3, 5, 2, 6, 1, 7):
        tz = (z + d) % 8
        push(sz.at[tz], zr.at[z], s3, r3, at(tz, x, y, core))
    zr[z] = sz[z]
    wait_bytes(zr.at[pl.ds(0, 7)], r3)
    v = [zr[i] for i in range(8)]
    out[...] = ((v[0] + v[1]) + (v[2] + v[3])) + ((v[4] + v[5]) + (v[6] + v[7]))
    wait_bytes(c_ref, s0)
    for n in range(2):
        wait_bytes(a1.at[pl.ds(0, 3)], s1.at[n])
        wait_bytes(a2.at[pl.ds(0, 3)], s2.at[n])
    wait_bytes(zr.at[pl.ds(0, 7)], s3)


def body(panel, signs, offsets, owners):
    params = functools.partial(pltpu.CompilerParams, has_side_effects=True)
    dma, vmem = pltpu.SemaphoreType.DMA, pltpu.VMEM
    result, crowded, lists, mixed = pl.pallas_call(
        mix_kernel,
        out_shape=[
            jax.ShapeDtypeStruct((16, 128), F32),
            jax.ShapeDtypeStruct((1, 1), jnp.int32),
            jax.ShapeDtypeStruct((4, 16, 4, 128), jnp.int32),
            jax.ShapeDtypeStruct((16, 4, 2, 16, 128), F32),
        ],
        in_specs=[HBM] * 4,
        out_specs=[VMEM, SMEM, VMEM, HBM],
        scratch_shapes=[
            vmem((16, 16384), F32),
            vmem((128, 128), jnp.int32),
            vmem((128, 16, 128), F32),
            vmem((128, 16, 128), F32),
            vmem((4, 16, 16, 128), F32),
            vmem((4, 128), jnp.int32),
            vmem((16, 128), jnp.int32),
            vmem((16, 4, 2, 16, 128), F32),
            vmem((16, 1024), F32),
            vmem((16, 1024), F32),
            vmem((16, 1024), F32),
            vmem((8, 256, TAKEN), BF16),
            vmem((8, TAKEN), F32),
            vmem((8, TAKEN), F32),
            vmem((128, TAKEN), F32),
            vmem((128, TAKEN), F32),
            vmem((2, 4, 2, 16, 2 * TAKEN), BF16),
            vmem((8, 128), jnp.int32),
            vmem((8, 128), jnp.int32),
            vmem((8, 4, 4, 8, 128), F32),
            vmem((8, 4, 4, 8, 128), F32),
            vmem((4, 8, 4, 8, 128), F32),
            vmem((4, 8, 4, 8, 128), F32),
            vmem((8, 4, 8, 128), F32),
            vmem((8, 4, 8, 128), F32),
            vmem((32, 8, 128), F32),
            vmem((32, 8, 128), F32),
            dma((4,)), dma((3,)), dma, dma((4,)), dma, dma, dma, dma,
            pltpu.SemaphoreType.REGULAR, pltpu.SemaphoreType.REGULAR,
            dma, dma, dma, dma, dma, dma, dma, dma, dma, dma((2,)), dma((8,)), dma((8,)),
            dma((2,)), dma((2,)),
        ],
        compiler_params=params(collective_id=1, vmem_limit_bytes=MIX_VMEM),
        name="mix",
    )(panel, signs.reshape(128, 128), offsets.reshape(8, 128), owners.reshape(8, 128))

    def in_rounds():
        gram = pl.pallas_call(
            gram_kernel,
            out_shape=jax.ShapeDtypeStruct((32, 128, 128), F32),
            in_specs=[VMEM] * 2,
            out_specs=VMEM,
            scratch_shapes=[vmem((256, 512), BF16)],
            compiler_params=pltpu.CompilerParams(vmem_limit_bytes=48 << 20),
            name="gram_rounds",
        )(mixed.reshape(16, 128, 128), lists)
        return pl.pallas_call(
            sum_kernel,
            out_shape=jax.ShapeDtypeStruct((16, 128), F32),
            in_specs=[VMEM],
            out_specs=VMEM,
            scratch_shapes=[
                vmem((8, 4, 4, 16, 128), F32),
                vmem((4, 8, 4, 8, 128), F32),
                vmem((4, 8, 4, 8, 128), F32),
                vmem((4, 8, 4, 8, 128), F32),
                vmem((4, 8, 4, 8, 128), F32),
                vmem((4, 8, 8, 128), F32),
                vmem((4, 8, 8, 128), F32),
                vmem((4, 8, 8, 128), F32),
                vmem((4, 8, 8, 128), F32),
                vmem((8, 16, 128), F32),
                vmem((8, 16, 128), F32),
            ] + [dma] * 2 + [dma((2,))] * 4 + [dma] * 2,
            compiler_params=params(collective_id=2, vmem_limit_bytes=48 << 20),
            name="sum_rounds",
        )(gram.reshape(8, 4, 4, 2, 16, 128))

    return lax.cond(crowded[0, 0] > 0, in_rounds, lambda: result)[None]


def solution(mesh):
    placed = (P("col", "row"), P("row"), P("row"), P("row", None))
    return jax.shard_map(
        body, mesh=mesh, in_specs=placed, out_specs=P("row", "col", None), check_vma=False
    )
```

```python
import functools

import jax
import jax.numpy as jnp
from jax import lax
from jax.experimental import pallas as pl
from jax.experimental.pallas import tpu as pltpu
from jax.sharding import PartitionSpec as P

MESH = pl.DeviceIdType.MESH
F32 = jnp.float32
BF16 = jnp.bfloat16
NT = (((1,), (1,)), ((), ()))
VMEM = pl.BlockSpec(memory_space=pltpu.VMEM)
SMEM = pl.BlockSpec(memory_space=pltpu.SMEM)
HBM = pl.BlockSpec(memory_space=pltpu.HBM)
SLOTS = 32
TAKEN = 256
MIX_VMEM = 60 << 20
GRAM_SCALE = 2.0 ** -29


def place():
    row, col = lax.axis_index("row"), lax.axis_index("col")
    return row // 4, row % 4, col // 2, col % 2


def at(z, x, y, core):
    return {"row": z * 4 + x, "col": y * 2 + core}


def iota(shape, dim):
    return lax.broadcasted_iota(jnp.int32, shape, dim)


def sylvester(order):
    v = iota((order, order), 0) & iota((order, order), 1)
    for shift in (4, 2, 1):
        v = v ^ (v >> shift)
    return (1 - 2 * (v & 1)).astype(F32)


def butterfly(vals):
    vals, step = list(vals), 1
    while step < len(vals):
        for i in range(len(vals)):
            if i & step == 0:
                a, b = vals[i], vals[i + step]
                vals[i], vals[i + step] = a + b, a - b
        step *= 2
    return vals


def split(v):
    hi = v.astype(BF16)
    return hi, (v - hi.astype(F32)).astype(BF16)


def wait_bytes(ref, sem):
    pltpu.make_async_copy(ref, ref, sem).wait()


def greet(z, x, y, core, barrier):
    for d in range(1, 8):
        tell(barrier, at((z + d) % 8, x, y, core))
    for d in range(1, 4):
        tell(barrier, at(z, (x + d) % 4, y, core))
        tell(barrier, at(z, x, (y + d) % 4, core))
    tell(barrier, at(z, x, y, 1 - core))


def tell(sem, where):
    pl.semaphore_signal(sem, inc=1, device_id=where, device_id_type=MESH)


def push(src, dst, send_sem, recv_sem, where):
    pltpu.make_async_remote_copy(
        src_ref=src, dst_ref=dst, send_sem=send_sem, recv_sem=recv_sem, device_id=where, device_id_type=MESH
    ).start()


def mix_kernel(
    panel_hbm, signs_hbm, offsets, owners, result, crowded, lists, kept_hbm,
    panel, signs, y_ref, r_ref, t_ref, mine, own, out, lanes, ids, ranks, picks, names_here, names_there,
    s_here, s_there, picked, full_here, full_there, ha, hb, a1, b1, sa, sb, fa, fb,
    load_sem, small_sem, send_sem, recv_sem, core_send, core_recv, list_send, list_recv, plane_sem, all_sem,
    keep_sem, full_send, full_recv, name_send, name_recv, pass_send, pass_recv, s0, r0, s1, r1a, r1b, s2, r2,
):
    z, x, y, core = place()
    barrier = pltpu.get_barrier_semaphore()
    greet(z, x, y, core, barrier)

    def load(i):
        span = pl.ds(4096 * i, 4096)
        return pltpu.make_async_copy(panel_hbm.at[:, span], panel.at[:, span], load_sem.at[i])

    small = [
        pltpu.make_async_copy(signs_hbm, signs, small_sem.at[0]),
        pltpu.make_async_copy(offsets, own.at[pl.ds(0, 8)], small_sem.at[1]),
        pltpu.make_async_copy(owners, own.at[pl.ds(8, 8)], small_sem.at[2]),
    ]
    small[0].start()
    for i in range(4):
        load(i).start()
    small[1].start()
    small[2].start()
    table = sylvester(128).astype(BF16)
    table = jnp.concatenate([table, table], axis=0)

    small[0].wait()
    for part in range(4):
        load(part).wait()
        for i in range(2 * part, 2 * part + 2):
            sign = signs[16 * i : 16 * i + 16, :].astype(F32)
            rows = []
            for j in range(16):
                start = (i * 16 + j) * 128
                rows.append(panel[:, start : start + 128] * sign[j : j + 1, :])
            hi, lo = split(jnp.concatenate(rows, axis=0))
            pieces = jnp.concatenate([hi, lo], axis=1)
            done = jnp.dot(pieces, table, preferred_element_type=F32)
            y_ref[16 * i : 16 * i + 16] = done.reshape(16, 16, 128)

    pl.semaphore_wait(barrier, 14)
    for d in range(1, 4):
        tell(plane_sem, at(z, (x + d) % 4, y, core))

    def outer_high(g, carry):
        vals = butterfly([y_ref[g + 8 * j] for j in range(16)])
        for j in range(16):
            y_ref[g + 8 * j] = vals[j]
        return carry

    lax.fori_loop(0, 8, outer_high, 0)

    def outer_low(g, carry):
        vals = butterfly([y_ref[g * 8 + j] for j in range(8)])
        for j in range(8):
            y_ref[g * 8 + j] = vals[j]
        return carry

    lax.fori_loop(0, 16, outer_low, 0)

    slot = y * 32 + z * 4 + x
    to_x = [(x + d) % 4 for d in range(4)]
    to_y = [(y + d) % 4 for d in range(4)]
    sends_list = z // 4 == core

    small[1].wait()
    small[2].wait()
    for r in range(2):
        mine[r : r + 1, :] = own[pl.ds(2 * y + r, 1), :]
        mine[2 + r : 3 + r, :] = own[pl.ds(8 + 2 * y + r, 1), :]

    def send(tz, dx, dy):
        push(
            y_ref.at[tz * 16 + to_x[dx] * 4 + to_y[dy]], r_ref.at[slot],
            send_sem, recv_sem.at[dy], at(tz, to_x[dx], to_y[dy], core),
        )

    def send_list(tz, dx):
        push(mine, lists.at[y, z % 4 * 4 + x], list_send, list_recv, at(tz, to_x[dx], y, core))

    for d in (4, 7, 2, 5, 3, 6, 1):
        tz = (z + d) % 8
        send(tz, 0, 0)
        pl.when(sends_list)(functools.partial(send_list, tz, 0))
    pl.semaphore_wait(plane_sem, 3)
    for d in range(1, 4):
        tell(all_sem, at(z, x, (y + d) % 4, core))

    def sweep(dy, carry_list):
        def some(i, carry):
            tz = (z + i * 3 + 4) % 8
            for dx in range(1 if carry_list else 0, 4):
                send(tz, dx, dy)
                if carry_list:
                    pl.when(sends_list)(functools.partial(send_list, tz, dx))
            return carry

        lax.fori_loop(0, 8, some, 0)

    sweep(0, True)
    pl.semaphore_wait(all_sem, 3)
    for dy in range(1, 4):
        sweep(dy, False)

    r_ref[slot] = y_ref[z * 16 + x * 4 + y]

    @pl.when(sends_list)
    def _():
        lists[y, z % 4 * 4 + x] = mine[...]
        wait_bytes(lists.at[0, pl.ds(0, 15)], list_recv)

    @pl.when(jnp.logical_not(sends_list))
    def _():
        wait_bytes(lists.at[0], list_recv)

    for d in (2, 1, 3):
        push(lists.at[y], lists.at[y], pass_send, pass_recv, at(z, x, to_y[d], core))
    wait_bytes(lists.at[pl.ds(0, 3)], pass_recv)

    turn = (1 - 2 * core).astype(F32)

    def across(dy, carry):
        v = (y + 4 - dy) % 4
        for h in range(2):
            rows = pl.ds(8 * h, 8)
            low = [r_ref[v * 32 + q, rows, :] for q in range(16)]
            high = [r_ref[v * 32 + 16 + q, rows, :] * turn for q in range(16)]
            given = butterfly([a - b for a, b in zip(low, high)])
            for p in range(16):
                t_ref[v, p, rows, :] = given[p]
            kept = butterfly([a + b for a, b in zip(low, high)])
            for p in range(16):
                out[p, v, core, rows, :] = kept[p]
        push(t_ref.at[v], out.at[:, v, core], core_send, core_recv, at(z, x, y, 1 - core))
        return carry

    rank, lane, name, seen = ranked(lists, z * 16 + x * 4 + y)
    lanes[...], ids[...] = lane, name
    ahead = jnp.zeros((1, 1), F32)
    for p in range(16):
        row = rank[p : p + 1, :]
        ranks[p : p + 1, :] = jnp.where(row >= 0.0, row + ahead, -1.0)
        ahead = ahead + seen[p : p + 1, :]

    def locate(p, carry):
        spot, its_name = carry
        one = pl.ds(p, 1)
        hot = (iota((TAKEN, 1024), 0).astype(F32) == ranks[one, :]).astype(F32).astype(BF16)
        facts = jnp.concatenate([lanes[one, :], ids[one, :], jnp.zeros((6, 1024), F32)], axis=0)
        found = lax.dot_general(facts.astype(BF16), hot, NT, preferred_element_type=F32)
        base = (p * 128).astype(F32)
        spot = jnp.where(found[1:2, :] > 0.5, found[0:1, :] + base, spot)
        return spot, its_name + found[1:2, :]

    nowhere = jnp.zeros((1, TAKEN), F32)
    spot, its_name = lax.fori_loop(0, 16, locate, (nowhere - 1.0, nowhere))
    names_here[...] = jnp.broadcast_to(its_name, (8, TAKEN))
    push(names_here, names_there, name_send, name_recv, at(z, x, y, 1 - core))

    def mark(k, carry):
        rows = iota((256, TAKEN), 0).astype(F32) + (k * 256).astype(F32)
        picks[k] = (rows == spot).astype(F32).astype(BF16)
        return carry

    lax.fori_loop(0, 8, mark, 0)

    def tally(p, count):
        for q in range(4):
            slabs = lists[q, p] // 128
            for r in range(2):
                count = count + (slabs[r : r + 1, :] == iota((128, 128), 0)).astype(F32)
        return count

    count = lax.fori_loop(0, 16, tally, jnp.zeros((128, 128), F32))
    most = jnp.max(jnp.sum(count, axis=1, keepdims=True), axis=0, keepdims=True)
    full_here[...] = jnp.broadcast_to(jnp.where(most > TAKEN, 1, 0), (8, 128))
    push(full_here, full_there, full_send, full_recv, at(z, x, y, 1 - core))

    wait_bytes(r_ref.at[pl.ds(0, 31)], recv_sem.at[0])
    across(0, 0)

    def across_next(dy, carry):
        wait_bytes(r_ref.at[pl.ds(0, 32)], recv_sem.at[dy])
        return across(dy, carry)

    lax.fori_loop(1, 4, across_next, 0)
    wait_bytes(t_ref, core_recv)
    keep = pltpu.make_async_copy(out, kept_hbm, keep_sem)
    keep.start()
    got = jnp.zeros((256, TAKEN), F32)
    for g in range(4):
        pick = picks[2 * g : 2 * g + 2].reshape(512, TAKEN)
        got = got + jnp.dot(stacked(out, g), pick, preferred_element_type=F32)
    s_here[...] = got[0:128] + got[128:256]
    push(s_here, s_there, s0, r0, at(z, x, y, 1 - core))
    picked[:, :, :, :, 0:TAKEN] = got.astype(BF16).reshape(2, 4, 2, 16, TAKEN)
    wait_bytes(names_there, name_recv)
    names = jnp.concatenate([names_here[0:1, :], names_there[0:1, :]], axis=1)
    wait_bytes(s_there, r0)
    hi, lo = split(s_there[...])
    picked[0, :, :, :, TAKEN : 2 * TAKEN] = hi.reshape(4, 2, 16, TAKEN)
    picked[1, :, :, :, TAKEN : 2 * TAKEN] = lo.reshape(4, 2, 16, TAKEN)

    def make(k, carry):
        i = (z + 4 + k // 2 * (1 - k % 2) - (k + 1) // 2 * (k % 2)) % 8
        whole = picked[...].reshape(256, 2 * TAKEN)
        half = picked[:, :, core].reshape(128, 2 * TAKEN)
        members = []
        for tx in range(4):
            wanted = (i * 4 + tx + 1).astype(F32)
            members.append(half * (names == wanted).astype(F32).astype(BF16))
        both = lax.dot_general(jnp.concatenate(members, axis=0), whole, NT, preferred_element_type=F32)
        for tx in range(4):
            one = both[128 * tx : 128 * tx + 64] + both[128 * tx + 64 : 128 * tx + 128]
            one = (one[:, :128] + one[:, 128:]).reshape(4, 2, 8, 128)
            ha[i, tx] = one[:, 0]
            hb[i, :, tx] = one[:, 1]
        for d in (2, 1, 3):
            push(ha.at[i, to_x[d]], a1.at[x, i], s1.at[0], r1a.at[i], at(z, to_x[d], y, core))
            push(hb.at[i, to_y[d]], b1.at[y, i], s1.at[1], r1b.at[i], at(z, x, to_y[d], core))
        a1[x, i] = ha[i, x]
        b1[y, i] = hb[i, y]
        return carry

    def direct(k, carry):
        i = (z + 4 + k // 2 * (1 - k % 2) - (k + 1) // 2 * (k % 2)) % 8
        wait_bytes(a1.at[pl.ds(0, 3), i], r1a.at[i])
        for t in range(4):
            sa[i, t] = (a1[0, i, t] + a1[1, i, t]) + (a1[2, i, t] + a1[3, i, t])
        for d in (2, 1, 3, 0):
            go = functools.partial(
                push, sa.at[i, to_y[d]], fa.at[z * 4 + y], s2.at[0], r2.at[0], at(i, x, to_y[d], core)
            )
            go() if d else pl.when(i != z)(go)
        wait_bytes(b1.at[pl.ds(0, 3), i], r1b.at[i])
        for t in range(4):
            sb[i, t] = (b1[0, i, t] + b1[1, i, t]) + (b1[2, i, t] + b1[3, i, t])
        for d in (2, 1, 3, 0):
            go = functools.partial(
                push, sb.at[i, to_x[d]], fb.at[z * 4 + x], s2.at[1], r2.at[1], at(i, to_x[d], y, core)
            )
            go() if d else pl.when(i != z)(go)
        return carry

    lax.fori_loop(0, 8, make, 0)
    lax.fori_loop(0, 8, direct, 0)
    fa[z * 4 + y] = sa[z, y]
    fb[z * 4 + x] = sb[z, x]
    for n, ref in enumerate((fa, fb)):
        wait_bytes(ref.at[pl.ds(0, 31)], r2.at[n])
        parts = [ref[i] for i in range(32)]
        while len(parts) > 1:
            parts = [a + b for a, b in zip(parts[::2], parts[1::2])]
        result[8 * n : 8 * n + 8, :] = parts[0] * GRAM_SCALE
    wait_bytes(full_there, full_recv)
    crowded[0, 0] = jnp.max(jnp.maximum(full_here[...], full_there[...]))

    wait_bytes(r_ref.at[pl.ds(0, 127)], send_sem)

    @pl.when(sends_list)
    def _():
        for n in range(31):
            wait_bytes(mine, list_send)

    keep.wait()
    wait_bytes(full_here, full_send)
    wait_bytes(names_here, name_send)
    wait_bytes(lists.at[pl.ds(0, 3)], pass_send)
    wait_bytes(s_here, s0)
    wait_bytes(t_ref, core_send)
    wait_bytes(a1.at[pl.ds(0, 3)], s1.at[0])
    wait_bytes(b1.at[pl.ds(0, 3)], s1.at[1])
    wait_bytes(fa.at[pl.ds(0, 31)], s2.at[0])
    wait_bytes(fb.at[pl.ds(0, 31)], s2.at[1])


def ranked(lists, slab):
    here = jnp.concatenate([lists[b // 2, :, b % 2, :] for b in range(8)], axis=1) - slab * 128
    owner = jnp.concatenate([lists[b // 2, :, 2 + b % 2, :] for b in range(8)], axis=1)
    inside = (here >= 0) & (here < 128)
    mask = jnp.where(inside, 1.0, 0.0).astype(F32)
    before = (iota((128, 128), 0) < iota((128, 128), 1)).astype(F32).astype(BF16)
    rank, seen = [], jnp.zeros((16, 1), F32)
    for b in range(8):
        piece = mask[:, 128 * b : 128 * b + 128]
        rank.append(jnp.dot(piece.astype(BF16), before, preferred_element_type=F32) + seen)
        seen = seen + jnp.sum(piece, axis=1, keepdims=True)
    rank = jnp.where(inside, jnp.concatenate(rank, axis=1), -1.0)
    lane = jnp.where(inside, here, 0).astype(F32)
    name = jnp.where(inside, owner + 1, 0).astype(F32)
    return rank, lane, name, seen


def chosen(rank, lane, name, g, first):
    wanted = iota((SLOTS, 1024), 0).astype(F32) + first
    hot = [rank[p : p + 1, :] == wanted for p in range(4 * g, 4 * g + 4)]
    hot = jnp.concatenate([h.astype(F32) for h in hot], axis=0).astype(BF16)
    facts = jnp.concatenate([lane[4 * g : 4 * g + 4], name[4 * g : 4 * g + 4]], axis=0)
    found = lax.dot_general(facts.astype(BF16), hot, NT, preferred_element_type=F32)
    which = iota((1, 128), 1) // SLOTS
    at_lane, its_name = jnp.zeros((1, 128), F32), jnp.zeros((1, 128), F32)
    for p in range(4):
        at_lane = jnp.where(which == p, found[p : p + 1, :] + 128.0 * p, at_lane)
        its_name = jnp.where(which == p, found[4 + p : 5 + p, :], its_name)
    spot = jnp.where(its_name > 0.5, at_lane, -1.0)
    pick = (iota((512, 128), 0).astype(F32) == spot).astype(F32).astype(BF16)
    return pick, its_name


def stacked(mixed, g):
    columns = []
    for p in range(4 * g, 4 * g + 4):
        hi, lo = split(mixed[p].reshape(128, 128))
        columns.append(jnp.concatenate([hi, lo], axis=0))
    return jnp.concatenate(columns, axis=1)


def folded(both):
    return (both[:128, :128] + both[128:, 128:]) + (both[:128, 128:] + both[128:, :128])


def owner_gram(picked, names, o):
    member = (names == o.astype(F32) + 1.0).astype(F32).astype(BF16)
    both = lax.dot_general(picked * member, picked, NT, preferred_element_type=F32)
    return folded(both)


def gram_kernel(mixed, lists, out, picked):
    z, x, y, core = place()
    rank, lane, name, seen = ranked(lists, z * 16 + x * 4 + y)
    rounds = (jnp.max(seen).astype(jnp.int32) + SLOTS - 1) // SLOTS
    out[...] = jnp.zeros_like(out)

    def one_round(r, carry):
        names = []
        for g in range(4):
            pick, its_name = chosen(rank, lane, name, g, (r * SLOTS).astype(F32))
            got = jnp.dot(stacked(mixed, g), pick, preferred_element_type=F32)
            picked[:, 128 * g : 128 * g + 128] = got.astype(BF16)
            names.append(its_name)
        names = jnp.concatenate(names, axis=1)

        def one_owner(o, carry):
            out[o] += owner_gram(picked[...], names, o) * GRAM_SCALE
            return carry

        lax.fori_loop(0, 32, one_owner, 0)
        return carry

    lax.fori_loop(0, rounds, one_round, 0)


def sum_kernel(gram, out, c_ref, ha, hb, a1, b1, sa, sb, a2, b2, sz, zr, s0, r0, s1, r1, s2, r2, s3, r3):
    z, x, y, core = place()

    barrier = pltpu.get_barrier_semaphore()
    greet(z, x, y, core, barrier)
    pl.semaphore_wait(barrier, 14)
    push(gram.at[:, :, :, 1 - core], c_ref, s0, r0, at(z, x, y, 1 - core))
    wait_bytes(c_ref, r0)

    def add_core(i, carry):
        for tx in range(4):
            for ty in range(4):
                ha[tx, i, ty] = gram[i, tx, ty, core, 0:8, :] + c_ref[i, tx, ty, 0:8, :]
                hb[ty, i, tx] = gram[i, tx, ty, core, 8:16, :] + c_ref[i, tx, ty, 8:16, :]
        return carry

    lax.fori_loop(0, 8, add_core, 0)
    for d in (2, 1, 3):
        tx, ty = (x + d) % 4, (y + d) % 4
        push(ha.at[tx], a1.at[x], s1.at[0], r1.at[0], at(z, tx, y, core))
        push(hb.at[ty], b1.at[y], s1.at[1], r1.at[1], at(z, x, ty, core))
    a1[x] = ha[x]
    b1[y] = hb[y]
    wait_bytes(a1.at[pl.ds(0, 3)], r1.at[0])
    wait_bytes(b1.at[pl.ds(0, 3)], r1.at[1])

    def add_first(i, carry):
        for t in range(4):
            sa[t, i] = (a1[0, i, t] + a1[1, i, t]) + (a1[2, i, t] + a1[3, i, t])
            sb[t, i] = (b1[0, i, t] + b1[1, i, t]) + (b1[2, i, t] + b1[3, i, t])
        return carry

    lax.fori_loop(0, 8, add_first, 0)
    for d in (2, 1, 3):
        tx, ty = (x + d) % 4, (y + d) % 4
        push(sa.at[ty], a2.at[y], s2.at[0], r2.at[0], at(z, x, ty, core))
        push(sb.at[tx], b2.at[x], s2.at[1], r2.at[1], at(z, tx, y, core))
    a2[y] = sa[y]
    b2[x] = sb[x]
    wait_bytes(a2.at[pl.ds(0, 3)], r2.at[0])
    wait_bytes(b2.at[pl.ds(0, 3)], r2.at[1])
    for i in range(8):
        sz[i, 0:8, :] = (a2[0, i] + a2[1, i]) + (a2[2, i] + a2[3, i])
        sz[i, 8:16, :] = (b2[0, i] + b2[1, i]) + (b2[2, i] + b2[3, i])
    for d in (4, 3, 5, 2, 6, 1, 7):
        tz = (z + d) % 8
        push(sz.at[tz], zr.at[z], s3, r3, at(tz, x, y, core))
    zr[z] = sz[z]
    wait_bytes(zr.at[pl.ds(0, 7)], r3)
    v = [zr[i] for i in range(8)]
    out[...] = ((v[0] + v[1]) + (v[2] + v[3])) + ((v[4] + v[5]) + (v[6] + v[7]))
    wait_bytes(c_ref, s0)
    for n in range(2):
        wait_bytes(a1.at[pl.ds(0, 3)], s1.at[n])
        wait_bytes(a2.at[pl.ds(0, 3)], s2.at[n])
    wait_bytes(zr.at[pl.ds(0, 7)], s3)


def body(panel, signs, offsets, owners):
    params = functools.partial(pltpu.CompilerParams, has_side_effects=True)
    dma, vmem = pltpu.SemaphoreType.DMA, pltpu.VMEM
    result, crowded, lists, mixed = pl.pallas_call(
        mix_kernel,
        out_shape=[
            jax.ShapeDtypeStruct((16, 128), F32),
            jax.ShapeDtypeStruct((1, 1), jnp.int32),
            jax.ShapeDtypeStruct((4, 16, 4, 128), jnp.int32),
            jax.ShapeDtypeStruct((16, 4, 2, 16, 128), F32),
        ],
        in_specs=[HBM] * 4,
        out_specs=[VMEM, SMEM, VMEM, HBM],
        scratch_shapes=[
            vmem((16, 16384), F32),
            vmem((128, 128), jnp.int32),
            vmem((128, 16, 128), F32),
            vmem((128, 16, 128), F32),
            vmem((4, 16, 16, 128), F32),
            vmem((4, 128), jnp.int32),
            vmem((16, 128), jnp.int32),
            vmem((16, 4, 2, 16, 128), F32),
            vmem((16, 1024), F32),
            vmem((16, 1024), F32),
            vmem((16, 1024), F32),
            vmem((8, 256, TAKEN), BF16),
            vmem((8, TAKEN), F32),
            vmem((8, TAKEN), F32),
            vmem((128, TAKEN), F32),
            vmem((128, TAKEN), F32),
            vmem((2, 4, 2, 16, 2 * TAKEN), BF16),
            vmem((8, 128), jnp.int32),
            vmem((8, 128), jnp.int32),
            vmem((8, 4, 4, 8, 128), F32),
            vmem((8, 4, 4, 8, 128), F32),
            vmem((4, 8, 4, 8, 128), F32),
            vmem((4, 8, 4, 8, 128), F32),
            vmem((8, 4, 8, 128), F32),
            vmem((8, 4, 8, 128), F32),
            vmem((32, 8, 128), F32),
            vmem((32, 8, 128), F32),
            dma((4,)), dma((3,)), dma, dma((4,)), dma, dma, dma, dma,
            pltpu.SemaphoreType.REGULAR, pltpu.SemaphoreType.REGULAR,
            dma, dma, dma, dma, dma, dma, dma, dma, dma, dma((2,)), dma((8,)), dma((8,)),
            dma((2,)), dma((2,)),
        ],
        compiler_params=params(collective_id=1, vmem_limit_bytes=MIX_VMEM),
        name="mix",
    )(panel, signs.reshape(128, 128), offsets.reshape(8, 128), owners.reshape(8, 128))

    def in_rounds():
        gram = pl.pallas_call(
            gram_kernel,
            out_shape=jax.ShapeDtypeStruct((32, 128, 128), F32),
            in_specs=[VMEM] * 2,
            out_specs=VMEM,
            scratch_shapes=[vmem((256, 512), BF16)],
            compiler_params=pltpu.CompilerParams(vmem_limit_bytes=48 << 20),
            name="gram_rounds",
        )(mixed.reshape(16, 128, 128), lists)
        return pl.pallas_call(
            sum_kernel,
            out_shape=jax.ShapeDtypeStruct((16, 128), F32),
            in_specs=[VMEM],
            out_specs=VMEM,
            scratch_shapes=[
                vmem((8, 4, 4, 16, 128), F32),
                vmem((4, 8, 4, 8, 128), F32),
                vmem((4, 8, 4, 8, 128), F32),
                vmem((4, 8, 4, 8, 128), F32),
                vmem((4, 8, 4, 8, 128), F32),
                vmem((4, 8, 8, 128), F32),
                vmem((4, 8, 8, 128), F32),
                vmem((4, 8, 8, 128), F32),
                vmem((4, 8, 8, 128), F32),
                vmem((8, 16, 128), F32),
                vmem((8, 16, 128), F32),
            ] + [dma] * 2 + [dma((2,))] * 4 + [dma] * 2,
            compiler_params=params(collective_id=2, vmem_limit_bytes=48 << 20),
            name="sum_rounds",
        )(gram.reshape(8, 4, 4, 2, 16, 128))

    return lax.cond(crowded[0, 0] > 0, in_rounds, lambda: result)[None]


def solution(mesh):
    placed = (P("col", "row"), P("row"), P("row"), P("row", None))
    return jax.shard_map(
        body, mesh=mesh, in_specs=placed, out_specs=P("row", "col", None), check_vma=False
    )
```
